128 devices in a mesh: row: 16 (over x, z), col: 8 (over y, core).
Axes of the slice: x: 4, y: 4, z: 4, core: 2. Of those that a mesh axis runs over, the one named last changes fastest.
Arguments:
- features: bfloat16 [262144, 128], P(('col', 'row')), may hold values from -6 to 6
- weight: bfloat16 [128, 256], replicated, may hold values from -0.5 to 0.5
- offset: float32 [256], replicated, may hold values from -3 to 3
- tile_values: bfloat16 [16, 8, 64, 128, 128], P('row', 'col'), may hold values from -0.25 to 0.25
- tile_rows: int32 [16, 8, 64], P('row', 'col'), may hold values from 0 to 127
- tile_cols: int32 [16, 8, 64], P('row', 'col'), may hold values from 0 to 255
- live_tiles: int32 [16, 8], P('row', 'col'), may hold values from 16 to 64, as said below
- grad_hidden: bfloat16 [262144, 256], P(('row', 'col')), may hold values from -6 to 6
Outputs:
- hidden: bfloat16 [262144, 256], P(('row', 'col'))
- grad_features: float32 [262144, 128], P(('col', 'row'))
- grad_weight: float32 [128, 256], replicated
- grad_offset: float32 [256], replicated
The draws below stay inside these ranges and needn't reach their ends.
Inputs may be any that keep to these rules, and one draw needn't show every extreme that they name: Only the first live_tiles[r, c] slots of block pair (r, c) are used; some block pair uses all 64 slots and some uses only 16; none uses fewer than 16.
All inputs are finite; a program needn't handle non-finite values.
Results may differ from the reference program's by a relative error of at most 0.0075.
Values may be sent and summed in bfloat16 or wider, within the bound.
No kernel may reach another device: no remote copies, remote signals or barrier semaphores. Data moves between devices by JAX's collectives and lax.ppermute only.
A program may use at most 192 MiB of HBM per device.

```python
import math
import jax
import jax.numpy as jnp
import numpy as np
from jax import lax

F_IN = 128
HIDDEN_SIZE = 256
TILE = 128
NODES_DEV = 2048
SLOTS = 64
NODES = 262144
ROW_BLOCKS = 128
COL_BLOCKS = 256
N_ROW = 16
N_COL = 8


def draw_live_tiles(key, part):
    key = jax.random.fold_in(key, 7)
    first_key, second_key = jax.random.split(key)
    lowest = max(1, SLOTS // 4)
    counts = jax.random.randint(first_key, (N_ROW * N_COL,), lowest, SLOTS + 1)
    chosen = jax.random.permutation(second_key, N_ROW * N_COL)
    counts = counts.at[chosen[0]].set(SLOTS).at[chosen[1]].set(lowest)
    return counts.reshape(N_ROW, N_COL).astype(jnp.int32)


def touch_ends(values, key, least, largest):
    longest = values.shape.index(max(values.shape))
    spots = []
    for shift in (0, 1):
        where = [jax.random.randint(jax.random.fold_in(key, axis), (), 0, length) for axis, length in enumerate(values.shape)]
        where[longest] = (where[longest] + shift) % values.shape[longest]
        spots.append(tuple(where))
    return values.at[spots[0]].set(least).at[spots[1]].set(largest)


def level_of(key, dims, cuts, smallest, high):
    level = 1.0
    for axis_at, parts in cuts:
        heights = jax.random.uniform(jax.random.fold_in(jax.random.fold_in(key, 6), axis_at), (parts,), jnp.float32, smallest / len(cuts), high / len(cuts))
        level = level * jnp.repeat(jnp.exp(heights), dims[axis_at] // parts).reshape((-1,) + (1,) * (len(dims) - 1 - axis_at))
    return level


def rank_bounds(amount, slope):
    loads = [(1 << 20) // math.isqrt(standing ** slope) + 1 for standing in range(1, amount + 1)]
    width = 1 + sum(loads) // (1 << 30)
    return np.cumsum(np.array([max(1, weight // width) for weight in loads]))


def ranked(own_key, shape, number_of, skew):
    listing = rank_bounds(number_of, skew)
    lot = jax.random.randint(jax.random.fold_in(own_key, 1), shape, 0, int(listing[number_of - 1]))
    rank = jnp.searchsorted(jnp.asarray(listing, jnp.int32), lot, side="right")
    return jax.random.permutation(jax.random.fold_in(own_key, 2), number_of)[rank].astype(jnp.int32)


def bell_draw(own_key, dims, spread, most, cuts=(), held_as=jnp.bfloat16):
    values = spread * jax.random.normal(own_key, dims, jnp.float32)
    if cuts:
        values = values * level_of(own_key, dims, cuts, -0.22, 0.18)
    return jnp.clip(values, -most, most).astype(held_as)


def setup_inputs(seed: int = 0) -> dict:
    seeds = jax.random.split(jax.random.key(seed), 9)
    features = bell_draw(seeds[0], (NODES, F_IN), 1.0, 6.0, ((0, 128),))
    weight = bell_draw(seeds[1], (F_IN, HIDDEN_SIZE), F_IN ** -0.5, 0.5)
    offset = bell_draw(seeds[2], (HIDDEN_SIZE,), 0.5, 3.0, (), jnp.float32)
    tile_values = bell_draw(seeds[3], (N_ROW, N_COL, SLOTS, TILE, TILE), (SLOTS * TILE * TILE // NODES_DEV) ** -0.5, 0.25, ((0, 16), (1, 8)))
    tile_rows = touch_ends(ranked(seeds[4], (N_ROW, N_COL, SLOTS), ROW_BLOCKS, 2), jax.random.fold_in(seeds[4], 3), 0, ROW_BLOCKS - 1).astype(jnp.int32)
    tile_cols = touch_ends(jax.random.randint(seeds[5], (N_ROW, N_COL, SLOTS), 0, COL_BLOCKS), jax.random.fold_in(seeds[5], 1), 0, COL_BLOCKS - 1).astype(jnp.int32)
    live_tiles = draw_live_tiles(jax.random.fold_in(seeds[8], 71), 0)
    grad_hidden = bell_draw(seeds[7], (NODES, HIDDEN_SIZE), 1.0, 6.0, ((0, 128),))
    return dict(features=features, weight=weight, offset=offset, tile_values=tile_values, tile_rows=tile_rows, tile_cols=tile_cols, live_tiles=live_tiles, grad_hidden=grad_hidden)


def activate(pre_act, grad_hidden):
    sigmoid_value = jax.nn.sigmoid(pre_act)
    hidden = (pre_act * sigmoid_value).astype(jnp.bfloat16)
    slope_grad = (grad_hidden.astype(jnp.float32) * sigmoid_value * (1.0 + pre_act * (1.0 - sigmoid_value))).astype(jnp.bfloat16)
    return (hidden, slope_grad)

def apply_tiles(tile_groups, out_index, in_index, keeping, source, out_blocks, flipped):
    feature_width = source.shape[1]
    blocks = source.reshape(-1, TILE, feature_width)
    pattern = 'sji,sjw->siw' if flipped else 'sij,sjw->siw'

    def step_device(running, item):
        tile_part, out_here, in_here, keep_here = item
        pieces = blocks[in_here].astype(jnp.float32)
        product = jnp.einsum(pattern, tile_part.astype(jnp.float32), pieces, precision=lax.Precision.HIGHEST)
        product = product * keep_here[:, None, None]
        return (running.at[out_here].add(product), None)
    start_sum = jnp.zeros((out_blocks, TILE, feature_width), jnp.float32)
    running, unused = lax.scan(step_device, start_sum, (tile_groups, out_index, in_index, keeping))
    return running.reshape(out_blocks * TILE, feature_width)

def reference(features, weight, offset, tile_values, tile_rows, tile_cols, live_tiles, grad_hidden):
    row_global = (jnp.arange(N_ROW, dtype=jnp.int32)[:, None, None] * ROW_BLOCKS + tile_rows).reshape(-1, SLOTS).astype(jnp.int32)
    col_global = (jnp.arange(N_COL, dtype=jnp.int32)[None, :, None] * COL_BLOCKS + tile_cols).reshape(-1, SLOTS).astype(jnp.int32)
    keeping = (jnp.arange(SLOTS, dtype=jnp.int32)[None, None, :] < live_tiles[:, :, None]).astype(jnp.float32).reshape(-1, SLOTS)
    tile_groups = tile_values.reshape(-1, SLOTS, TILE, TILE)
    total_blocks = NODES // TILE
    mixed = apply_tiles(tile_groups, row_global, col_global, keeping, features, total_blocks, False)
    pre_act = jnp.dot(mixed, weight.astype(jnp.float32), precision=lax.Precision.HIGHEST) + offset
    hidden, slope_grad = activate(pre_act, grad_hidden)
    projected = jnp.dot(slope_grad, weight.T, preferred_element_type=jnp.float32)
    grad_features = apply_tiles(tile_groups, col_global, row_global, keeping, projected, total_blocks, True)
    scaling = 1.0 / jnp.sqrt(jnp.float32(NODES))
    grad_weight = jnp.dot(mixed.T, slope_grad.astype(jnp.float32), precision=lax.Precision.HIGHEST) * scaling
    grad_offset = lax.optimization_barrier(jnp.sum(slope_grad.astype(jnp.float32), axis=0)) * scaling
    return (hidden, grad_features, grad_weight, grad_offset)
```

```python
import math

import jax
import jax.numpy as jnp
from jax import lax
from jax.experimental import pallas as pl
from jax.experimental.pallas import tpu as pltpu
from jax.sharding import PartitionSpec as P

T = 128
F32, BF16 = jnp.float32, jnp.bfloat16
VMEM_BYTES = 56 * 1024 * 1024
GROUP = 4


def along_x(value, step):
    pairs = [(x * 4 + z, (x + step) % 4 * 4 + z) for x in range(4) for z in range(4)]
    return lax.ppermute(value, "row", pairs)


def along_z(value, step):
    pairs = [(x * 4 + z, x * 4 + (z + step) % 4) for x in range(4) for z in range(4)]
    return lax.ppermute(value, "row", pairs)


def along_y(value, step):
    pairs = [(y * 2 + k, (y + step) % 4 * 2 + k) for y in range(4) for k in range(2)]
    return lax.ppermute(value, "col", pairs)


def other_core(value):
    pairs = [(y * 2 + k, y * 2 + 1 - k) for y in range(4) for k in range(2)]
    return lax.ppermute(value, "col", pairs)


def ring_gather(value, along):
    return [value, along(value, -1), along(value, 2), along(value, 1)]


def ring_send(pieces, along):
    return [pieces[0], along(pieces[1], 1), along(pieces[2], 2), along(pieces[3], -1)]


def col_place(col, here):
    x, z = here // 4, lax.rem(here, 4)
    owner, block = col // 16, lax.rem(col, 16)
    dx = lax.rem(owner // 4 - x + 4, 4)
    dz = lax.rem(lax.rem(owner, 4) - z + 4, 4)
    half, block = block // 8, lax.rem(block, 8)
    outer = jnp.where(half == 0, dz, dx)
    inner = jnp.where(half == 0, dx, dz)
    return ((half * 4 + outer) * 4 + inner) * 8 + block


def row_place(row, here):
    y, core = here // 2, lax.rem(here, 2)
    owner, block = row // 16, lax.rem(row, 16)
    dy = lax.rem(owner // 2 - y + 4, 4)
    same = jnp.where(lax.rem(owner, 2) == core, 1, 0)
    return (same * 4 + dy) * 16 + block


def load_all(sources, held, sems):
    size = held.shape[0] // len(sources)
    return [
        pltpu.make_async_copy(ref, held.at[pl.ds(k * size, size)], sems.at[k])
        for k, ref in enumerate(sources)
    ]


def clear(total):
    zeros = jnp.zeros((4,) + total.shape[1:], F32)

    def step(k, carry):
        total[pl.ds(k * 4, 4)] = zeros
        return carry

    lax.fori_loop(0, total.shape[0] // 4, step, 0)


def add_tiles(live, tiles, in_place, out_place, held, total, contract):
    def group(number, carry):
        products, places = [], []
        for k in range(GROUP):
            slot = number * GROUP + k
            product = lax.dot_general(
                tiles[slot],
                held[in_place(slot)],
                ((contract, (0,)), ((), ())),
                preferred_element_type=F32,
            )
            products.append(jnp.where(slot < live, product, 0.0))
            places.append(out_place(slot))
        for product, place in zip(products, places):
            total[place] += product
        return carry

    lax.fori_loop(0, (live + GROUP - 1) // GROUP, group, 0)


def forward_kernel(live, rows, cols, at_row, at_col, tiles, *refs):
    sources, (send, keep), (held, total, sems) = refs[:8], refs[8:10], refs[10:]
    copies = load_all(sources, held, sems)
    for copy in copies:
        copy.start()
    clear(total)
    for copy in copies:
        copy.wait()
    here_row, here_col = at_row[0], at_col[0]
    add_tiles(
        live[0],
        tiles,
        lambda s: col_place(cols[s], here_row),
        lambda s: row_place(rows[s], here_col),
        held,
        total,
        (1,),
    )

    def out(k, carry):
        send[k] = total[k].astype(BF16)
        keep[k] = total[64 + k].astype(BF16)
        return carry

    lax.fori_loop(0, 64, out, 0)


def backward_kernel(live, rows, cols, at_row, at_col, tiles, *refs):
    sources, outs, (held, total, sems) = refs[:8], refs[8:16], refs[16:]
    copies = load_all(sources, held, sems)
    for copy in copies:
        copy.start()
    clear(total)
    for copy in copies:
        copy.wait()
    here_row, here_col = at_row[0], at_col[0]
    add_tiles(
        live[0],
        tiles,
        lambda s: row_place(rows[s], here_col),
        lambda s: col_place(cols[s], here_row),
        held,
        total,
        (0,),
    )
    for n, ref in enumerate(outs):

        def out(k, carry, n=n, ref=ref):
            ref[k] = total[n * 32 + k].astype(BF16)
            return carry

        lax.fori_loop(0, 32, out, 0)


def aggregate(kernel, scalars, tiles, sources, in_blocks, out_blocks, outs):
    smem = pl.BlockSpec(memory_space=pltpu.SMEM)
    return pl.pallas_call(
        kernel,
        out_shape=[jax.ShapeDtypeStruct((n, T, T), BF16) for n in outs],
        in_specs=[smem] * 5
        + [pl.BlockSpec(memory_space=pltpu.VMEM)]
        + [pl.BlockSpec(memory_space=pl.ANY)] * 8,
        out_specs=[pl.BlockSpec(memory_space=pltpu.VMEM)] * len(outs),
        scratch_shapes=[
            pltpu.VMEM((in_blocks, T, T), BF16),
            pltpu.VMEM((out_blocks, T, T), F32),
            pltpu.SemaphoreType.DMA((8,)),
        ],
        compiler_params=pltpu.CompilerParams(vmem_limit_bytes=VMEM_BYTES),
    )(*scalars, tiles, *sources)


def dense_kernel(m0, m1, m2, m3, grad, weight, offset, hidden, projected, sums):
    @pl.when(pl.program_id(0) == 0)
    def _():
        sums[...] = jnp.zeros_like(sums)

    mixed = m0[...].astype(F32) + m1[...].astype(F32) + m2[...].astype(F32) + m3[...].astype(F32)
    high = mixed.astype(BF16)
    low = (mixed - high.astype(F32)).astype(BF16)
    w = weight[...]
    pre = jnp.dot(high, w, preferred_element_type=F32)
    pre = pre + jnp.dot(low, w, preferred_element_type=F32) + offset[...]
    s = jax.nn.sigmoid(pre)
    hidden[...] = (pre * s).astype(BF16)
    slope = (grad[...].astype(F32) * s * (1.0 + pre * (1.0 - s))).astype(BF16)
    projected[...] = lax.dot_general(
        slope, w, (((1,), (1,)), ((), ())), preferred_element_type=F32
    ).astype(BF16)
    over_rows = (((0,), (0,)), ((), ()))
    sums[:T] += lax.dot_general(
        high, slope, over_rows, preferred_element_type=F32
    ) + lax.dot_general(low, slope, over_rows, preferred_element_type=F32)
    sums[T:] += jnp.sum(slope.astype(F32).reshape(-1, 8, slope.shape[1]), axis=0)


def dense(parts, grad, weight, offset):
    rows, width = parts[0].shape[0], weight.shape[1]
    step = 512
    half = pl.BlockSpec((step, T), lambda i: (i, 0))
    full = pl.BlockSpec((step, width), lambda i: (i, 0))
    return pl.pallas_call(
        dense_kernel,
        grid=(rows // step,),
        out_shape=[
            jax.ShapeDtypeStruct((rows, width), BF16),
            jax.ShapeDtypeStruct((rows, T), BF16),
            jax.ShapeDtypeStruct((T + 8, width), F32),
        ],
        in_specs=[half] * 4
        + [
            full,
            pl.BlockSpec((T, width), lambda i: (0, 0)),
            pl.BlockSpec((1, width), lambda i: (0, 0)),
        ],
        out_specs=[full, half, pl.BlockSpec((T + 8, width), lambda i: (0, 0))],
        compiler_params=pltpu.CompilerParams(vmem_limit_bytes=VMEM_BYTES),
    )(*parts, grad, weight, offset)


def on_device(features, weight, offset, tile_values, tile_rows, tile_cols, live_tiles, grad_hidden):
    tiles = tile_values.reshape(tile_values.shape[2:])
    nodes_here = features.shape[0]
    scaling = 1.0 / math.sqrt(nodes_here * lax.axis_size("row") * lax.axis_size("col"))
    scalars = (
        live_tiles.reshape(1),
        tile_rows.reshape(-1),
        tile_cols.reshape(-1),
        lax.axis_index("row").reshape(1),
        lax.axis_index("col").reshape(1),
    )

    blocks = features.reshape(16, T, T)
    first, second = blocks[:8], blocks[8:]
    first = jnp.concatenate(ring_gather(first, along_x))
    second = jnp.concatenate(ring_gather(second, along_z))
    gathered = ring_gather(first, along_z) + ring_gather(second, along_x)
    send, keep = aggregate(forward_kernel, scalars, tiles, gathered, 256, 128, (64, 64))

    both = keep.astype(F32) + other_core(send).astype(F32)
    both = both.reshape(4, nodes_here, T)
    mixed_parts = ring_send([both[d].astype(BF16) for d in range(4)], along_y)
    hidden, projected, sums = dense(mixed_parts, grad_hidden, weight, offset.reshape(1, -1))

    own = ring_gather(projected.reshape(16, T, T), along_y)
    others = [other_core(piece) for piece in own]
    outs = aggregate(backward_kernel, scalars, tiles, others + own, 128, 256, (32,) * 8)

    sums = jnp.sum(lax.all_gather(sums, "col", axis=0), axis=0)
    sums = jnp.sum(lax.all_gather(sums, "row", axis=0), axis=0) * scaling

    def total(pieces):
        return sum(piece.astype(F32) for piece in pieces)

    first = total(ring_send(outs[:4], along_z)).reshape(4, 8 * T, T)
    second = total(ring_send(outs[4:], along_x)).reshape(4, 8 * T, T)
    first = ring_send([first[0]] + [first[d].astype(BF16) for d in (1, 2, 3)], along_x)
    second = ring_send([second[0]] + [second[d].astype(BF16) for d in (1, 2, 3)], along_z)
    grad_features = jnp.concatenate([total(first), total(second)])
    return (hidden, grad_features, sums[:T], jnp.sum(sums[T:], axis=0))


def solution(mesh):
    in_specs = (
        P(("col", "row"), None),
        P(),
        P(),
        P("row", "col", None, None, None),
        P("row", "col", None),
        P("row", "col", None),
        P("row", "col"),
        P(("row", "col"), None),
    )
    out_specs = (P(("row", "col"), None), P(("col", "row"), None), P(), P())
    return jax.shard_map(
        on_device, mesh=mesh, in_specs=in_specs, out_specs=out_specs, check_vma=False
    )
```

```python
import functools
import math

import jax
import jax.numpy as jnp
from jax import lax
from jax.experimental import pallas as pl
from jax.experimental.pallas import tpu as pltpu
from jax.sharding import PartitionSpec as P

T = 128
F32, BF16, I32 = jnp.float32, jnp.bfloat16, jnp.int32
VMEM_BYTES = 56 * 1024 * 1024
GROUP = 4
HALF = 8 * T
META = 16
CAP = 16
SMEM = pl.BlockSpec(memory_space=pltpu.SMEM)
VMEM = pl.BlockSpec(memory_space=pltpu.VMEM)
ANY = pl.BlockSpec(memory_space=pl.ANY)
PARAMS = pltpu.CompilerParams(vmem_limit_bytes=VMEM_BYTES)


def along_x(value, step):
    pairs = [(x * 4 + z, (x + step) % 4 * 4 + z) for x in range(4) for z in range(4)]
    return lax.ppermute(value, "row", pairs)


def along_z(value, step):
    pairs = [(x * 4 + z, x * 4 + (z + step) % 4) for x in range(4) for z in range(4)]
    return lax.ppermute(value, "row", pairs)


def along_y(value, step):
    pairs = [(y * 2 + k, (y + step) % 4 * 2 + k) for y in range(4) for k in range(2)]
    return lax.ppermute(value, "col", pairs)


def other_core(value):
    pairs = [(y * 2 + k, y * 2 + 1 - k) for y in range(4) for k in range(2)]
    return lax.ppermute(value, "col", pairs)


def ring_gather(value, along):
    return [value, along(value, -1), along(value, 2), along(value, 1)]


def ring_send(pieces, along):
    return [pieces[0], along(pieces[3], -1), along(pieces[2], 2), along(pieces[1], 1)]


def ring_sum(value, along):
    a, b, c, d = ring_gather(value, along)
    return a + b + c + d


def total_of(pieces):
    return sum(piece.astype(F32) for piece in pieces)


def block(place):
    return pl.ds(pl.multiple_of(place * T, T), T)


def places(rows, cols, live, at_row, at_col):
    x, z, y, core = at_row // 4, at_row % 4, at_col // 2, at_col % 2
    owner = rows // 16
    same_core = (owner % 2 == core).astype(I32)
    row_place = (same_core * 4 + (owner // 2 - y) % 4) * 16 + rows % 16

    owner = cols // 16
    dx, dz = (owner // 4 - x) % 4, (owner % 4 - z) % 4
    half = cols % 16 // 8
    outer, inner = jnp.where(half == 0, dz, dx), jnp.where(half == 0, dx, dz)
    group, code = half * 4 + outer, inner * 8 + cols % 8
    dense_place = group * 32 + code

    slot = jnp.arange(cols.shape[0], dtype=I32)
    valid = slot < live
    same = cols[:, None] == cols[None, :]
    earlier = slot[None, :] < slot[:, None]
    first = valid & ~jnp.any(same & earlier, axis=1)
    ahead = earlier & first[None, :] & (group[:, None] == group[None, :])
    rank = jnp.sum(ahead.astype(I32), axis=1)
    overflow = jnp.any(first & (outer != 0) & (rank >= CAP))
    far = 64 + (half * 3 + outer - 1) * CAP + jnp.minimum(rank, CAP - 1)
    place = jnp.where(outer == 0, half * 32 + code, far)
    place = jnp.sum(jnp.where(same & first[None, :], place[None, :], 0), axis=1)
    place = jnp.where(valid, place, 0)
    return row_place, place, dense_place, jnp.where(first, cols, -1), overflow


def products_kernel(live, in_place, out_place, tiles_ref, *refs, spans, outs, contract):
    n = len(spans)
    sources, out_refs, (tiles, held, total, sems) = refs[:n], refs[n:-4], refs[-4:]
    copies = [pltpu.make_async_copy(tiles_ref, tiles, sems.at[n])]
    start = 0
    for k, (ref, rows) in enumerate(zip(sources, spans)):
        copies.append(
            pltpu.make_async_copy(
                ref.at[pl.ds(0, rows)], held.at[pl.ds(start, rows)], sems.at[k]
            )
        )
        start += rows
    for copy in copies:
        copy.start()

    zeros = jnp.zeros((4, T, T), F32)

    def clear(k, carry):
        total[pl.ds(k * 4, 4)] = zeros
        return carry

    lax.fori_loop(0, total.shape[0] // 4, clear, 0)
    for copy in copies:
        copy.wait()

    def group(number, carry):
        products = []
        for k in range(GROUP):
            slot = number * GROUP + k
            product = lax.dot_general(
                tiles[slot],
                held[block(in_place[slot])],
                ((contract, (0,)), ((), ())),
                preferred_element_type=F32,
            )
            products.append(jnp.where(slot < live[0], product, 0.0))
        for k, product in enumerate(products):
            total[out_place[number * GROUP + k]] += product
        return carry

    lax.fori_loop(0, (live[0] + GROUP - 1) // GROUP, group, 0)
    start = 0
    for ref, blocks in zip(out_refs, outs):

        def out(k, carry, ref=ref, start=start):
            ref[block(k)] = total[start + k].astype(BF16)
            return carry

        lax.fori_loop(0, blocks, out, 0)
        start += blocks


def products(live, in_place, out_place, tiles, sources, spans, outs, contract):
    return pl.pallas_call(
        functools.partial(products_kernel, spans=spans, outs=outs, contract=contract),
        out_shape=[jax.ShapeDtypeStruct((n * T, T), BF16) for n in outs],
        in_specs=[SMEM] * 3 + [ANY] * (1 + len(sources)),
        out_specs=[VMEM] * len(outs),
        scratch_shapes=[
            pltpu.VMEM(tiles.shape, BF16),
            pltpu.VMEM((sum(spans), T), BF16),
            pltpu.VMEM((sum(outs), T, T), F32),
            pltpu.SemaphoreType.DMA((len(spans) + 1,)),
        ],
        compiler_params=PARAMS,
    )(live, in_place, out_place, tiles, *sources)


def pack_kernel(at_row, *refs):
    pieces, sends, (lists, counts), (held, words, table, sems) = (
        refs[:8],
        refs[8:14],
        refs[14:16],
        refs[16:],
    )
    copies = [pltpu.make_async_copy(p, held.at[k], sems.at[k]) for k, p in enumerate(pieces)]
    for copy in copies:
        copy.start()
    for copy in copies:
        copy.wait()
    for n in range(6):
        piece = n + 5 if n < 3 else n - 2
        words[pl.ds(n * 8, 8)] = held[piece, pl.ds(HALF, META)].astype(F32)[:8].astype(I32)
    copy = pltpu.make_async_copy(words, table, sems.at[0])
    copy.start()
    copy.wait()
    x, z = at_row[0] // 4, lax.rem(at_row[0], 4)
    for n in range(6):

        def step(slot, count, n=n):
            col = table[n * 8, slot]
            if n < 3:
                match = (col >= 0) & ((col & 0x38) == z * 16)
                inner = ((col >> 6) - x) & 3
                piece = inner
            else:
                match = (col >= 0) & ((col & 0xC8) == x * 64 + 8)
                inner = ((col >> 4) - z) & 3
                piece = 4 + inner
            match = match & (count < CAP)

            @pl.when(match)
            def _():
                lists[n * CAP + count] = inner * 8 + (col & 7)
                sends[n][block(count)] = held[piece, block(col & 7)]

            return count + jnp.where(match, 1, 0)

        counts[n] = lax.fori_loop(0, table[n * 8, 65], step, 0)


def pack(at_row, pieces):
    return pl.pallas_call(
        pack_kernel,
        out_shape=[jax.ShapeDtypeStruct((CAP * T, T), BF16)] * 6
        + [jax.ShapeDtypeStruct((6 * CAP,), I32), jax.ShapeDtypeStruct((6,), I32)],
        in_specs=[SMEM] + [ANY] * 8,
        out_specs=[VMEM] * 6 + [SMEM] * 2,
        scratch_shapes=[
            pltpu.VMEM((8, HALF + META, T), BF16),
            pltpu.VMEM((48, T), I32),
            pltpu.SMEM((48, T), I32),
            pltpu.SemaphoreType.DMA((8,)),
        ],
        compiler_params=PARAMS,
    )(at_row, *pieces)


def combine_kernel(lists, counts, own, *refs):
    parts, outs, (total,) = refs[:6], refs[6:14], refs[14:]

    def widen(k, carry):
        total[k] = own[block(k)].astype(F32)
        return carry

    lax.fori_loop(0, 64, widen, 0)
    for n, part in enumerate(parts):

        def add(k, carry, n=n, part=part):
            total[lists[n * CAP + k] + n // 3 * 32] += part[block(k)].astype(F32)
            return carry

        lax.fori_loop(0, counts[n], add, 0)
    for n, ref in enumerate(outs):

        def out(k, carry, n=n, ref=ref):
            ref[block(k)] = total[n * 8 + k].astype(ref.dtype)
            return carry

        lax.fori_loop(0, 8, out, 0)


def combine(lists, counts, own, parts):
    return pl.pallas_call(
        combine_kernel,
        out_shape=[
            jax.ShapeDtypeStruct((HALF, T), BF16 if d else F32) for _ in range(2) for d in range(4)
        ],
        in_specs=[SMEM] * 2 + [VMEM] * 7,
        out_specs=[VMEM] * 8,
        scratch_shapes=[pltpu.VMEM((64, T, T), F32)],
        compiler_params=PARAMS,
    )(lists, counts, own, *parts)


def dense_kernel(m0, m1, m2, m3, grad, weight, offset, hidden, projected, sums):
    @pl.when(pl.program_id(0) == 0)
    def _():
        sums[...] = jnp.zeros_like(sums)

    mixed = m0[...].astype(F32) + m1[...].astype(F32) + m2[...].astype(F32) + m3[...].astype(F32)
    high = mixed.astype(BF16)
    low = (mixed - high.astype(F32)).astype(BF16)
    w = weight[...]
    pre = jnp.dot(high, w, preferred_element_type=F32)
    pre = pre + jnp.dot(low, w, preferred_element_type=F32) + offset[...]
    s = jax.nn.sigmoid(pre)
    hidden[...] = (pre * s).astype(BF16)
    slope = (grad[...].astype(F32) * s * (1.0 + pre * (1.0 - s))).astype(BF16)
    projected[...] = lax.dot_general(
        slope, w, (((1,), (1,)), ((), ())), preferred_element_type=F32
    ).astype(BF16)
    over_rows = (((0,), (0,)), ((), ()))
    sums[:T] += lax.dot_general(
        high, slope, over_rows, preferred_element_type=F32
    ) + lax.dot_general(low, slope, over_rows, preferred_element_type=F32)
    sums[T:] += jnp.sum(slope.astype(F32).reshape(-1, 8, slope.shape[1]), axis=0)


def dense(parts, grad, weight, offset):
    rows, width = parts[0].shape[0], weight.shape[1]
    step = 512
    half = pl.BlockSpec((step, T), lambda i: (i, 0))
    full = pl.BlockSpec((step, width), lambda i: (i, 0))
    return pl.pallas_call(
        dense_kernel,
        grid=(rows // step,),
        out_shape=[
            jax.ShapeDtypeStruct((rows, width), BF16),
            jax.ShapeDtypeStruct((rows, T), BF16),
            jax.ShapeDtypeStruct((T + 8, width), F32),
        ],
        in_specs=[half] * 4
        + [
            full,
            pl.BlockSpec((T, width), lambda i: (0, 0)),
            pl.BlockSpec((1, width), lambda i: (0, 0)),
        ],
        out_specs=[full, half, pl.BlockSpec((T + 8, width), lambda i: (0, 0))],
        compiler_params=PARAMS,
    )(*parts, grad, weight, offset)


def on_device(features, weight, offset, tile_values, tile_rows, tile_cols, live_tiles, grad_hidden):
    tiles = tile_values.reshape(tile_values.shape[2:])
    nodes_here = features.shape[0]
    scaling = 1.0 / math.sqrt(nodes_here * lax.axis_size("row") * lax.axis_size("col"))
    at_row, at_col = lax.axis_index("row"), lax.axis_index("col")
    live, cols = live_tiles.reshape(1), tile_cols.reshape(-1)
    row_place, col_place, dense_place, named, overflow = places(
        tile_rows.reshape(-1), cols, live, at_row, at_col
    )

    meta = jnp.concatenate([named, overflow.astype(I32)[None], live, jnp.zeros(62, I32)])
    meta = jnp.broadcast_to(meta.astype(BF16), (META, T))
    first = ring_gather(jnp.concatenate([features[:HALF], meta]), along_x)
    second = ring_gather(jnp.concatenate([features[HALF:], meta]), along_z)
    *sends, lists, counts = pack(at_row.reshape(1), first + second)
    named_blocks = (
        ring_send([None] + sends[:3], along_z)[1:] + ring_send([None] + sends[3:], along_x)[1:]
    )
    full = functools.reduce(jnp.maximum, [piece[HALF, 64] for piece in first])
    full = jnp.broadcast_to(full.astype(F32), (8, T))
    for along in (along_z, along_y):
        full = functools.reduce(jnp.maximum, ring_gather(full, along))
    full = jnp.maximum(full, other_core(full))[0, 0] > 0.5

    def forward_all(first, second, named_blocks):
        whole = [jnp.concatenate([p[:HALF] for p in half]) for half in (first, second)]
        whole = ring_gather(whole[0], along_z) + ring_gather(whole[1], along_x)
        return products(
            live, dense_place, row_place, tiles, whole, (4 * HALF,) * 8, (64, 64), (1,)
        )

    def forward_named(first, second, named_blocks):
        return products(
            live,
            col_place,
            row_place,
            tiles,
            first + second + named_blocks,
            (HALF,) * 8 + (CAP * T,) * 6,
            (64, 64),
            (1,),
        )

    send, keep = lax.cond(full, forward_all, forward_named, first, second, named_blocks)

    both = keep.astype(F32) + other_core(send).astype(F32)
    both = both.reshape(4, nodes_here, T)
    mixed_parts = ring_send([both[d].astype(BF16) for d in range(4)], along_y)
    hidden, projected, sums = dense(mixed_parts, grad_hidden, weight, offset.reshape(1, -1))

    own = ring_gather(projected, along_y)
    gathered = [other_core(piece) for piece in own] + own

    for along in (along_x, along_z, along_y):
        sums = ring_sum(sums, along)
    sums = (sums + other_core(sums)) * scaling

    here, *parts = products(
        live,
        row_place,
        col_place,
        tiles,
        gathered,
        (nodes_here,) * 8,
        (64,) + (CAP,) * 6,
        (0,),
    )
    parts = (
        ring_send([None] + parts[:3], along_z)[1:] + ring_send([None] + parts[3:], along_x)[1:]
    )

    def backward_all(here, parts, gathered):
        outs = products(
            live, row_place, dense_place, tiles, gathered, (nodes_here,) * 8, (32,) * 8, (0,)
        )
        result = []
        for pieces, along in ((outs[:4], along_z), (outs[4:], along_x)):
            mine = total_of(ring_send(pieces, along)).reshape(4, HALF, T)
            result += [mine[0]] + [mine[d].astype(BF16) for d in (1, 2, 3)]
        return result

    def backward_named(here, parts, gathered):
        return list(combine(lists, counts, here, parts))

    outs = lax.cond(full, backward_all, backward_named, here, parts, gathered)
    first = total_of(ring_send(outs[:4], along_x))
    second = total_of(ring_send(outs[4:], along_z))
    grad_features = jnp.concatenate([first, second])
    return (hidden, grad_features, sums[:T], jnp.sum(sums[T:], axis=0))


def solution(mesh):
    in_specs = (
        P(("col", "row"), None),
        P(),
        P(),
        P("row", "col", None, None, None),
        P("row", "col", None),
        P("row", "col", None),
        P("row", "col"),
        P(("row", "col"), None),
    )
    out_specs = (P(("row", "col"), None), P(("col", "row"), None), P(), P())
    return jax.shard_map(
        on_device, mesh=mesh, in_specs=in_specs, out_specs=out_specs, check_vma=False
    )
```

```python
import functools
import math

import jax
import jax.numpy as jnp
from jax import lax
from jax.experimental import pallas as pl
from jax.experimental.pallas import tpu as pltpu
from jax.sharding import PartitionSpec as P

T = 128
F32, BF16, I32 = jnp.float32, jnp.bfloat16, jnp.int32
VMEM_BYTES = 56 * 1024 * 1024
GROUP = 4
HALF = 8 * T
META = 16
CAP = 16
FLAG_LANE = 64
SMEM = pl.BlockSpec(memory_space=pltpu.SMEM)
VMEM = pl.BlockSpec(memory_space=pltpu.VMEM)
ANY = pl.BlockSpec(memory_space=pl.ANY)
PARAMS = pltpu.CompilerParams(vmem_limit_bytes=VMEM_BYTES)


def along_x(value, to):
    pairs = [(x * 4 + z, to(x) % 4 * 4 + z) for x in range(4) for z in range(4)]
    return lax.ppermute(value, "row", pairs)


def along_z(value, to):
    pairs = [(x * 4 + z, x * 4 + to(z) % 4) for x in range(4) for z in range(4)]
    return lax.ppermute(value, "row", pairs)


def along_y(value, to):
    pairs = [(y * 2 + k, to(y) % 4 * 2 + k) for y in range(4) for k in range(2)]
    return lax.ppermute(value, "col", pairs)


def other_core(value):
    pairs = [(y * 2 + k, y * 2 + 1 - k) for y in range(4) for k in range(2)]
    return lax.ppermute(value, "col", pairs)


def ahead(step):
    return lambda at: at + step


def ring_gather(value, along):
    return [value, along(value, ahead(-1)), along(value, ahead(2)), along(value, ahead(1))]


def ring_swap(pieces, along):
    return [
        pieces[0],
        along(pieces[3], ahead(-1)),
        along(pieces[2], ahead(2)),
        along(pieces[1], ahead(1)),
    ]


def swap_pairs(value, along, bit):
    return along(value, lambda at: at ^ bit)


def total_of(pieces):
    return sum(piece.astype(F32) for piece in pieces)


def block(place):
    return pl.ds(pl.multiple_of(place * T, T), T)


def prepare_kernel(at_row, at_col, live_ref, rows_ref, cols_ref, features, first_out, second_out, tables, sems):
    outs = (first_out, second_out)
    copies = [
        pltpu.make_async_copy(
            features.at[pl.ds(k * HALF, HALF)], outs[k].at[pl.ds(0, HALF)], sems.at[k]
        )
        for k in range(2)
    ]
    for copy in copies:
        copy.start()
    live = live_ref[0]
    x, z = at_row[0] >> 2, at_row[0] & 3
    y, core = at_col[0] >> 1, at_col[0] & 1
    rows, cols = rows_ref[...], cols_ref[...]
    slots = cols.shape[1]

    same_core = jnp.where(((rows >> 4) & 1) == core, 64, 0)
    row_place = same_core + (((rows >> 5) - y) & 3) * 16 + (rows & 15)
    dx, dz = ((cols >> 6) - x) & 3, ((cols >> 4) - z) & 3
    half = (cols >> 3) & 1
    outer, inner = jnp.where(half == 0, dz, dx), jnp.where(half == 0, dx, dz)
    group, code = half * 4 + outer, inner * 8 + (cols & 7)
    dense_place = group * 32 + code

    t = lax.broadcasted_iota(I32, (slots, slots), 0)
    s = lax.broadcasted_iota(I32, (slots, slots), 1)
    lane = lax.broadcasted_iota(I32, (slots, T), 1).astype(F32)

    def column(row):
        return jnp.sum(jnp.where(t == s, row, 0.0), axis=1, keepdims=True)

    def count(mask, value=1.0):
        return jnp.sum(jnp.where(mask, value, 0.0), axis=0, keepdims=True)

    valid = lax.broadcasted_iota(I32, (1, slots), 1) < live
    cols_f, group_f = cols.astype(F32), group.astype(F32)
    same = column(cols_f) == cols_f
    first = valid & (count(same & (t < s)) == 0.0)
    first_c = column(jnp.where(first, 1.0, 0.0)) > 0.0
    group_c = column(group_f)
    rank = count((t < s) & first_c & (group_c == group_f))
    over = jnp.where(first & (outer != 0) & (rank >= CAP), 1.0, 0.0)
    over = jnp.max(over, axis=1, keepdims=True)
    far = (64 + (half * 3 + outer - 1) * CAP).astype(F32) + jnp.minimum(rank, CAP - 1.0)
    place = jnp.where(outer == 0, (half * 32 + code).astype(F32), far)
    place = count(same & first_c, column(place))
    place = jnp.where(valid, place, 0.0).astype(I32)
    pad = jnp.zeros((5, slots), I32)
    tables[...] = jnp.concatenate([row_place, place, dense_place, pad], axis=0)

    key = column(jnp.where(first & (rank < CAP), group_f * CAP + rank, -1.0))
    wanted = count(key == lane, column(code.astype(F32)))
    amounts = jnp.minimum(count((group_c == lane) & first_c), 1.0 * CAP)
    line = lax.broadcasted_iota(I32, (META, T), 0)
    amounts = jnp.where(lax.broadcasted_iota(I32, (1, T), 1) == FLAG_LANE, over, amounts)
    meta = jnp.where(line == 0, wanted, jnp.where(line == 1, amounts, 0.0)).astype(BF16)
    for ref in outs:
        ref[pl.ds(HALF, META)] = meta
    for copy in copies:
        copy.wait()


def prepare(at_row, at_col, live, rows, cols, features):
    slots = cols.shape[-1]
    return pl.pallas_call(
        prepare_kernel,
        out_shape=[jax.ShapeDtypeStruct((HALF + META, T), BF16)] * 2
        + [jax.ShapeDtypeStruct((8, slots), I32)],
        in_specs=[SMEM] * 3 + [VMEM] * 2 + [ANY],
        out_specs=[VMEM] * 3,
        scratch_shapes=[pltpu.SemaphoreType.DMA((2,))],
        compiler_params=PARAMS,
    )(at_row, at_col, live, rows.reshape(1, slots), cols.reshape(1, slots), features)


def products_kernel(live, tables, tiles_ref, *refs, spans, outs, contract, in_row, out_row):
    n = len(spans)
    sources, out_refs, (tiles, held, total, sems) = refs[:n], refs[n:-4], refs[-4:]
    copies = [pltpu.make_async_copy(tiles_ref, tiles, sems.at[n])]
    start = 0
    for k, (ref, rows) in enumerate(zip(sources, spans)):
        copies.append(
            pltpu.make_async_copy(
                ref.at[pl.ds(0, rows)], held.at[pl.ds(start, rows)], sems.at[k]
            )
        )
        start += rows
    if len(out_refs) > len(outs):
        sources, passed = out_refs[0], out_refs[-1]
        out_refs = out_refs[1:-1]
        copies.append(pltpu.make_async_copy(sources, passed, sems.at[n + 1]))
    for copy in copies:
        copy.start()

    zeros = jnp.zeros((4, T, T), F32)

    def clear(k, carry):
        total[pl.ds(k * 4, 4)] = zeros
        return carry

    lax.fori_loop(0, total.shape[0] // 4, clear, 0)
    for copy in copies:
        copy.wait()

    def group(number, carry):
        products = []
        for k in range(GROUP):
            slot = number * GROUP + k
            product = lax.dot_general(
                tiles[slot],
                held[block(tables[in_row, slot])],
                ((contract, (0,)), ((), ())),
                preferred_element_type=F32,
            )
            products.append(jnp.where(slot < live[0], product, 0.0))
        for k, product in enumerate(products):
            total[tables[out_row, number * GROUP + k]] += product
        return carry

    lax.fori_loop(0, (live[0] + GROUP - 1) // GROUP, group, 0)
    start = 0
    for ref, blocks in zip(out_refs, outs):

        def out(k, carry, ref=ref, start=start):
            ref[block(k)] = total[start + k].astype(BF16)
            return carry

        lax.fori_loop(0, blocks, out, 0)
        start += blocks


def products(live, tables, in_row, out_row, tiles, sources, spans, outs, contract, passed=()):
    kernel = functools.partial(
        products_kernel,
        spans=spans,
        outs=outs,
        contract=contract,
        in_row=in_row,
        out_row=out_row,
    )
    return pl.pallas_call(
        kernel,
        out_shape=[jax.ShapeDtypeStruct((n * T, T), BF16) for n in outs]
        + [jax.ShapeDtypeStruct(p.shape, p.dtype) for p in passed],
        in_specs=[SMEM] * 2 + [ANY] * (1 + len(sources) + len(passed)),
        out_specs=[VMEM] * len(outs) + [ANY] * len(passed),
        scratch_shapes=[
            pltpu.VMEM(tiles.shape, BF16),
            pltpu.VMEM((sum(spans), T), BF16),
            pltpu.VMEM((sum(outs), T, T), F32),
            pltpu.SemaphoreType.DMA((len(spans) + 2,)),
        ],
        compiler_params=PARAMS,
    )(live, tables, tiles, *sources, *passed)


def pack_kernel(*refs):
    pieces, sends, (lists, counts), (held, words, table, sems) = (
        refs[:8],
        refs[8:14],
        refs[14:16],
        refs[16:],
    )
    copies = [pltpu.make_async_copy(p, held.at[k], sems.at[k]) for k, p in enumerate(pieces)]
    for copy in copies:
        copy.start()
    for copy in copies:
        copy.wait()
    metas = [held[k, pl.ds(HALF, META)].astype(F32) for k in range(8)]
    for n in range(6):
        words[pl.ds(n * 8, 8)] = metas[n + 5 if n < 3 else n - 2][:8].astype(I32)
    copy = pltpu.make_async_copy(words, table, sems.at[0])
    copy.start()
    flags = functools.reduce(jnp.maximum, metas[:4]).astype(BF16)
    for n in range(3):
        sends[n][pl.ds(CAP * T, META)] = flags
    copy.wait()
    for n in range(6):
        group = 3 - n if n < 3 else 10 - n
        amount = table[n * 8 + 1, group]
        counts[n] = amount

        def step(k, carry, n=n, group=group):
            code = table[n * 8, group * CAP + k]
            lists[n * CAP + k] = code
            sends[n][block(k)] = held[n // 3 * 4 + (code >> 3), block(code & 7)]
            return carry

        lax.fori_loop(0, amount, step, 0)


def pack(pieces):
    return pl.pallas_call(
        pack_kernel,
        out_shape=[
            jax.ShapeDtypeStruct((CAP * T + (META if n < 3 else 0), T), BF16) for n in range(6)
        ]
        + [jax.ShapeDtypeStruct((6 * CAP,), I32), jax.ShapeDtypeStruct((6,), I32)],
        in_specs=[ANY] * 8,
        out_specs=[VMEM] * 6 + [SMEM] * 2,
        scratch_shapes=[
            pltpu.VMEM((8, HALF + META, T), BF16),
            pltpu.VMEM((48, T), I32),
            pltpu.SMEM((48, T), I32),
            pltpu.SemaphoreType.DMA((8,)),
        ],
        compiler_params=PARAMS,
    )(*pieces)


def combine_kernel(lists, counts, own, *refs):
    parts, outs, (total,) = refs[:6], refs[6:14], refs[14:]

    def widen(k, carry):
        total[k] = own[block(k)].astype(F32)
        return carry

    lax.fori_loop(0, 64, widen, 0)
    for n, part in enumerate(parts):

        def add(k, carry, n=n, part=part):
            total[lists[n * CAP + k] + n // 3 * 32] += part[block(k)].astype(F32)
            return carry

        lax.fori_loop(0, counts[n], add, 0)
    for n, ref in enumerate(outs):

        def out(k, carry, n=n, ref=ref):
            ref[block(k)] = total[n * 8 + k].astype(ref.dtype)
            return carry

        lax.fori_loop(0, 8, out, 0)


def combine(lists, counts, own, parts):
    return pl.pallas_call(
        combine_kernel,
        out_shape=[
            jax.ShapeDtypeStruct((HALF, T), BF16 if d else F32) for _ in range(2) for d in range(4)
        ],
        in_specs=[SMEM] * 2 + [VMEM] * 7,
        out_specs=[VMEM] * 8,
        scratch_shapes=[pltpu.VMEM((64, T, T), F32)],
        compiler_params=PARAMS,
    )(lists, counts, own, *parts)


def dense_kernel(m0, m1, m2, m3, grad, weight, offset, hidden, projected, sums):
    @pl.when(pl.program_id(0) == 0)
    def _():
        sums[...] = jnp.zeros_like(sums)

    mixed = m0[...].astype(F32) + m1[...].astype(F32) + m2[...].astype(F32) + m3[...].astype(F32)
    high = mixed.astype(BF16)
    low = (mixed - high.astype(F32)).astype(BF16)
    w = weight[...]
    pre = jnp.dot(high, w, preferred_element_type=F32)
    pre = pre + jnp.dot(low, w, preferred_element_type=F32) + offset[...]
    s = jax.nn.sigmoid(pre)
    hidden[...] = (pre * s).astype(BF16)
    slope = (grad[...].astype(F32) * s * (1.0 + pre * (1.0 - s))).astype(BF16)
    projected[...] = lax.dot_general(
        slope, w, (((1,), (1,)), ((), ())), preferred_element_type=F32
    ).astype(BF16)
    over_rows = (((0,), (0,)), ((), ()))
    sums[:T] += lax.dot_general(
        high, slope, over_rows, preferred_element_type=F32
    ) + lax.dot_general(low, slope, over_rows, preferred_element_type=F32)
    sums[T:] += jnp.sum(slope.astype(F32).reshape(-1, 8, slope.shape[1]), axis=0)


def dense(parts, grad, weight, offset):
    rows, width = parts[0].shape[0], weight.shape[1]
    step = 512
    half = pl.BlockSpec((step, T), lambda i: (i, 0))
    full = pl.BlockSpec((step, width), lambda i: (i, 0))
    return pl.pallas_call(
        dense_kernel,
        grid=(rows // step,),
        out_shape=[
            jax.ShapeDtypeStruct((rows, width), BF16),
            jax.ShapeDtypeStruct((rows, T), BF16),
            jax.ShapeDtypeStruct((T + 8, width), F32),
        ],
        in_specs=[half] * 4
        + [
            full,
            pl.BlockSpec((T, width), lambda i: (0, 0)),
            pl.BlockSpec((1, width), lambda i: (0, 0)),
        ],
        out_specs=[full, half, pl.BlockSpec((T + 8, width), lambda i: (0, 0))],
        compiler_params=PARAMS,
    )(*parts, grad, weight, offset)


def on_device(features, weight, offset, tile_values, tile_rows, tile_cols, live_tiles, grad_hidden):
    tiles = tile_values.reshape(tile_values.shape[2:])
    nodes_here = features.shape[0]
    scaling = 1.0 / math.sqrt(nodes_here * lax.axis_size("row") * lax.axis_size("col"))
    at_row, at_col = lax.axis_index("row"), lax.axis_index("col")
    live = live_tiles.reshape(1)
    first, second, tables = prepare(
        at_row.reshape(1), at_col.reshape(1), live, tile_rows, tile_cols, features
    )

    first, second = ring_gather(first, along_x), ring_gather(second, along_z)
    *sends, lists, counts = pack(first + second)
    named = (
        ring_swap([None] + sends[:3], along_z)[1:] + ring_swap([None] + sends[3:], along_x)[1:]
    )
    flags = [sends[0]] + named[:3]
    full = functools.reduce(jnp.maximum, [f[CAP * T + 1, FLAG_LANE] for f in flags]) > 0.5

    def forward_all(first, second, named):
        whole = [jnp.concatenate([p[:HALF] for p in half]) for half in (first, second)]
        whole = ring_gather(whole[0], along_z) + ring_gather(whole[1], along_x)
        return products(live, tables, 2, 0, tiles, whole, (4 * HALF,) * 8, (64, 64), (1,))

    def forward_named(first, second, named):
        spans = (HALF,) * 8 + (CAP * T,) * 6
        return products(
            live, tables, 1, 0, tiles, first + second + named, spans, (64, 64), (1,)
        )

    send, keep = lax.cond(full, forward_all, forward_named, first, second, named)

    both = keep.astype(F32) + other_core(send).astype(F32)
    both = both.reshape(4, nodes_here, T)
    mixed_parts = ring_swap([both[d].astype(BF16) for d in range(4)], along_y)
    hidden, projected, sums = dense(mixed_parts, grad_hidden, weight, offset.reshape(1, -1))

    own = ring_gather(projected, along_y)
    gathered = [other_core(piece) for piece in own] + own

    for along in (along_x, along_z):
        sums = sums + swap_pairs(sums, along, 1)
        sums = sums + swap_pairs(sums, along, 2)

    here, *parts, sums = products(
        live,
        tables,
        0,
        1,
        tiles,
        gathered,
        (nodes_here,) * 8,
        (64,) + (CAP,) * 6,
        (0,),
        (sums,),
    )
    sums = sums + swap_pairs(sums, along_y, 1)
    sums = sums + swap_pairs(sums, along_y, 2)
    sums = (sums + other_core(sums)) * scaling

    parts = (
        ring_swap([None] + parts[:3], along_z)[1:] + ring_swap([None] + parts[3:], along_x)[1:]
    )

    def backward_all(here, parts, gathered):
        outs = products(
            live, tables, 0, 2, tiles, gathered, (nodes_here,) * 8, (32,) * 8, (0,)
        )
        result = []
        for pieces, along in ((outs[:4], along_z), (outs[4:], along_x)):
            mine = total_of(ring_swap(pieces, along)).reshape(4, HALF, T)
            result += [mine[0]] + [mine[d].astype(BF16) for d in (1, 2, 3)]
        return result

    def backward_named(here, parts, gathered):
        return list(combine(lists, counts, here, parts))

    outs = lax.cond(full, backward_all, backward_named, here, parts, gathered)
    first = total_of(ring_swap(outs[:4], along_x))
    second = total_of(ring_swap(outs[4:], along_z))
    grad_features = jnp.concatenate([first, second])
    return (hidden, grad_features, sums[:T], jnp.sum(sums[T:], axis=0))


def solution(mesh):
    in_specs = (
        P(("col", "row"), None),
        P(),
        P(),
        P("row", "col", None, None, None),
        P("row", "col", None),
        P("row", "col", None),
        P("row", "col"),
        P(("row", "col"), None),
    )
    out_specs = (P(("row", "col"), None), P(("col", "row"), None), P(), P())
    return jax.shard_map(
        on_device, mesh=mesh, in_specs=in_specs, out_specs=out_specs, check_vma=False
    )
```

```python
import functools
import math

import jax
import jax.numpy as jnp
from jax import lax
from jax.experimental import pallas as pl
from jax.experimental.pallas import tpu as pltpu
from jax.sharding import PartitionSpec as P

T = 128
F32, BF16, I32 = jnp.float32, jnp.bfloat16, jnp.int32
VMEM_BYTES = 56 * 1024 * 1024
GROUP = 4
HALF = 8 * T
META = 16
CAP = 16
FLAG_LANE = 64
SMEM = pl.BlockSpec(memory_space=pltpu.SMEM)
VMEM = pl.BlockSpec(memory_space=pltpu.VMEM)
ANY = pl.BlockSpec(memory_space=pl.ANY)
PARAMS = pltpu.CompilerParams(vmem_limit_bytes=VMEM_BYTES)


def along_x(value, to):
    pairs = [(x * 4 + z, to(x) % 4 * 4 + z) for x in range(4) for z in range(4)]
    return lax.ppermute(value, "row", pairs)


def along_z(value, to):
    pairs = [(x * 4 + z, x * 4 + to(z) % 4) for x in range(4) for z in range(4)]
    return lax.ppermute(value, "row", pairs)


def along_y(value, to):
    pairs = [(y * 2 + k, to(y) % 4 * 2 + k) for y in range(4) for k in range(2)]
    return lax.ppermute(value, "col", pairs)


def other_core(value):
    pairs = [(y * 2 + k, y * 2 + 1 - k) for y in range(4) for k in range(2)]
    return lax.ppermute(value, "col", pairs)


def ahead(step):
    return lambda at: at + step


def ring_gather(value, along):
    return [value, along(value, ahead(-1)), along(value, ahead(2)), along(value, ahead(1))]


def ring_swap(pieces, along):
    return [
        pieces[0],
        along(pieces[3], ahead(-1)),
        along(pieces[2], ahead(2)),
        along(pieces[1], ahead(1)),
    ]


def total_of(pieces):
    return sum(piece.astype(F32) for piece in pieces)


def block(place):
    return pl.ds(pl.multiple_of(place * T, T), T)


def prepare_kernel(at_row, at_col, live_ref, rows_ref, cols_ref, features, first_out, second_out, tables, sems):
    outs = (first_out, second_out)
    copies = [
        pltpu.make_async_copy(
            features.at[pl.ds(k * HALF, HALF)], outs[k].at[pl.ds(0, HALF)], sems.at[k]
        )
        for k in range(2)
    ]
    for copy in copies:
        copy.start()
    live = live_ref[0]
    x, z = at_row[0] >> 2, at_row[0] & 3
    y, core = at_col[0] >> 1, at_col[0] & 1
    rows, cols = rows_ref[...], cols_ref[...]
    slots = cols.shape[1]

    same_core = jnp.where(((rows >> 4) & 1) == core, 64, 0)
    row_place = same_core + (((rows >> 5) - y) & 3) * 16 + (rows & 15)
    dx, dz = ((cols >> 6) - x) & 3, ((cols >> 4) - z) & 3
    half = (cols >> 3) & 1
    outer, inner = jnp.where(half == 0, dz, dx), jnp.where(half == 0, dx, dz)
    group, code = half * 4 + outer, inner * 8 + (cols & 7)
    dense_place = group * 32 + code

    t = lax.broadcasted_iota(I32, (slots, slots), 0)
    s = lax.broadcasted_iota(I32, (slots, slots), 1)
    lane = lax.broadcasted_iota(I32, (slots, T), 1).astype(F32)

    def column(row):
        return jnp.sum(jnp.where(t == s, row, 0.0), axis=1, keepdims=True)

    def count(mask, value=1.0):
        return jnp.sum(jnp.where(mask, value, 0.0), axis=0, keepdims=True)

    valid = lax.broadcasted_iota(I32, (1, slots), 1) < live
    cols_f, group_f = cols.astype(F32), group.astype(F32)
    same = column(cols_f) == cols_f
    first = valid & (count(same & (t < s)) == 0.0)
    first_c = column(jnp.where(first, 1.0, 0.0)) > 0.0
    group_c = column(group_f)
    rank = count((t < s) & first_c & (group_c == group_f))
    over = jnp.where(first & (outer != 0) & (rank >= CAP), 1.0, 0.0)
    over = jnp.max(over, axis=1, keepdims=True)
    far = (64 + (half * 3 + outer - 1) * CAP).astype(F32) + jnp.minimum(rank, CAP - 1.0)
    place = jnp.where(outer == 0, (half * 32 + code).astype(F32), far)
    place = count(same & first_c, column(place))
    place = jnp.where(valid, place, 0.0).astype(I32)
    pad = jnp.zeros((5, slots), I32)
    tables[...] = jnp.concatenate([row_place, place, dense_place, pad], axis=0)

    key = column(jnp.where(first & (rank < CAP), group_f * CAP + rank, -1.0))
    wanted = count(key == lane, column(code.astype(F32)))
    amounts = jnp.minimum(count((group_c == lane) & first_c), 1.0 * CAP)
    line = lax.broadcasted_iota(I32, (META, T), 0)
    amounts = jnp.where(lax.broadcasted_iota(I32, (1, T), 1) == FLAG_LANE, over, amounts)
    meta = jnp.where(line == 0, wanted, jnp.where(line == 1, amounts, 0.0)).astype(BF16)
    for ref in outs:
        ref[pl.ds(HALF, META)] = meta
    for copy in copies:
        copy.wait()


def prepare(at_row, at_col, live, rows, cols, features):
    slots = cols.shape[-1]
    return pl.pallas_call(
        prepare_kernel,
        out_shape=[jax.ShapeDtypeStruct((HALF + META, T), BF16)] * 2
        + [jax.ShapeDtypeStruct((8, slots), I32)],
        in_specs=[SMEM] * 3 + [VMEM] * 2 + [ANY],
        out_specs=[VMEM] * 3,
        scratch_shapes=[pltpu.SemaphoreType.DMA((2,))],
        compiler_params=PARAMS,
    )(at_row, at_col, live, rows.reshape(1, slots), cols.reshape(1, slots), features)


def products_kernel(live, tables, tiles_ref, *refs, spans, outs, contract, in_row, out_row):
    n = len(spans)
    sources, out_refs, (tiles, held, total, sems) = refs[:n], refs[n:-4], refs[-4:]
    copies = [pltpu.make_async_copy(tiles_ref, tiles, sems.at[n])]
    start = 0
    for k, (ref, rows) in enumerate(zip(sources, spans)):
        copies.append(
            pltpu.make_async_copy(
                ref.at[pl.ds(0, rows)], held.at[pl.ds(start, rows)], sems.at[k]
            )
        )
        start += rows
    for copy in copies:
        copy.start()

    zeros = jnp.zeros((4, T, T), F32)

    def clear(k, carry):
        total[pl.ds(k * 4, 4)] = zeros
        return carry

    lax.fori_loop(0, total.shape[0] // 4, clear, 0)
    for copy in copies:
        copy.wait()

    def group(number, carry):
        products = []
        for k in range(GROUP):
            slot = number * GROUP + k
            product = lax.dot_general(
                tiles[slot],
                held[block(tables[in_row, slot])],
                ((contract, (0,)), ((), ())),
                preferred_element_type=F32,
            )
            products.append(jnp.where(slot < live[0], product, 0.0))
        for k, product in enumerate(products):
            total[tables[out_row, number * GROUP + k]] += product
        return carry

    lax.fori_loop(0, (live[0] + GROUP - 1) // GROUP, group, 0)
    start = 0
    for ref, blocks in zip(out_refs, outs):

        def out(k, carry, ref=ref, start=start):
            ref[block(k)] = total[start + k].astype(BF16)
            return carry

        lax.fori_loop(0, blocks, out, 0)
        start += blocks


def products(live, tables, in_row, out_row, tiles, sources, spans, outs, contract):
    kernel = functools.partial(
        products_kernel,
        spans=spans,
        outs=outs,
        contract=contract,
        in_row=in_row,
        out_row=out_row,
    )
    return pl.pallas_call(
        kernel,
        out_shape=[jax.ShapeDtypeStruct((n * T, T), BF16) for n in outs],
        in_specs=[SMEM] * 2 + [ANY] * (1 + len(sources)),
        out_specs=[VMEM] * len(outs),
        scratch_shapes=[
            pltpu.VMEM(tiles.shape, BF16),
            pltpu.VMEM((sum(spans), T), BF16),
            pltpu.VMEM((sum(outs), T, T), F32),
            pltpu.SemaphoreType.DMA((len(spans) + 1,)),
        ],
        compiler_params=PARAMS,
    )(live, tables, tiles, *sources)


def pack_kernel(*refs):
    pieces, sends, (lists, counts), (held, words, table, sems) = (
        refs[:8],
        refs[8:14],
        refs[14:16],
        refs[16:],
    )
    copies = [pltpu.make_async_copy(p, held.at[k], sems.at[k]) for k, p in enumerate(pieces)]
    for copy in copies:
        copy.start()
    for copy in copies:
        copy.wait()
    metas = [held[k, pl.ds(HALF, META)].astype(F32) for k in range(8)]
    for n in range(6):
        words[pl.ds(n * 8, 8)] = metas[n + 5 if n < 3 else n - 2][:8].astype(I32)
    copy = pltpu.make_async_copy(words, table, sems.at[0])
    copy.start()
    flags = functools.reduce(jnp.maximum, metas[:4]).astype(BF16)
    for n in range(3):
        sends[n][pl.ds(CAP * T, META)] = flags
    copy.wait()
    for n in range(6):
        group = 3 - n if n < 3 else 10 - n
        amount = table[n * 8 + 1, group]
        counts[n] = amount

        def step(k, carry, n=n, group=group):
            code = table[n * 8, group * CAP + k]
            lists[n * CAP + k] = code
            sends[n][block(k)] = held[n // 3 * 4 + (code >> 3), block(code & 7)]
            return carry

        lax.fori_loop(0, amount, step, 0)


def pack(pieces):
    return pl.pallas_call(
        pack_kernel,
        out_shape=[
            jax.ShapeDtypeStruct((CAP * T + (META if n < 3 else 0), T), BF16) for n in range(6)
        ]
        + [jax.ShapeDtypeStruct((6 * CAP,), I32), jax.ShapeDtypeStruct((6,), I32)],
        in_specs=[ANY] * 8,
        out_specs=[VMEM] * 6 + [SMEM] * 2,
        scratch_shapes=[
            pltpu.VMEM((8, HALF + META, T), BF16),
            pltpu.VMEM((48, T), I32),
            pltpu.SMEM((48, T), I32),
            pltpu.SemaphoreType.DMA((8,)),
        ],
        compiler_params=PARAMS,
    )(*pieces)


def combine_kernel(lists, counts, own, *refs):
    parts, outs, (total,) = refs[:6], refs[6:14], refs[14:]

    def widen(k, carry):
        total[k] = own[block(k)].astype(F32)
        return carry

    lax.fori_loop(0, 64, widen, 0)
    for n, part in enumerate(parts):

        def add(k, carry, n=n, part=part):
            total[lists[n * CAP + k] + n // 3 * 32] += part[block(k)].astype(F32)
            return carry

        lax.fori_loop(0, counts[n], add, 0)
    for n, ref in enumerate(outs):

        def out(k, carry, n=n, ref=ref):
            ref[block(k)] = total[n * 8 + k].astype(ref.dtype)
            return carry

        lax.fori_loop(0, 8, out, 0)


def combine(lists, counts, own, parts):
    return pl.pallas_call(
        combine_kernel,
        out_shape=[
            jax.ShapeDtypeStruct((HALF, T), BF16 if d else F32) for _ in range(2) for d in range(4)
        ],
        in_specs=[SMEM] * 2 + [VMEM] * 7,
        out_specs=[VMEM] * 8,
        scratch_shapes=[pltpu.VMEM((64, T, T), F32)],
        compiler_params=PARAMS,
    )(lists, counts, own, *parts)


def add_up_kernel(sums, _, out):
    out[...] = jnp.sum(sums[...], axis=0)


def add_up(sums, after):
    return pl.pallas_call(
        add_up_kernel,
        out_shape=jax.ShapeDtypeStruct(sums.shape[1:], F32),
        in_specs=[VMEM, ANY],
        out_specs=VMEM,
        compiler_params=PARAMS,
    )(sums, after)


def finish_kernel(*refs, scaling):
    pieces, sums, (nodes, weight, offset) = refs[:8], refs[8], refs[9:]
    for k in range(2):
        nodes[pl.ds(k * HALF, HALF)] = total_of([ref[...] for ref in pieces[4 * k : 4 * k + 4]])
    total = jnp.sum(sums[...], axis=0) * scaling
    weight[...] = total[:T]
    offset[...] = jnp.sum(total[T:], axis=0, keepdims=True)


def finish(pieces, sums, scaling):
    width = sums.shape[-1]
    return pl.pallas_call(
        functools.partial(finish_kernel, scaling=scaling),
        out_shape=[
            jax.ShapeDtypeStruct((2 * HALF, T), F32),
            jax.ShapeDtypeStruct((T, width), F32),
            jax.ShapeDtypeStruct((1, width), F32),
        ],
        in_specs=[VMEM] * 9,
        out_specs=[VMEM] * 3,
        compiler_params=PARAMS,
    )(*pieces, sums)


def dense_kernel(m0, m1, m2, m3, grad, weight, offset, hidden, projected, sums):
    @pl.when(pl.program_id(0) == 0)
    def _():
        sums[...] = jnp.zeros_like(sums)

    mixed = m0[...].astype(F32) + m1[...].astype(F32) + m2[...].astype(F32) + m3[...].astype(F32)
    high = mixed.astype(BF16)
    low = (mixed - high.astype(F32)).astype(BF16)
    w = weight[...]
    pre = jnp.dot(high, w, preferred_element_type=F32)
    pre = pre + jnp.dot(low, w, preferred_element_type=F32) + offset[...]
    s = jax.nn.sigmoid(pre)
    hidden[...] = (pre * s).astype(BF16)
    slope = (grad[...].astype(F32) * s * (1.0 + pre * (1.0 - s))).astype(BF16)
    projected[...] = lax.dot_general(
        slope, w, (((1,), (1,)), ((), ())), preferred_element_type=F32
    ).astype(BF16)
    over_rows = (((0,), (0,)), ((), ()))
    sums[:T] += lax.dot_general(
        high, slope, over_rows, preferred_element_type=F32
    ) + lax.dot_general(low, slope, over_rows, preferred_element_type=F32)
    sums[T:] += jnp.sum(slope.astype(F32).reshape(-1, 8, slope.shape[1]), axis=0)


def dense(parts, grad, weight, offset):
    rows, width = parts[0].shape[0], weight.shape[1]
    step = 512
    half = pl.BlockSpec((step, T), lambda i: (i, 0))
    full = pl.BlockSpec((step, width), lambda i: (i, 0))
    return pl.pallas_call(
        dense_kernel,
        grid=(rows // step,),
        out_shape=[
            jax.ShapeDtypeStruct((rows, width), BF16),
            jax.ShapeDtypeStruct((rows, T), BF16),
            jax.ShapeDtypeStruct((T + 8, width), F32),
        ],
        in_specs=[half] * 4
        + [
            full,
            pl.BlockSpec((T, width), lambda i: (0, 0)),
            pl.BlockSpec((1, width), lambda i: (0, 0)),
        ],
        out_specs=[full, half, pl.BlockSpec((T + 8, width), lambda i: (0, 0))],
        compiler_params=PARAMS,
    )(*parts, grad, weight, offset)


def on_device(features, weight, offset, tile_values, tile_rows, tile_cols, live_tiles, grad_hidden):
    tiles = tile_values.reshape(tile_values.shape[2:])
    nodes_here = features.shape[0]
    scaling = 1.0 / math.sqrt(nodes_here * lax.axis_size("row") * lax.axis_size("col"))
    at_row, at_col = lax.axis_index("row"), lax.axis_index("col")
    live = live_tiles.reshape(1)
    first, second, tables = prepare(
        at_row.reshape(1), at_col.reshape(1), live, tile_rows, tile_cols, features
    )

    first, second = ring_gather(first, along_x), ring_gather(second, along_z)
    *sends, lists, counts = pack(first + second)
    named = (
        ring_swap([None] + sends[:3], along_z)[1:] + ring_swap([None] + sends[3:], along_x)[1:]
    )
    flags = [sends[0]] + named[:3]
    full = functools.reduce(jnp.maximum, [f[CAP * T + 1, FLAG_LANE] for f in flags]) > 0.5

    def forward_all(first, second, named):
        whole = [jnp.concatenate([p[:HALF] for p in half]) for half in (first, second)]
        whole = ring_gather(whole[0], along_z) + ring_gather(whole[1], along_x)
        return products(live, tables, 2, 0, tiles, whole, (4 * HALF,) * 8, (64, 64), (1,))

    def forward_named(first, second, named):
        spans = (HALF,) * 8 + (CAP * T,) * 6
        return products(
            live, tables, 1, 0, tiles, first + second + named, spans, (64, 64), (1,)
        )

    send, keep = lax.cond(full, forward_all, forward_named, first, second, named)

    both = keep.astype(F32) + other_core(send).astype(F32)
    both = both.reshape(4, nodes_here, T)
    mixed_parts = ring_swap([both[d].astype(BF16) for d in range(4)], along_y)
    hidden, projected, sums = dense(mixed_parts, grad_hidden, weight, offset.reshape(1, -1))

    own = ring_gather(projected, along_y)
    gathered = [other_core(piece) for piece in own] + own

    sums = lax.all_gather(sums, "row", axis=0)

    spans, outs = (nodes_here,) * 8, (64,) + (CAP,) * 6
    here, *parts = products(live, tables, 0, 1, tiles, gathered, spans, outs, (0,))
    sums = lax.all_gather(add_up(sums, here), "col", axis=0)
    parts = (
        ring_swap([None] + parts[:3], along_z)[1:] + ring_swap([None] + parts[3:], along_x)[1:]
    )

    def backward_all(here, parts, gathered):
        outs = products(
            live, tables, 0, 2, tiles, gathered, (nodes_here,) * 8, (32,) * 8, (0,)
        )
        result = []
        for pieces, along in ((outs[:4], along_z), (outs[4:], along_x)):
            mine = total_of(ring_swap(pieces, along)).reshape(4, HALF, T)
            result += [mine[0]] + [mine[d].astype(BF16) for d in (1, 2, 3)]
        return result

    def backward_named(here, parts, gathered):
        return list(combine(lists, counts, here, parts))

    outs = lax.cond(full, backward_all, backward_named, here, parts, gathered)
    pieces = ring_swap(outs[:4], along_x) + ring_swap(outs[4:], along_z)
    grad_features, grad_weight, grad_offset = finish(pieces, sums, scaling)
    return (hidden, grad_features, grad_weight, grad_offset.reshape(-1))


def solution(mesh):
    in_specs = (
        P(("col", "row"), None),
        P(),
        P(),
        P("row", "col", None, None, None),
        P("row", "col", None),
        P("row", "col", None),
        P("row", "col"),
        P(("row", "col"), None),
    )
    out_specs = (P(("row", "col"), None), P(("col", "row"), None), P(), P())
    return jax.shard_map(
        on_device, mesh=mesh, in_specs=in_specs, out_specs=out_specs, check_vma=False
    )
```

```python
import functools
import itertools
import math

import jax
import jax.numpy as jnp
from jax import lax
from jax.experimental import pallas as pl
from jax.experimental.pallas import tpu as pltpu
from jax.sharding import PartitionSpec as P

T = 128
F32, BF16, I32 = jnp.float32, jnp.bfloat16, jnp.int32
VMEM_BYTES = 56 * 1024 * 1024
GROUP = 4
META = 16
CAP = 26
LANES = 32
SMEM = pl.BlockSpec(memory_space=pltpu.SMEM)
VMEM = pl.BlockSpec(memory_space=pltpu.VMEM)
ANY = pl.BlockSpec(memory_space=pl.ANY)
PARAMS = pltpu.CompilerParams(vmem_limit_bytes=VMEM_BYTES)


def along_xz(value, to, x_core):
    pairs = []
    for x, z, y, core in itertools.product(range(4), range(4), range(4), range(2)):
        far = (to(x) % 4, z) if core == x_core else (x, to(z) % 4)
        pairs.append(((x * 4 + z) * 8 + y * 2 + core, (far[0] * 4 + far[1]) * 8 + y * 2 + core))
    return lax.ppermute(value, ("row", "col"), pairs)


def along_inner(value, to):
    return along_xz(value, to, 0)


def along_outer(value, to):
    return along_xz(value, to, 1)


def along_y(value, to):
    pairs = [(y * 2 + k, to(y) % 4 * 2 + k) for y in range(4) for k in range(2)]
    return lax.ppermute(value, "col", pairs)


def other_core(value):
    pairs = [(y * 2 + k, y * 2 + 1 - k) for y in range(4) for k in range(2)]
    return lax.ppermute(value, "col", pairs)


def ahead(step):
    return lambda at: at + step


def ring_gather(value, along):
    return [value, along(value, ahead(-1)), along(value, ahead(2)), along(value, ahead(1))]


def ring_swap(pieces, along):
    return [
        pieces[0],
        along(pieces[3], ahead(-1)),
        along(pieces[2], ahead(2)),
        along(pieces[1], ahead(1)),
    ]


def total_of(pieces):
    return sum(piece.astype(F32) for piece in pieces)


def block(place):
    return pl.ds(pl.multiple_of(place * T, T), T)


def prepare_kernel(
    at_row, at_col, live_ref, rows_ref, cols_ref, features, payload, meta, tables, sem
):
    nodes = features.shape[0]
    copy = pltpu.make_async_copy(features, payload.at[pl.ds(0, nodes)], sem)
    copy.start()
    live = live_ref[0]
    x, z = at_row[0] >> 2, at_row[0] & 3
    y, core = at_col[0] >> 1, at_col[0] & 1
    rows, cols = rows_ref[...], cols_ref[...]
    slots = cols.shape[1]

    same_core = jnp.where(((rows >> 4) & 1) == core, 64, 0)
    row_place = same_core + (((rows >> 5) - y) & 3) * 16 + (rows & 15)
    dx, dz = ((cols >> 6) - x) & 3, ((cols >> 4) - z) & 3
    outer, inner = jnp.where(core == 0, dz, dx), jnp.where(core == 0, dx, dz)
    code = inner * 16 + (cols & 15)
    dense_place = outer * 64 + code

    t = lax.broadcasted_iota(I32, (slots, slots), 0)
    s = lax.broadcasted_iota(I32, (slots, slots), 1)
    lane = lax.broadcasted_iota(I32, (slots, T), 1).astype(F32)

    def column(row):
        return jnp.sum(jnp.where(t == s, row, 0.0), axis=1, keepdims=True)

    def count(mask, value=1.0):
        return jnp.sum(jnp.where(mask, value, 0.0), axis=0, keepdims=True)

    valid = lax.broadcasted_iota(I32, (1, slots), 1) < live
    cols_f, outer_f = cols.astype(F32), outer.astype(F32)
    same = column(cols_f) == cols_f
    first = valid & (count(same & (t < s)) == 0.0)
    first_c = column(jnp.where(first, 1.0, 0.0)) > 0.0
    outer_c = column(outer_f)
    rank = count((t < s) & first_c & (outer_c == outer_f))
    over = jnp.where(first & (outer != 0) & (rank >= CAP), 1.0, 0.0)
    over = jnp.max(over, axis=1, keepdims=True)
    far = (64 + (outer - 1) * CAP).astype(F32) + jnp.minimum(rank, CAP - 1.0)
    place = jnp.where(outer == 0, code.astype(F32), far)
    place = count(same & first_c, column(place))
    place = jnp.where(valid, place, 0.0).astype(I32)
    pad = jnp.zeros((5, slots), I32)
    tables[...] = jnp.concatenate([row_place, place, dense_place, pad], axis=0)

    key = column(jnp.where(first & (rank < CAP), outer_f * LANES + rank, -1.0))
    wanted = count(key == lane, column(code.astype(F32)))
    amounts = jnp.minimum(count((outer_c == lane) & first_c), 1.0 * CAP)
    line = lax.broadcasted_iota(I32, (META, T), 0)
    lines = [wanted, amounts, jnp.broadcast_to(over, (1, T)), jnp.zeros((META - 3, T), F32)]
    meta[...] = jnp.concatenate(lines, axis=0).astype(BF16)
    payload[pl.ds(nodes, META)] = meta[...]
    copy.wait()


def prepare(at_row, at_col, live, rows, cols, features):
    slots = cols.shape[-1]
    return pl.pallas_call(
        prepare_kernel,
        out_shape=[
            jax.ShapeDtypeStruct((features.shape[0] + META, T), BF16),
            jax.ShapeDtypeStruct((META, T), BF16),
            jax.ShapeDtypeStruct((8, slots), I32),
        ],
        in_specs=[SMEM] * 3 + [VMEM] * 2 + [ANY],
        out_specs=[VMEM] * 3,
        scratch_shapes=[pltpu.SemaphoreType.DMA],
        compiler_params=PARAMS,
    )(at_row, at_col, live, rows.reshape(1, slots), cols.reshape(1, slots), features)


def products_kernel(live, tables, tiles_ref, *refs, spans, outs, contract, in_row, out_row):
    n = len(spans)
    sources, out_refs, (tiles, held, total, sems) = refs[:n], refs[n:-4], refs[-4:]
    copies = [pltpu.make_async_copy(tiles_ref, tiles, sems.at[n])]
    start = 0
    for k, (ref, rows) in enumerate(zip(sources, spans)):
        copies.append(
            pltpu.make_async_copy(
                ref.at[pl.ds(0, rows)], held.at[pl.ds(start, rows)], sems.at[k]
            )
        )
        start += rows
    for copy in copies:
        copy.start()

    zeros = jnp.zeros((4, T, T), F32)

    def clear(k, carry):
        total[pl.ds(k * 4, 4)] = zeros
        return carry

    lax.fori_loop(0, total.shape[0] // 4, clear, 0)
    for copy in copies:
        copy.wait()

    def group(number, carry):
        products = []
        for k in range(GROUP):
            slot = number * GROUP + k
            product = lax.dot_general(
                tiles[slot],
                held[block(tables[in_row, slot])],
                ((contract, (0,)), ((), ())),
                preferred_element_type=F32,
            )
            products.append(jnp.where(slot < live[0], product, 0.0))
        for k, product in enumerate(products):
            total[tables[out_row, number * GROUP + k]] += product
        return carry

    lax.fori_loop(0, (live[0] + GROUP - 1) // GROUP, group, 0)
    start = 0
    for ref, blocks in zip(out_refs, outs):

        def out(k, carry, ref=ref, start=start):
            ref[block(k)] = total[start + k].astype(BF16)
            return carry

        lax.fori_loop(0, blocks, out, 0)
        start += blocks


def products(live, tables, in_row, out_row, tiles, sources, spans, outs, contract):
    kernel = functools.partial(
        products_kernel,
        spans=spans,
        outs=outs,
        contract=contract,
        in_row=in_row,
        out_row=out_row,
    )
    return pl.pallas_call(
        kernel,
        out_shape=[jax.ShapeDtypeStruct((n * T, T), BF16) for n in outs],
        in_specs=[SMEM] * 2 + [ANY] * (1 + len(sources)),
        out_specs=[VMEM] * len(outs),
        scratch_shapes=[
            pltpu.VMEM(tiles.shape, BF16),
            pltpu.VMEM((sum(spans), T), BF16),
            pltpu.VMEM((sum(outs), T, T), F32),
            pltpu.SemaphoreType.DMA((len(spans) + 1,)),
        ],
        compiler_params=PARAMS,
    )(live, tables, tiles, *sources)


def pack_kernel(*refs):
    pieces, metas, sends, (lists, counts), (held, words, table, sems) = (
        refs[:4],
        refs[4:7],
        refs[7:10],
        refs[10:12],
        refs[12:],
    )
    nodes = held.shape[1] - META
    copies = [pltpu.make_async_copy(p, held.at[k], sems.at[k]) for k, p in enumerate(pieces)]
    for copy in copies:
        copy.start()
    for n in range(3):
        words[pl.ds(n * 8, 8)] = metas[n][...].astype(F32)[:8].astype(I32)
    fetch = pltpu.make_async_copy(words, table, sems.at[4])
    fetch.start()
    fetch.wait()
    for copy in copies:
        copy.wait()
    said = [held[k, pl.ds(nodes, META)].astype(F32) for k in range(4)]
    said = functools.reduce(jnp.maximum, said).astype(BF16)
    for n in range(3):
        sends[n][pl.ds(CAP * T, META)] = said
        group = 3 - n
        amount = table[n * 8 + 1, group]
        counts[n] = amount

        def step(k, carry, n=n, group=group):
            code = table[n * 8, group * LANES + k]
            lists[n * CAP + k] = code
            sends[n][block(k)] = held[code >> 4, block(code & 15)]
            return carry

        lax.fori_loop(0, amount, step, 0)


def pack(pieces, metas):
    return pl.pallas_call(
        pack_kernel,
        out_shape=[jax.ShapeDtypeStruct((CAP * T + META, T), BF16)] * 3
        + [jax.ShapeDtypeStruct((3 * CAP,), I32), jax.ShapeDtypeStruct((3,), I32)],
        in_specs=[ANY] * 4 + [VMEM] * 3,
        out_specs=[VMEM] * 3 + [SMEM] * 2,
        scratch_shapes=[
            pltpu.VMEM((4,) + pieces[0].shape, BF16),
            pltpu.VMEM((24, T), I32),
            pltpu.SMEM((24, T), I32),
            pltpu.SemaphoreType.DMA((5,)),
        ],
        compiler_params=PARAMS,
    )(*pieces, *metas)


def combine_kernel(lists, counts, own, sums, *refs):
    parts, outs, (total,) = refs[:3], refs[3:7], refs[7:]

    def widen(k, carry):
        total[k] = own[block(k)].astype(F32)
        return carry

    lax.fori_loop(0, 64, widen, 0)
    for n, part in enumerate(parts):

        def add(k, carry, n=n, part=part):
            total[lists[n * CAP + k]] += part[block(k)].astype(F32)
            return carry

        lax.fori_loop(0, counts[n], add, 0)
    for n, ref in enumerate(outs):

        def out(k, carry, n=n, ref=ref):
            ref[block(k)] = total[n * 16 + k].astype(ref.dtype)
            return carry

        lax.fori_loop(0, 16, out, 0)
        if n:
            ref[pl.ds(16 * T, sums.shape[0])] = sums[...]


def combine(lists, counts, own, sums, parts):
    rows = 16 * T
    return pl.pallas_call(
        combine_kernel,
        out_shape=[jax.ShapeDtypeStruct((rows, T), F32)]
        + [jax.ShapeDtypeStruct((rows + sums.shape[0], T), BF16)] * 3,
        in_specs=[SMEM] * 2 + [VMEM] * 5,
        out_specs=[VMEM] * 4,
        scratch_shapes=[pltpu.VMEM((64, T, T), F32)],
        compiler_params=PARAMS,
    )(lists, counts, own, sums, *parts)


def finish_kernel(*refs, scaling):
    pieces, sums, (nodes, weight, offset) = refs[:4], refs[4], refs[5:]
    rows = nodes.shape[0]
    nodes[...] = total_of([ref[pl.ds(0, rows)] for ref in pieces])
    lines = sums.shape[0]
    for k in range(2):
        part = pl.ds(k * T, T)
        total = sums[:, part]
        for ref in pieces[1:]:
            total = total + ref[pl.ds(rows + k * lines, lines)].astype(F32)
        total = total * scaling
        weight[:, part] = total[:T]
        offset[:, part] = jnp.sum(total[T:], axis=0, keepdims=True)


def finish(pieces, sums, scaling):
    width = sums.shape[-1]
    return pl.pallas_call(
        functools.partial(finish_kernel, scaling=scaling),
        out_shape=[
            jax.ShapeDtypeStruct(pieces[0].shape, F32),
            jax.ShapeDtypeStruct((T, width), F32),
            jax.ShapeDtypeStruct((1, width), F32),
        ],
        in_specs=[VMEM] * 5,
        out_specs=[VMEM] * 3,
        compiler_params=PARAMS,
    )(*pieces, sums)


def dense_kernel(m0, m1, m2, m3, grad, weight, offset, hidden, projected, sums):
    @pl.when(pl.program_id(0) == 0)
    def _():
        sums[...] = jnp.zeros_like(sums)

    mixed = m0[...].astype(F32) + m1[...].astype(F32) + m2[...].astype(F32) + m3[...].astype(F32)
    high = mixed.astype(BF16)
    low = (mixed - high.astype(F32)).astype(BF16)
    w = weight[...]
    pre = jnp.dot(high, w, preferred_element_type=F32)
    pre = pre + jnp.dot(low, w, preferred_element_type=F32) + offset[...]
    s = jax.nn.sigmoid(pre)
    hidden[...] = (pre * s).astype(BF16)
    slope = (grad[...].astype(F32) * s * (1.0 + pre * (1.0 - s))).astype(BF16)
    projected[...] = lax.dot_general(
        slope, w, (((1,), (1,)), ((), ())), preferred_element_type=F32
    ).astype(BF16)
    over_rows = (((0,), (0,)), ((), ()))
    sums[:T] += lax.dot_general(
        high, slope, over_rows, preferred_element_type=F32
    ) + lax.dot_general(low, slope, over_rows, preferred_element_type=F32)
    sums[T:] += jnp.sum(slope.astype(F32).reshape(-1, 8, slope.shape[1]), axis=0)


def dense(parts, grad, weight, offset):
    rows, width = parts[0].shape[0], weight.shape[1]
    step = 512
    half = pl.BlockSpec((step, T), lambda i: (i, 0))
    full = pl.BlockSpec((step, width), lambda i: (i, 0))
    return pl.pallas_call(
        dense_kernel,
        grid=(rows // step,),
        out_shape=[
            jax.ShapeDtypeStruct((rows, width), BF16),
            jax.ShapeDtypeStruct((rows, T), BF16),
            jax.ShapeDtypeStruct((T + 8, width), F32),
        ],
        in_specs=[half] * 4
        + [
            full,
            pl.BlockSpec((T, width), lambda i: (0, 0)),
            pl.BlockSpec((1, width), lambda i: (0, 0)),
        ],
        out_specs=[full, half, pl.BlockSpec((T + 8, width), lambda i: (0, 0))],
        compiler_params=PARAMS,
    )(*parts, grad, weight, offset)


def on_device(features, weight, offset, tile_values, tile_rows, tile_cols, live_tiles, grad_hidden):
    tiles = tile_values.reshape(tile_values.shape[2:])
    nodes_here = features.shape[0]
    scaling = 1.0 / math.sqrt(nodes_here * lax.axis_size("row") * lax.axis_size("col"))
    at_row, at_col = lax.axis_index("row"), lax.axis_index("col")
    live = live_tiles.reshape(1)
    payload, meta, tables = prepare(
        at_row.reshape(1), at_col.reshape(1), live, tile_rows, tile_cols, features
    )

    pieces = ring_gather(payload, along_inner)
    *sends, lists, counts = pack(pieces, ring_gather(meta, along_outer)[1:])
    named = ring_swap([None] + sends, along_outer)[1:]
    flags = [sends[0]] + named
    full = functools.reduce(jnp.maximum, [f[CAP * T + 2, 0] for f in flags]) > 0.5

    def forward_all(pieces, named):
        whole = jnp.concatenate([p[:nodes_here] for p in pieces])
        whole = ring_gather(whole, along_outer)
        spans = (4 * nodes_here,) * 4
        return products(live, tables, 2, 0, tiles, whole, spans, (64, 64), (1,))

    def forward_named(pieces, named):
        spans = (nodes_here,) * 4 + (CAP * T,) * 3
        return products(live, tables, 1, 0, tiles, pieces + named, spans, (64, 64), (1,))

    send, keep = lax.cond(full, forward_all, forward_named, pieces, named)

    both = keep.astype(F32) + other_core(send).astype(F32)
    both = both.reshape(4, nodes_here, T)
    mixed_parts = ring_swap([both[d].astype(BF16) for d in range(4)], along_y)
    hidden, projected, sums = dense(mixed_parts, grad_hidden, weight, offset.reshape(1, -1))

    own = ring_gather(projected, along_y)
    gathered = [other_core(piece) for piece in own] + own

    sums = sums + other_core(sums)
    for along in (along_outer, along_y):
        sums = total_of(ring_gather(sums, along))
    rounded = jnp.concatenate([sums[:, :T], sums[:, T:]]).astype(BF16)

    spans, outs = (nodes_here,) * 8, (64,) + (CAP,) * 3
    here, *parts = products(live, tables, 0, 1, tiles, gathered, spans, outs, (0,))
    parts = ring_swap([None] + parts, along_outer)[1:]

    def backward_all(here, rounded, parts, gathered):
        outs = products(live, tables, 0, 2, tiles, gathered, spans, (64,) * 4, (0,))
        mine = total_of(ring_swap(outs, along_outer)).reshape(4, nodes_here, T)
        far = [jnp.concatenate([mine[d].astype(BF16), rounded]) for d in (1, 2, 3)]
        return [mine[0]] + far

    def backward_named(here, rounded, parts, gathered):
        return list(combine(lists, counts, here, rounded, parts))

    outs = lax.cond(full, backward_all, backward_named, here, rounded, parts, gathered)
    outs = ring_swap(outs, along_inner)
    grad_features, grad_weight, grad_offset = finish(outs, sums, scaling)
    return (hidden, grad_features, grad_weight, grad_offset.reshape(-1))


def solution(mesh):
    in_specs = (
        P(("col", "row"), None),
        P(),
        P(),
        P("row", "col", None, None, None),
        P("row", "col", None),
        P("row", "col", None),
        P("row", "col"),
        P(("row", "col"), None),
    )
    out_specs = (P(("row", "col"), None), P(("col", "row"), None), P(), P())
    return jax.shard_map(
        on_device, mesh=mesh, in_specs=in_specs, out_specs=out_specs, check_vma=False
    )
```

```python
import functools
import itertools
import math

import jax
import jax.numpy as jnp
from jax import lax
from jax.experimental import pallas as pl
from jax.experimental.pallas import tpu as pltpu
from jax.sharding import PartitionSpec as P

T = 128
F32, BF16, I32 = jnp.float32, jnp.bfloat16, jnp.int32
VMEM_BYTES = 56 * 1024 * 1024
GROUP = 4
META = 16
CAP = 26
LANES = 32
SMEM = pl.BlockSpec(memory_space=pltpu.SMEM)
VMEM = pl.BlockSpec(memory_space=pltpu.VMEM)
ANY = pl.BlockSpec(memory_space=pl.ANY)
PARAMS = pltpu.CompilerParams(vmem_limit_bytes=VMEM_BYTES)


def along_xz(value, to, x_core):
    pairs = []
    for x, z, y, core in itertools.product(range(4), range(4), range(4), range(2)):
        far = (to(x) % 4, z) if core == x_core else (x, to(z) % 4)
        pairs.append(((x * 4 + z) * 8 + y * 2 + core, (far[0] * 4 + far[1]) * 8 + y * 2 + core))
    return lax.ppermute(value, ("row", "col"), pairs)


def along_inner(value, to):
    return along_xz(value, to, 0)


def along_outer(value, to):
    return along_xz(value, to, 1)


def along_y(value, to):
    pairs = [(y * 2 + k, to(y) % 4 * 2 + k) for y in range(4) for k in range(2)]
    return lax.ppermute(value, "col", pairs)


def other_core(value):
    pairs = [(y * 2 + k, y * 2 + 1 - k) for y in range(4) for k in range(2)]
    return lax.ppermute(value, "col", pairs)


def ahead(step):
    return lambda at: at + step


def ring_gather(value, along):
    return [value, along(value, ahead(-1)), along(value, ahead(2)), along(value, ahead(1))]


def ring_swap(pieces, along):
    return [
        pieces[0],
        along(pieces[3], ahead(-1)),
        along(pieces[2], ahead(2)),
        along(pieces[1], ahead(1)),
    ]


def total_of(pieces):
    return sum(piece.astype(F32) for piece in pieces)


def block(place):
    return pl.ds(pl.multiple_of(place * T, T), T)


def prepare_kernel(
    at_row, at_col, live_ref, rows_ref, cols_ref, features, payload, meta, tables, sem
):
    nodes = features.shape[0]
    copy = pltpu.make_async_copy(features, payload.at[pl.ds(0, nodes)], sem)
    copy.start()
    live = live_ref[0]
    x, z = at_row[0] >> 2, at_row[0] & 3
    y, core = at_col[0] >> 1, at_col[0] & 1
    rows, cols = rows_ref[...], cols_ref[...]
    slots = cols.shape[1]

    same_core = jnp.where(((rows >> 4) & 1) == core, 64, 0)
    row_place = same_core + ((rows >> 3) & 1) * 32 + (((rows >> 5) - y) & 3) * 8 + (rows & 7)
    dx, dz = ((cols >> 6) - x) & 3, ((cols >> 4) - z) & 3
    outer, inner = jnp.where(core == 0, dz, dx), jnp.where(core == 0, dx, dz)
    code = inner * 16 + (cols & 15)
    dense_place = outer * 64 + code

    t = lax.broadcasted_iota(I32, (slots, slots), 0)
    s = lax.broadcasted_iota(I32, (slots, slots), 1)
    lane = lax.broadcasted_iota(I32, (slots, T), 1).astype(F32)

    def column(row):
        return jnp.sum(jnp.where(t == s, row, 0.0), axis=1, keepdims=True)

    def count(mask, value=1.0):
        return jnp.sum(jnp.where(mask, value, 0.0), axis=0, keepdims=True)

    valid = lax.broadcasted_iota(I32, (1, slots), 1) < live
    cols_f, outer_f = cols.astype(F32), outer.astype(F32)
    same = column(cols_f) == cols_f
    first = valid & (count(same & (t < s)) == 0.0)
    first_c = column(jnp.where(first, 1.0, 0.0)) > 0.0
    outer_c = column(outer_f)
    rank = count((t < s) & first_c & (outer_c == outer_f))
    over = jnp.where(first & (outer != 0) & (rank >= CAP), 1.0, 0.0)
    over = jnp.max(over, axis=1, keepdims=True)
    far = (64 + (outer - 1) * CAP).astype(F32) + jnp.minimum(rank, CAP - 1.0)
    place = jnp.where(outer == 0, code.astype(F32), far)
    place = count(same & first_c, column(place))
    place = jnp.where(valid, place, 0.0).astype(I32)
    pad = jnp.zeros((5, slots), I32)
    tables[...] = jnp.concatenate([row_place, place, dense_place, pad], axis=0)

    key = column(jnp.where(first & (rank < CAP), outer_f * LANES + rank, -1.0))
    wanted = count(key == lane, column(code.astype(F32)))
    amounts = jnp.minimum(count((outer_c == lane) & first_c), 1.0 * CAP)
    line = lax.broadcasted_iota(I32, (META, T), 0)
    lines = [wanted, amounts, jnp.broadcast_to(over, (1, T)), jnp.zeros((META - 3, T), F32)]
    meta[...] = jnp.concatenate(lines, axis=0).astype(BF16)
    payload[pl.ds(nodes, META)] = meta[...]
    copy.wait()


def prepare(at_row, at_col, live, rows, cols, features):
    slots = cols.shape[-1]
    return pl.pallas_call(
        prepare_kernel,
        out_shape=[
            jax.ShapeDtypeStruct((features.shape[0] + META, T), BF16),
            jax.ShapeDtypeStruct((META, T), BF16),
            jax.ShapeDtypeStruct((8, slots), I32),
        ],
        in_specs=[SMEM] * 3 + [VMEM] * 2 + [ANY],
        out_specs=[VMEM] * 3,
        scratch_shapes=[pltpu.SemaphoreType.DMA],
        compiler_params=PARAMS,
    )(at_row, at_col, live, rows.reshape(1, slots), cols.reshape(1, slots), features)


def products_kernel(live, tables, tiles_ref, *refs, spans, outs, contract, in_row, out_row):
    n = len(spans)
    sources, out_refs, (tiles, held, total, sems) = refs[:n], refs[n:-4], refs[-4:]
    if len(out_refs) > len(outs):
        out_refs[-1][...] = out_refs[0][...]
        out_refs = out_refs[1:-1]
    copies = [pltpu.make_async_copy(tiles_ref, tiles, sems.at[n])]
    start = 0
    for k, (ref, rows) in enumerate(zip(sources, spans)):
        copies.append(
            pltpu.make_async_copy(
                ref.at[pl.ds(0, rows)], held.at[pl.ds(start, rows)], sems.at[k]
            )
        )
        start += rows
    for copy in copies:
        copy.start()

    zeros = jnp.zeros((4, T, T), F32)

    def clear(k, carry):
        total[pl.ds(k * 4, 4)] = zeros
        return carry

    lax.fori_loop(0, total.shape[0] // 4, clear, 0)
    for copy in copies:
        copy.wait()

    def group(number, carry):
        products = []
        for k in range(GROUP):
            slot = number * GROUP + k
            product = lax.dot_general(
                tiles[slot],
                held[block(tables[in_row, slot])],
                ((contract, (0,)), ((), ())),
                preferred_element_type=F32,
            )
            products.append(jnp.where(slot < live[0], product, 0.0))
        for k, product in enumerate(products):
            total[tables[out_row, number * GROUP + k]] += product
        return carry

    lax.fori_loop(0, (live[0] + GROUP - 1) // GROUP, group, 0)
    start = 0
    for ref, blocks in zip(out_refs, outs):

        def out(k, carry, ref=ref, start=start):
            ref[block(k)] = total[start + k].astype(BF16)
            return carry

        lax.fori_loop(0, blocks, out, 0)
        start += blocks


def products(live, tables, in_row, out_row, tiles, sources, spans, outs, contract, passed=()):
    kernel = functools.partial(
        products_kernel,
        spans=spans,
        outs=outs,
        contract=contract,
        in_row=in_row,
        out_row=out_row,
    )
    return pl.pallas_call(
        kernel,
        out_shape=[jax.ShapeDtypeStruct((n * T, T), BF16) for n in outs]
        + [jax.ShapeDtypeStruct(p.shape, p.dtype) for p in passed],
        in_specs=[SMEM] * 2 + [ANY] * (1 + len(sources)) + [VMEM] * len(passed),
        out_specs=[VMEM] * (len(outs) + len(passed)),
        scratch_shapes=[
            pltpu.VMEM(tiles.shape, BF16),
            pltpu.VMEM((sum(spans), T), BF16),
            pltpu.VMEM((sum(outs), T, T), F32),
            pltpu.SemaphoreType.DMA((len(spans) + 1,)),
        ],
        compiler_params=PARAMS,
    )(live, tables, tiles, *sources, *passed)


def pack_kernel(*refs):
    pieces, metas, sends, (lists, counts), (held, words, table, sems) = (
        refs[:4],
        refs[4:7],
        refs[7:10],
        refs[10:12],
        refs[12:],
    )
    nodes = held.shape[1] - META
    copies = [pltpu.make_async_copy(p, held.at[k], sems.at[k]) for k, p in enumerate(pieces)]
    for copy in copies:
        copy.start()
    for n in range(3):
        words[pl.ds(n * 8, 8)] = metas[n][...].astype(F32)[:8].astype(I32)
    fetch = pltpu.make_async_copy(words, table, sems.at[4])
    fetch.start()
    fetch.wait()
    for copy in copies:
        copy.wait()
    said = [held[k, pl.ds(nodes, META)].astype(F32) for k in range(4)]
    said = functools.reduce(jnp.maximum, said).astype(BF16)
    for n in range(3):
        sends[n][pl.ds(CAP * T, META)] = said
        group = 3 - n
        amount = table[n * 8 + 1, group]
        counts[n] = amount

        def step(k, carry, n=n, group=group):
            code = table[n * 8, group * LANES + k]
            lists[n * CAP + k] = code
            sends[n][block(k)] = held[code >> 4, block(code & 15)]
            return carry

        lax.fori_loop(0, amount, step, 0)


def pack(pieces, metas):
    return pl.pallas_call(
        pack_kernel,
        out_shape=[jax.ShapeDtypeStruct((CAP * T + META, T), BF16)] * 3
        + [jax.ShapeDtypeStruct((3 * CAP,), I32), jax.ShapeDtypeStruct((3,), I32)],
        in_specs=[ANY] * 4 + [VMEM] * 3,
        out_specs=[VMEM] * 3 + [SMEM] * 2,
        scratch_shapes=[
            pltpu.VMEM((4,) + pieces[0].shape, BF16),
            pltpu.VMEM((24, T), I32),
            pltpu.SMEM((24, T), I32),
            pltpu.SemaphoreType.DMA((5,)),
        ],
        compiler_params=PARAMS,
    )(*pieces, *metas)


def flag_kernel(*refs):
    sources, out, held, sems = refs[:4], refs[4], refs[5], refs[6]
    copies = [
        pltpu.make_async_copy(ref.at[pl.ds(CAP * T, META)], held.at[k], sems.at[k])
        for k, ref in enumerate(sources)
    ]
    for copy in copies:
        copy.start()
    for copy in copies:
        copy.wait()
    said = functools.reduce(jnp.maximum, [held[k].astype(F32) for k in range(4)])
    out[0] = jnp.max(said[2:3]).astype(I32)


def overflow(sources):
    return pl.pallas_call(
        flag_kernel,
        out_shape=jax.ShapeDtypeStruct((1,), I32),
        in_specs=[ANY] * 4,
        out_specs=SMEM,
        scratch_shapes=[pltpu.VMEM((4, META, T), BF16), pltpu.SemaphoreType.DMA((4,))],
        compiler_params=PARAMS,
    )(*sources)


def combine_kernel(lists, counts, own, sums, *refs):
    parts, outs, (total,) = refs[:3], refs[3:7], refs[7:]

    def widen(k, carry):
        total[k] = own[block(k)].astype(F32)
        return carry

    lax.fori_loop(0, 64, widen, 0)
    for n, part in enumerate(parts):

        def add(k, carry, n=n, part=part):
            total[lists[n * CAP + k]] += part[block(k)].astype(F32)
            return carry

        lax.fori_loop(0, counts[n], add, 0)
    for n, ref in enumerate(outs):

        def out(k, carry, n=n, ref=ref):
            ref[block(k)] = total[n * 16 + k].astype(ref.dtype)
            return carry

        lax.fori_loop(0, 16, out, 0)
        if n:
            ref[pl.ds(16 * T, sums.shape[0])] = sums[...]


def combine(lists, counts, own, sums, parts):
    rows = 16 * T
    return pl.pallas_call(
        combine_kernel,
        out_shape=[jax.ShapeDtypeStruct((rows, T), F32)]
        + [jax.ShapeDtypeStruct((rows + sums.shape[0], T), BF16)] * 3,
        in_specs=[SMEM] * 2 + [VMEM] * 5,
        out_specs=[VMEM] * 4,
        scratch_shapes=[pltpu.VMEM((64, T, T), F32)],
        compiler_params=PARAMS,
    )(lists, counts, own, sums, *parts)


def finish_kernel(*refs, scaling):
    pieces, sums, (nodes, weight, offset) = refs[:4], refs[4], refs[5:]
    rows = nodes.shape[0]
    nodes[...] = total_of([ref[pl.ds(0, rows)] for ref in pieces])
    lines = sums.shape[0]
    for k in range(2):
        part = pl.ds(k * T, T)
        total = sums[:, part]
        for ref in pieces[1:]:
            total = total + ref[pl.ds(rows + k * lines, lines)].astype(F32)
        total = total * scaling
        weight[:, part] = total[:T]
        offset[:, part] = jnp.sum(total[T:], axis=0, keepdims=True)


def finish(pieces, sums, scaling):
    width = sums.shape[-1]
    return pl.pallas_call(
        functools.partial(finish_kernel, scaling=scaling),
        out_shape=[
            jax.ShapeDtypeStruct(pieces[0].shape, F32),
            jax.ShapeDtypeStruct((T, width), F32),
            jax.ShapeDtypeStruct((1, width), F32),
        ],
        in_specs=[VMEM] * 5,
        out_specs=[VMEM] * 3,
        compiler_params=PARAMS,
    )(*pieces, sums)


def dense_kernel(*refs):
    parts, (grad, weight, offset), (hidden, projected, sums) = refs[:5], refs[5:8], refs[-3:]

    @pl.when(pl.program_id(0) == 0)
    def _():
        sums[...] = refs[9][...] if len(refs) > 11 else jnp.zeros_like(sums)

    mixed = total_of([ref[...] for ref in parts])
    high = mixed.astype(BF16)
    low = (mixed - high.astype(F32)).astype(BF16)
    w = weight[...]
    pre = jnp.dot(high, w, preferred_element_type=F32)
    pre = pre + jnp.dot(low, w, preferred_element_type=F32) + offset[...]
    s = jax.nn.sigmoid(pre)
    hidden[...] = (pre * s).astype(BF16)
    slope = (grad[...].astype(F32) * s * (1.0 + pre * (1.0 - s))).astype(BF16)
    projected[...] = lax.dot_general(
        slope, w, (((1,), (1,)), ((), ())), preferred_element_type=F32
    ).astype(BF16)
    over_rows = (((0,), (0,)), ((), ()))
    sums[:T] += lax.dot_general(
        high, slope, over_rows, preferred_element_type=F32
    ) + lax.dot_general(low, slope, over_rows, preferred_element_type=F32)
    sums[T:] += jnp.sum(slope.astype(F32).reshape(-1, 8, slope.shape[1]), axis=0)


def dense(parts, grad, weight, offset, part, before):
    width, rows = weight.shape[1], grad.shape[0]
    step = 512
    steps = rows // 2 // step
    shift = part * steps
    half = pl.BlockSpec((step, T), lambda i: (i, 0))
    full = pl.BlockSpec((step, width), lambda i: (i + shift, 0))
    whole = pl.BlockSpec((T + 8, width), lambda i: (0, 0))
    return pl.pallas_call(
        dense_kernel,
        grid=(steps,),
        out_shape=[
            jax.ShapeDtypeStruct((rows, width), BF16),
            jax.ShapeDtypeStruct((rows // 2, T), BF16),
            jax.ShapeDtypeStruct((T + 8, width), F32),
        ],
        in_specs=[half] * 5
        + [
            full,
            pl.BlockSpec((T, width), lambda i: (0, 0)),
            pl.BlockSpec((1, width), lambda i: (0, 0)),
        ]
        + ([ANY, whole] + [ANY] * (len(before) - 2) if before else []),
        out_specs=[full, half, whole],
        input_output_aliases={8: 0} if before else {},
        compiler_params=PARAMS,
    )(*parts, grad, weight, offset, *before)


def on_device(features, weight, offset, tile_values, tile_rows, tile_cols, live_tiles, grad_hidden):
    tiles = tile_values.reshape(tile_values.shape[2:])
    nodes_here = features.shape[0]
    scaling = 1.0 / math.sqrt(nodes_here * lax.axis_size("row") * lax.axis_size("col"))
    at_row, at_col = lax.axis_index("row"), lax.axis_index("col")
    live = live_tiles.reshape(1)
    payload, meta, tables = prepare(
        at_row.reshape(1), at_col.reshape(1), live, tile_rows, tile_cols, features
    )

    pieces = ring_gather(payload, along_inner)
    *sends, lists, counts = pack(pieces, ring_gather(meta, along_outer)[1:])
    named = ring_swap([None] + sends, along_outer)[1:]
    flags = [sends[0]] + named
    full = overflow(flags)[0] > 0

    def forward_all(pieces, named):
        whole = jnp.concatenate([p[:nodes_here] for p in pieces])
        whole = ring_gather(whole, along_outer)
        spans = (4 * nodes_here,) * 4
        return products(live, tables, 2, 0, tiles, whole, spans, (32,) * 4, (1,))

    def forward_named(pieces, named):
        spans = (nodes_here,) * 4 + (CAP * T,) * 3
        return products(live, tables, 1, 0, tiles, pieces + named, spans, (32,) * 4, (1,))

    outs = lax.cond(full, forward_all, forward_named, pieces, named)

    part_rows = nodes_here // 2
    halves = []
    for send, keep in zip(outs[:2], outs[2:]):
        got = other_core(send)
        far = []
        for d in (1, 2, 3):
            at = slice(d * part_rows, (d + 1) * part_rows)
            far.append((keep[at].astype(F32) + got[at].astype(F32)).astype(BF16))
        halves.append([keep, got] + ring_swap([None] + far, along_y)[1:])
    before, own, others = (), [], []
    for part, parts in enumerate(halves):
        hidden, projected, sums = dense(
            parts, grad_hidden, weight, offset.reshape(1, -1), part, before
        )
        here = ring_gather(projected, along_y)
        before = (hidden, sums, *here[1:])
        own += here
        others += [other_core(piece) for piece in here]

    sums = total_of(ring_gather(sums + other_core(sums), along_outer))

    gathered, spans, outs = others + own, (part_rows,) * 16, (64,) + (CAP,) * 3
    here, *parts, sums = products(
        live, tables, 0, 1, tiles, gathered, spans, outs, (0,), (sums,)
    )
    sums = total_of(ring_gather(sums, along_y))
    rounded = jnp.concatenate([sums[:, :T], sums[:, T:]]).astype(BF16)
    parts = ring_swap([None] + parts, along_outer)[1:]

    def backward_all(here, rounded, parts, gathered):
        outs = products(live, tables, 0, 2, tiles, gathered, spans, (64,) * 4, (0,))
        mine = total_of(ring_swap(outs, along_outer)).reshape(4, nodes_here, T)
        far = [jnp.concatenate([mine[d].astype(BF16), rounded]) for d in (1, 2, 3)]
        return [mine[0]] + far

    def backward_named(here, rounded, parts, gathered):
        return list(combine(lists, counts, here, rounded, parts))

    outs = lax.cond(full, backward_all, backward_named, here, rounded, parts, gathered)
    outs = ring_swap(outs, along_inner)
    grad_features, grad_weight, grad_offset = finish(outs, sums, scaling)
    return (hidden, grad_features, grad_weight, grad_offset.reshape(-1))


def solution(mesh):
    in_specs = (
        P(("col", "row"), None),
        P(),
        P(),
        P("row", "col", None, None, None),
        P("row", "col", None),
        P("row", "col", None),
        P("row", "col"),
        P(("row", "col"), None),
    )
    out_specs = (P(("row", "col"), None), P(("col", "row"), None), P(), P())
    return jax.shard_map(
        on_device, mesh=mesh, in_specs=in_specs, out_specs=out_specs, check_vma=False
    )
```

```python
import functools
import itertools
import math

import jax
import jax.numpy as jnp
from jax import lax
from jax.experimental import pallas as pl
from jax.experimental.pallas import tpu as pltpu
from jax.sharding import PartitionSpec as P

T = 128
F32, BF16, I32 = jnp.float32, jnp.bfloat16, jnp.int32
VMEM_BYTES = 56 * 1024 * 1024
GROUP = 4
META = 16
CAP = 26
LANES = 32
SMEM = pl.BlockSpec(memory_space=pltpu.SMEM)
VMEM = pl.BlockSpec(memory_space=pltpu.VMEM)
ANY = pl.BlockSpec(memory_space=pl.ANY)
PARAMS = pltpu.CompilerParams(vmem_limit_bytes=VMEM_BYTES)


def along_xz(value, to, x_core):
    pairs = []
    for x, z, y, core in itertools.product(range(4), range(4), range(4), range(2)):
        far = (to(x) % 4, z) if core == x_core else (x, to(z) % 4)
        pairs.append(((x * 4 + z) * 8 + y * 2 + core, (far[0] * 4 + far[1]) * 8 + y * 2 + core))
    return lax.ppermute(value, ("row", "col"), pairs)


def along_inner(value, to):
    return along_xz(value, to, 0)


def along_outer(value, to):
    return along_xz(value, to, 1)


def along_y(value, to):
    pairs = [(y * 2 + k, to(y) % 4 * 2 + k) for y in range(4) for k in range(2)]
    return lax.ppermute(value, "col", pairs)


def other_core(value):
    pairs = [(y * 2 + k, y * 2 + 1 - k) for y in range(4) for k in range(2)]
    return lax.ppermute(value, "col", pairs)


def ahead(step):
    return lambda at: at + step


def ring_gather(value, along):
    return [value, along(value, ahead(-1)), along(value, ahead(2)), along(value, ahead(1))]


def ring_swap(pieces, along):
    return [
        pieces[0],
        along(pieces[3], ahead(-1)),
        along(pieces[2], ahead(2)),
        along(pieces[1], ahead(1)),
    ]


def total_of(pieces):
    return sum(piece.astype(F32) for piece in pieces)


def block(place):
    return pl.ds(pl.multiple_of(place * T, T), T)


def prepare_kernel(at_row, at_col, live_ref, rows_ref, cols_ref, meta, tables):
    live = live_ref[0]
    x, z = at_row[0] >> 2, at_row[0] & 3
    y, core = at_col[0] >> 1, at_col[0] & 1
    rows, cols = rows_ref[...], cols_ref[...]
    slots = cols.shape[1]

    same_core = jnp.where(((rows >> 4) & 1) == core, 64, 0)
    row_place = same_core + ((rows >> 3) & 1) * 32 + (((rows >> 5) - y) & 3) * 8 + (rows & 7)
    dx, dz = ((cols >> 6) - x) & 3, ((cols >> 4) - z) & 3
    outer, inner = jnp.where(core == 0, dz, dx), jnp.where(core == 0, dx, dz)
    code = inner * 16 + (cols & 15)
    dense_place = outer * 64 + code

    t = lax.broadcasted_iota(I32, (slots, slots), 0)
    s = lax.broadcasted_iota(I32, (slots, slots), 1)
    lane = lax.broadcasted_iota(I32, (slots, T), 1).astype(F32)

    def column(row):
        return jnp.sum(jnp.where(t == s, row, 0.0), axis=1, keepdims=True)

    def count(mask, value=1.0):
        return jnp.sum(jnp.where(mask, value, 0.0), axis=0, keepdims=True)

    valid = lax.broadcasted_iota(I32, (1, slots), 1) < live
    cols_f, outer_f = cols.astype(F32), outer.astype(F32)
    same = column(cols_f) == cols_f
    first = valid & (count(same & (t < s)) == 0.0)
    first_c = column(jnp.where(first, 1.0, 0.0)) > 0.0
    outer_c = column(outer_f)
    rank = count((t < s) & first_c & (outer_c == outer_f))
    over = jnp.where(first & (outer != 0) & (rank >= CAP), 1.0, 0.0)
    over = jnp.max(over, axis=1, keepdims=True)
    far = (64 + (outer - 1) * CAP).astype(F32) + jnp.minimum(rank, CAP - 1.0)
    place = jnp.where(outer == 0, code.astype(F32), far)
    place = count(same & first_c, column(place))
    place = jnp.where(valid, place, 0.0).astype(I32)
    pad = jnp.zeros((5, slots), I32)
    tables[...] = jnp.concatenate([row_place, place, dense_place, pad], axis=0)

    key = column(jnp.where(first & (rank < CAP), outer_f * LANES + rank, -1.0))
    wanted = count(key == lane, column(code.astype(F32)))
    amounts = jnp.minimum(count((outer_c == lane) & first_c), 1.0 * CAP)
    line = lax.broadcasted_iota(I32, (META, T), 0)
    lines = [wanted, amounts, jnp.broadcast_to(over, (1, T)), jnp.zeros((META - 3, T), F32)]
    meta[...] = jnp.concatenate(lines, axis=0).astype(BF16)


def prepare(at_row, at_col, live, rows, cols):
    slots = cols.shape[-1]
    return pl.pallas_call(
        prepare_kernel,
        out_shape=[
            jax.ShapeDtypeStruct((META, T), BF16),
            jax.ShapeDtypeStruct((8, slots), I32),
        ],
        in_specs=[SMEM] * 3 + [VMEM] * 2,
        out_specs=[VMEM] * 2,
        compiler_params=PARAMS,
    )(at_row, at_col, live, rows.reshape(1, slots), cols.reshape(1, slots))


def products_kernel(live, tables, tiles_ref, *refs, spans, outs, contract, in_row, out_row):
    n = len(spans)
    sources, out_refs, (tiles, held, total, sems) = refs[:n], refs[n:-4], refs[-4:]
    if len(out_refs) > len(outs):
        out_refs[-1][...] = out_refs[0][...]
        out_refs = out_refs[1:-1]
    copies = [pltpu.make_async_copy(tiles_ref, tiles, sems.at[n])]
    start = 0
    for k, (ref, rows) in enumerate(zip(sources, spans)):
        copies.append(
            pltpu.make_async_copy(
                ref.at[pl.ds(0, rows)], held.at[pl.ds(start, rows)], sems.at[k]
            )
        )
        start += rows
    for copy in copies:
        copy.start()

    zeros = jnp.zeros((4, T, T), F32)

    def clear(k, carry):
        total[pl.ds(k * 4, 4)] = zeros
        return carry

    lax.fori_loop(0, total.shape[0] // 4, clear, 0)
    for copy in copies:
        copy.wait()

    def group(number, carry):
        products = []
        for k in range(GROUP):
            slot = number * GROUP + k
            product = lax.dot_general(
                tiles[slot],
                held[block(tables[in_row, slot])],
                ((contract, (0,)), ((), ())),
                preferred_element_type=F32,
            )
            products.append(jnp.where(slot < live[0], product, 0.0))
        for k, product in enumerate(products):
            total[tables[out_row, number * GROUP + k]] += product
        return carry

    lax.fori_loop(0, (live[0] + GROUP - 1) // GROUP, group, 0)
    start = 0
    for ref, blocks in zip(out_refs, outs):

        def out(k, carry, ref=ref, start=start):
            for at in range(2):
                ref[block(k * 2 + at)] = total[start + k * 2 + at].astype(BF16)
            return carry

        lax.fori_loop(0, blocks // 2, out, 0)
        start += blocks


def products(live, tables, in_row, out_row, tiles, sources, spans, outs, contract, passed=()):
    kernel = functools.partial(
        products_kernel,
        spans=spans,
        outs=outs,
        contract=contract,
        in_row=in_row,
        out_row=out_row,
    )
    return pl.pallas_call(
        kernel,
        out_shape=[jax.ShapeDtypeStruct((n * T, T), BF16) for n in outs]
        + [jax.ShapeDtypeStruct(p.shape, p.dtype) for p in passed],
        in_specs=[SMEM] * 2 + [ANY] * (1 + len(sources)) + [VMEM] * len(passed),
        out_specs=[VMEM] * (len(outs) + len(passed)),
        scratch_shapes=[
            pltpu.VMEM(tiles.shape, BF16),
            pltpu.VMEM((sum(spans), T), BF16),
            pltpu.VMEM((sum(outs), T, T), F32),
            pltpu.SemaphoreType.DMA((len(spans) + 1,)),
        ],
        compiler_params=PARAMS,
    )(live, tables, tiles, *sources, *passed)


def pack_kernel(*refs):
    pieces, metas, sends, (said, lists, counts), (held, words, table, sems) = (
        refs[:4],
        refs[4:8],
        refs[8:11],
        refs[11:14],
        refs[14:],
    )
    copies = [pltpu.make_async_copy(p, held.at[k], sems.at[k]) for k, p in enumerate(pieces)]
    for copy in copies:
        copy.start()
    for n in range(3):
        words[pl.ds(n * 8, 8)] = metas[n + 1][...].astype(F32)[:8].astype(I32)
    fetch = pltpu.make_async_copy(words, table, sems.at[4])
    fetch.start()
    over = functools.reduce(jnp.maximum, [ref[...].astype(F32)[2:3] for ref in metas])
    said[...] = jnp.broadcast_to(over, (8, T))
    fetch.wait()
    for copy in copies:
        copy.wait()
    for n in range(3):
        group = 3 - n
        amount = table[n * 8 + 1, group]
        counts[n] = amount

        def step(k, carry, n=n, group=group):
            code = table[n * 8, group * LANES + k]
            lists[n * CAP + k] = code
            sends[n][block(k)] = held[code >> 4, block(code & 15)]
            return carry

        lax.fori_loop(0, amount, step, 0)


def pack(pieces, metas):
    return pl.pallas_call(
        pack_kernel,
        out_shape=[jax.ShapeDtypeStruct((CAP * T, T), BF16)] * 3
        + [jax.ShapeDtypeStruct((8, T), F32)]
        + [jax.ShapeDtypeStruct((3 * CAP,), I32), jax.ShapeDtypeStruct((3,), I32)],
        in_specs=[ANY] * 4 + [VMEM] * 4,
        out_specs=[VMEM] * 4 + [SMEM] * 2,
        scratch_shapes=[
            pltpu.VMEM((4,) + pieces[0].shape, BF16),
            pltpu.VMEM((24, T), I32),
            pltpu.SMEM((24, T), I32),
            pltpu.SemaphoreType.DMA((5,)),
        ],
        compiler_params=PARAMS,
    )(*pieces, *metas)


def combine_kernel(lists, counts, own_ref, sums, *refs):
    part_refs, outs, (own, parts, total, sems) = refs[:3], refs[3:7], refs[7:]
    copies = [pltpu.make_async_copy(own_ref, own, sems.at[3])]
    for n, ref in enumerate(part_refs):
        copies.append(pltpu.make_async_copy(ref, parts.at[n], sems.at[n]))
    for copy in copies:
        copy.start()
    for ref in outs[1:]:
        ref[pl.ds(16 * T, sums.shape[0])] = sums[...]
    copies[0].wait()

    def widen(k, carry):
        for at in range(4):
            total[k * 4 + at] = own[block(k * 4 + at)].astype(F32)
        return carry

    lax.fori_loop(0, 16, widen, 0)
    for copy in copies[1:]:
        copy.wait()
    for n in range(3):

        def add(k, carry, n=n):
            total[lists[n * CAP + k]] += parts[n, block(k)].astype(F32)
            return carry

        lax.fori_loop(0, counts[n], add, 0)
    for n, ref in enumerate(outs):

        def out(k, carry, n=n, ref=ref):
            for at in range(4):
                ref[block(k * 4 + at)] = total[n * 16 + k * 4 + at].astype(ref.dtype)
            return carry

        lax.fori_loop(0, 4, out, 0)


def combine(lists, counts, own, sums, parts):
    rows = 16 * T
    return pl.pallas_call(
        combine_kernel,
        out_shape=[jax.ShapeDtypeStruct((rows, T), F32)]
        + [jax.ShapeDtypeStruct((rows + sums.shape[0], T), BF16)] * 3,
        in_specs=[SMEM] * 2 + [ANY, VMEM] + [ANY] * 3,
        out_specs=[VMEM] * 4,
        scratch_shapes=[
            pltpu.VMEM(own.shape, BF16),
            pltpu.VMEM((3,) + parts[0].shape, BF16),
            pltpu.VMEM((64, T, T), F32),
            pltpu.SemaphoreType.DMA((4,)),
        ],
        compiler_params=PARAMS,
    )(lists, counts, own, sums, *parts)


def finish_kernel(*refs, scaling):
    pieces, sums, (nodes, weight, offset) = refs[:4], refs[4], refs[5:]
    rows = nodes.shape[0]
    nodes[...] = total_of([ref[pl.ds(0, rows)] for ref in pieces])
    lines = sums.shape[0]
    for k in range(2):
        part = pl.ds(k * T, T)
        total = sums[:, part]
        for ref in pieces[1:]:
            total = total + ref[pl.ds(rows + k * lines, lines)].astype(F32)
        total = total * scaling
        weight[:, part] = total[:T]
        offset[:, part] = jnp.sum(total[T:], axis=0, keepdims=True)


def finish(pieces, sums, scaling):
    width = sums.shape[-1]
    return pl.pallas_call(
        functools.partial(finish_kernel, scaling=scaling),
        out_shape=[
            jax.ShapeDtypeStruct(pieces[0].shape, F32),
            jax.ShapeDtypeStruct((T, width), F32),
            jax.ShapeDtypeStruct((1, width), F32),
        ],
        in_specs=[VMEM] * 5,
        out_specs=[VMEM] * 3,
        compiler_params=PARAMS,
    )(*pieces, sums)


def dense_kernel(*refs):
    parts, (grad, weight, offset), (hidden, projected, sums) = refs[:5], refs[5:8], refs[-3:]

    @pl.when(pl.program_id(0) == 0)
    def _():
        sums[...] = refs[9][...] if len(refs) > 11 else jnp.zeros_like(sums)

    mixed = total_of([ref[...] for ref in parts])
    high = mixed.astype(BF16)
    low = (mixed - high.astype(F32)).astype(BF16)
    w = weight[...]
    pre = jnp.dot(high, w, preferred_element_type=F32)
    pre = pre + jnp.dot(low, w, preferred_element_type=F32) + offset[...]
    s = jax.nn.sigmoid(pre)
    hidden[...] = (pre * s).astype(BF16)
    slope = (grad[...].astype(F32) * s * (1.0 + pre * (1.0 - s))).astype(BF16)
    projected[...] = lax.dot_general(
        slope, w, (((1,), (1,)), ((), ())), preferred_element_type=F32
    ).astype(BF16)
    over_rows = (((0,), (0,)), ((), ()))
    sums[:T] += lax.dot_general(
        high, slope, over_rows, preferred_element_type=F32
    ) + lax.dot_general(low, slope, over_rows, preferred_element_type=F32)
    sums[T:] += jnp.sum(slope.astype(F32).reshape(-1, 8, slope.shape[1]), axis=0)


def dense(parts, grad, weight, offset, part, before):
    width, rows = weight.shape[1], grad.shape[0]
    step = 512
    steps = rows // 2 // step
    shift = part * steps
    half = pl.BlockSpec((step, T), lambda i: (i, 0))
    full = pl.BlockSpec((step, width), lambda i: (i + shift, 0))
    whole = pl.BlockSpec((T + 8, width), lambda i: (0, 0))
    return pl.pallas_call(
        dense_kernel,
        grid=(steps,),
        out_shape=[
            jax.ShapeDtypeStruct((rows, width), BF16),
            jax.ShapeDtypeStruct((rows // 2, T), BF16),
            jax.ShapeDtypeStruct((T + 8, width), F32),
        ],
        in_specs=[half] * 5
        + [
            full,
            pl.BlockSpec((T, width), lambda i: (0, 0)),
            pl.BlockSpec((1, width), lambda i: (0, 0)),
        ]
        + ([ANY, whole] + [ANY] * (len(before) - 2) if before else []),
        out_specs=[full, half, whole],
        input_output_aliases={8: 0} if before else {},
        compiler_params=PARAMS,
    )(*parts, grad, weight, offset, *before)


def on_device(features, weight, offset, tile_values, tile_rows, tile_cols, live_tiles, grad_hidden):
    tiles = tile_values.reshape(tile_values.shape[2:])
    nodes_here = features.shape[0]
    scaling = 1.0 / math.sqrt(nodes_here * lax.axis_size("row") * lax.axis_size("col"))
    at_row, at_col = lax.axis_index("row"), lax.axis_index("col")
    live = live_tiles.reshape(1)
    meta, tables = prepare(at_row.reshape(1), at_col.reshape(1), live, tile_rows, tile_cols)

    pieces = ring_gather(features, along_inner)
    *sends, said, lists, counts = pack(pieces, ring_gather(meta, along_outer))
    named = ring_swap([None] + sends, along_outer)[1:]
    full = functools.reduce(jnp.maximum, ring_gather(said, along_inner))[0, 0] > 0.5

    def forward_all(pieces, named):
        whole = jnp.concatenate(pieces)
        whole = ring_gather(whole, along_outer)
        spans = (4 * nodes_here,) * 4
        return products(live, tables, 2, 0, tiles, whole, spans, (32,) * 4, (1,))

    def forward_named(pieces, named):
        spans = (nodes_here,) * 4 + (CAP * T,) * 3
        return products(live, tables, 1, 0, tiles, pieces + named, spans, (32,) * 4, (1,))

    outs = lax.cond(full, forward_all, forward_named, pieces, named)

    part_rows = nodes_here // 2
    halves = []
    for send, keep in zip(outs[:2], outs[2:]):
        got = other_core(send)
        far = []
        for d in (1, 2, 3):
            at = slice(d * part_rows, (d + 1) * part_rows)
            far.append((keep[at].astype(F32) + got[at].astype(F32)).astype(BF16))
        halves.append([keep, got] + ring_swap([None] + far, along_y)[1:])
    before, own, others = (), [], []
    for part, parts in enumerate(halves):
        hidden, projected, sums = dense(
            parts, grad_hidden, weight, offset.reshape(1, -1), part, before
        )
        here = ring_gather(projected, along_y)
        own += here
        others += [other_core(piece) for piece in here]
        before = (hidden, sums, others[0])

    sums = total_of(ring_gather(sums + other_core(sums), along_outer))

    gathered, spans, outs = others + own, (part_rows,) * 16, (64,) + (CAP,) * 3
    here, *parts, sums = products(
        live, tables, 0, 1, tiles, gathered, spans, outs, (0,), (sums,)
    )
    sums = total_of(ring_gather(sums, along_y))
    rounded = jnp.concatenate([sums[:, :T], sums[:, T:]]).astype(BF16)
    parts = ring_swap([None] + parts, along_outer)[1:]

    def backward_all(here, rounded, parts, gathered):
        outs = products(live, tables, 0, 2, tiles, gathered, spans, (64,) * 4, (0,))
        mine = total_of(ring_swap(outs, along_outer)).reshape(4, nodes_here, T)
        far = [jnp.concatenate([mine[d].astype(BF16), rounded]) for d in (1, 2, 3)]
        return [mine[0]] + far

    def backward_named(here, rounded, parts, gathered):
        return list(combine(lists, counts, here, rounded, parts))

    outs = lax.cond(full, backward_all, backward_named, here, rounded, parts, gathered)
    outs = ring_swap(outs, along_inner)
    grad_features, grad_weight, grad_offset = finish(outs, sums, scaling)
    return (hidden, grad_features, grad_weight, grad_offset.reshape(-1))


def solution(mesh):
    in_specs = (
        P(("col", "row"), None),
        P(),
        P(),
        P("row", "col", None, None, None),
        P("row", "col", None),
        P("row", "col", None),
        P("row", "col"),
        P(("row", "col"), None),
    )
    out_specs = (P(("row", "col"), None), P(("col", "row"), None), P(), P())
    return jax.shard_map(
        on_device, mesh=mesh, in_specs=in_specs, out_specs=out_specs, check_vma=False
    )
```

```python
import functools
import itertools
import math

import jax
import jax.numpy as jnp
from jax import lax
from jax.experimental import pallas as pl
from jax.experimental.pallas import tpu as pltpu
from jax.sharding import PartitionSpec as P

T = 128
F32, BF16, I32 = jnp.float32, jnp.bfloat16, jnp.int32
VMEM_BYTES = 56 * 1024 * 1024
GROUP = 4
META = 16
CAP = 26
LANES = 32
SMEM = pl.BlockSpec(memory_space=pltpu.SMEM)
VMEM = pl.BlockSpec(memory_space=pltpu.VMEM)
ANY = pl.BlockSpec(memory_space=pl.ANY)
PARAMS = pltpu.CompilerParams(vmem_limit_bytes=VMEM_BYTES)


def along_xz(value, to, x_core):
    pairs = []
    for x, z, y, core in itertools.product(range(4), range(4), range(4), range(2)):
        far = (to(x) % 4, z) if core == x_core else (x, to(z) % 4)
        pairs.append(((x * 4 + z) * 8 + y * 2 + core, (far[0] * 4 + far[1]) * 8 + y * 2 + core))
    return lax.ppermute(value, ("row", "col"), pairs)


def along_inner(value, to):
    return along_xz(value, to, 0)


def along_outer(value, to):
    return along_xz(value, to, 1)


def along_y(value, to):
    pairs = [(y * 2 + k, to(y) % 4 * 2 + k) for y in range(4) for k in range(2)]
    return lax.ppermute(value, "col", pairs)


def other_core(value):
    pairs = [(y * 2 + k, y * 2 + 1 - k) for y in range(4) for k in range(2)]
    return lax.ppermute(value, "col", pairs)


def ahead(step):
    return lambda at: at + step


def ring_gather(value, along):
    after, before, across = [along(value, ahead(step)) for step in (-1, 1, 2)]
    return [value, after, across, before]


def ring_swap(pieces, along):
    after, before = along(pieces[3], ahead(-1)), along(pieces[1], ahead(1))
    return [pieces[0], after, along(pieces[2], ahead(2)), before]


def total_of(pieces):
    return sum(piece.astype(F32) for piece in pieces)


def block(place):
    return pl.ds(pl.multiple_of(place * T, T), T)


def prepare_kernel(at_row, at_col, live_ref, rows_ref, cols_ref, meta, tables):
    live = live_ref[0]
    x, z = at_row[0] >> 2, at_row[0] & 3
    y, core = at_col[0] >> 1, at_col[0] & 1
    rows, cols = rows_ref[...], cols_ref[...]
    slots = cols.shape[1]

    same_core = jnp.where(((rows >> 4) & 1) == core, 64, 0)
    row_place = same_core + ((rows >> 3) & 1) * 32 + (((rows >> 5) - y) & 3) * 8 + (rows & 7)
    dx, dz = ((cols >> 6) - x) & 3, ((cols >> 4) - z) & 3
    outer, inner = jnp.where(core == 0, dz, dx), jnp.where(core == 0, dx, dz)
    code = inner * 16 + (cols & 15)
    dense_place = outer * 64 + code

    t = lax.broadcasted_iota(I32, (slots, slots), 0)
    s = lax.broadcasted_iota(I32, (slots, slots), 1)
    lane = lax.broadcasted_iota(I32, (slots, T), 1).astype(F32)

    def column(row):
        return jnp.sum(jnp.where(t == s, row, 0.0), axis=1, keepdims=True)

    def count(mask, value=1.0):
        return jnp.sum(jnp.where(mask, value, 0.0), axis=0, keepdims=True)

    valid = lax.broadcasted_iota(I32, (1, slots), 1) < live
    cols_f, outer_f = cols.astype(F32), outer.astype(F32)
    same = column(cols_f) == cols_f
    first = valid & (count(same & (t < s)) == 0.0)
    first_c = column(jnp.where(first, 1.0, 0.0)) > 0.0
    outer_c = column(outer_f)
    rank = count((t < s) & first_c & (outer_c == outer_f))
    over = jnp.where(first & (outer != 0) & (rank >= CAP), 1.0, 0.0)
    over = jnp.max(over, axis=1, keepdims=True)
    far = (64 + (outer - 1) * CAP).astype(F32) + jnp.minimum(rank, CAP - 1.0)
    place = jnp.where(outer == 0, code.astype(F32), far)
    place = count(same & first_c, column(place))
    place = jnp.where(valid, place, 0.0).astype(I32)
    second = (rows >> 3) & 1
    source = (1 - second) * 64 + ((row_place & 64) >> 1) + (row_place & 31)
    pad = jnp.zeros((4, slots), I32)
    tables[...] = jnp.concatenate([row_place, place, dense_place, source, pad], axis=0)

    key = column(jnp.where(first & (rank < CAP), outer_f * LANES + rank, -1.0))
    wanted = count(key == lane, column(code.astype(F32)))
    amounts = jnp.minimum(count((outer_c == lane) & first_c), 1.0 * CAP)
    line = lax.broadcasted_iota(I32, (META, T), 0)
    lines = [wanted, amounts, jnp.broadcast_to(over, (1, T)), jnp.zeros((META - 3, T), F32)]
    meta[...] = jnp.concatenate(lines, axis=0).astype(BF16)


def prepare(at_row, at_col, live, rows, cols):
    slots = cols.shape[-1]
    return pl.pallas_call(
        prepare_kernel,
        out_shape=[
            jax.ShapeDtypeStruct((META, T), BF16),
            jax.ShapeDtypeStruct((8, slots), I32),
        ],
        in_specs=[SMEM] * 3 + [VMEM] * 2,
        out_specs=[VMEM] * 2,
        compiler_params=PARAMS,
    )(at_row, at_col, live, rows.reshape(1, slots), cols.reshape(1, slots))


def products_kernel(
    live, tables, tiles_ref, *refs, spans, outs, contract, in_row, out_row, tailed
):
    n = len(spans)
    sources, out_refs, (tiles, held, total, tails, sems) = refs[:n], refs[n:-5], refs[-5:]
    copies = [pltpu.make_async_copy(tiles_ref, tiles, sems.at[n])]
    start = 0
    for k, (ref, rows) in enumerate(zip(sources, spans)):
        copies.append(
            pltpu.make_async_copy(
                ref.at[pl.ds(0, rows)], held.at[pl.ds(start, rows)], sems.at[k]
            )
        )
        start += rows
    for k in range(tailed):
        tail = sources[k].at[pl.ds(spans[k], tails.shape[1])]
        copies.append(pltpu.make_async_copy(tail, tails.at[k], sems.at[n + 1 + k]))
    for copy in copies:
        copy.start()

    zeros = jnp.zeros((4, T, T), F32)

    def clear(k, carry):
        total[pl.ds(k * 4, 4)] = zeros
        return carry

    lax.fori_loop(0, total.shape[0] // 4, clear, 0)
    for copy in copies:
        copy.wait()
    if tailed:
        summed = jnp.sum(tails[...].astype(F32), axis=0)
        lines = summed.shape[0] // 2
        out_refs[-1][:, :T] = summed[:lines]
        out_refs[-1][:, T:] = summed[lines:]

    def group(number, carry):
        products = []
        for k in range(GROUP):
            slot = number * GROUP + k
            product = lax.dot_general(
                tiles[slot],
                held[block(tables[in_row, slot])],
                ((contract, (0,)), ((), ())),
                preferred_element_type=F32,
            )
            products.append(jnp.where(slot < live[0], product, 0.0))
        for k, product in enumerate(products):
            total[tables[out_row, number * GROUP + k]] += product
        return carry

    lax.fori_loop(0, (live[0] + GROUP - 1) // GROUP, group, 0)
    start = 0
    for ref, blocks in zip(out_refs, outs):

        def out(k, carry, ref=ref, start=start):
            for at in range(2):
                ref[block(k * 2 + at)] = total[start + k * 2 + at].astype(BF16)
            return carry

        lax.fori_loop(0, blocks // 2, out, 0)
        start += blocks


def products(live, tables, in_row, out_row, tiles, sources, spans, outs, contract, tailed=0):
    lines = sources[0].shape[0] - spans[0] if tailed else 16
    kernel = functools.partial(
        products_kernel,
        spans=spans,
        outs=outs,
        contract=contract,
        in_row=in_row,
        out_row=out_row,
        tailed=tailed,
    )
    return pl.pallas_call(
        kernel,
        out_shape=[jax.ShapeDtypeStruct((n * T, T), BF16) for n in outs]
        + ([jax.ShapeDtypeStruct((lines // 2, 2 * T), F32)] if tailed else []),
        in_specs=[SMEM] * 2 + [ANY] * (1 + len(sources)),
        out_specs=[VMEM] * (len(outs) + (tailed > 0)),
        scratch_shapes=[
            pltpu.VMEM(tiles.shape, BF16),
            pltpu.VMEM((sum(spans), T), BF16),
            pltpu.VMEM((sum(outs), T, T), F32),
            pltpu.VMEM((max(tailed, 1), lines, T), BF16),
            pltpu.SemaphoreType.DMA((len(spans) + 1 + tailed,)),
        ],
        compiler_params=PARAMS,
    )(live, tables, tiles, *sources)


def pack_kernel(*refs):
    pieces, metas, sends, (said, lists, counts), (held, heard, words, table, sems) = (
        refs[:4],
        refs[4:8],
        refs[8:11],
        refs[11:14],
        refs[14:],
    )
    fetches = [pltpu.make_async_copy(p, heard.at[k], sems.at[k + 4]) for k, p in enumerate(metas)]
    copies = [pltpu.make_async_copy(p, held.at[k], sems.at[k]) for k, p in enumerate(pieces)]
    for copy in fetches + copies:
        copy.start()
    for copy in fetches:
        copy.wait()
    told = [heard[k].astype(F32)[:8] for k in range(4)]
    for n in range(3):
        words[pl.ds(n * 8, 8)] = told[n + 1].astype(I32)
    fetch = pltpu.make_async_copy(words, table, sems.at[8])
    fetch.start()
    over = functools.reduce(jnp.maximum, told)[2:3]
    said[...] = jnp.broadcast_to(over, (8, T))
    fetch.wait()
    for copy in copies:
        copy.wait()
    for n in range(3):
        group = 3 - n
        amount = table[n * 8 + 1, group]
        counts[n] = amount

        def step(k, carry, n=n, group=group):
            code = table[n * 8, group * LANES + k]
            lists[n * CAP + k] = code
            sends[n][block(k)] = held[code >> 4, block(code & 15)]
            return carry

        lax.fori_loop(0, amount, step, 0)


def pack(pieces, metas):
    return pl.pallas_call(
        pack_kernel,
        out_shape=[jax.ShapeDtypeStruct((CAP * T, T), BF16)] * 3
        + [jax.ShapeDtypeStruct((8, T), F32)]
        + [jax.ShapeDtypeStruct((3 * CAP,), I32), jax.ShapeDtypeStruct((3,), I32)],
        in_specs=[ANY] * 8,
        out_specs=[VMEM] * 4 + [SMEM] * 2,
        scratch_shapes=[
            pltpu.VMEM((4,) + pieces[0].shape, BF16),
            pltpu.VMEM((4, META, T), BF16),
            pltpu.VMEM((24, T), I32),
            pltpu.SMEM((24, T), I32),
            pltpu.SemaphoreType.DMA((9,)),
        ],
        compiler_params=PARAMS,
    )(*pieces, *metas)


def combine_kernel(lists, counts, own_ref, sums, *refs):
    part_refs, outs, (own, parts, total, sems) = refs[:3], refs[3:7], refs[7:]
    copies = [pltpu.make_async_copy(own_ref, own, sems.at[3])]
    for n, ref in enumerate(part_refs):
        copies.append(pltpu.make_async_copy(ref, parts.at[n], sems.at[n]))
    for copy in copies:
        copy.start()
    for ref in outs[1:]:
        ref[pl.ds(16 * T, sums.shape[0])] = sums[...]
    copies[0].wait()

    def widen(k, carry):
        for at in range(4):
            total[k * 4 + at] = own[block(k * 4 + at)].astype(F32)
        return carry

    lax.fori_loop(0, 16, widen, 0)
    for copy in copies[1:]:
        copy.wait()
    for n in range(3):

        def add(k, carry, n=n):
            total[lists[n * CAP + k]] += parts[n, block(k)].astype(F32)
            return carry

        lax.fori_loop(0, counts[n], add, 0)
    for n, ref in enumerate(outs):

        def out(k, carry, n=n, ref=ref):
            for at in range(4):
                ref[block(k * 4 + at)] = total[n * 16 + k * 4 + at].astype(ref.dtype)
            return carry

        lax.fori_loop(0, 4, out, 0)


def combine(lists, counts, own, sums, parts):
    rows = 16 * T
    return pl.pallas_call(
        combine_kernel,
        out_shape=[jax.ShapeDtypeStruct((rows, T), F32)]
        + [jax.ShapeDtypeStruct((rows + sums.shape[0], T), BF16)] * 3,
        in_specs=[SMEM] * 2 + [ANY, VMEM] + [ANY] * 3,
        out_specs=[VMEM] * 4,
        scratch_shapes=[
            pltpu.VMEM(own.shape, BF16),
            pltpu.VMEM((3,) + parts[0].shape, BF16),
            pltpu.VMEM((64, T, T), F32),
            pltpu.SemaphoreType.DMA((4,)),
        ],
        compiler_params=PARAMS,
    )(lists, counts, own, sums, *parts)


def finish_kernel(*refs, scaling):
    pieces, sums, (nodes, weight, offset) = refs[:4], refs[4], refs[5:]
    rows = nodes.shape[0]
    nodes[...] = total_of([ref[pl.ds(0, rows)] for ref in pieces])
    lines = sums.shape[0]
    for k in range(2):
        part = pl.ds(k * T, T)
        total = sums[:, part]
        for ref in pieces[1:]:
            total = total + ref[pl.ds(rows + k * lines, lines)].astype(F32)
        total = total * scaling
        weight[:, part] = total[:T]
        offset[:, part] = jnp.sum(total[T:], axis=0, keepdims=True)


def finish(pieces, sums, scaling):
    width = sums.shape[-1]
    return pl.pallas_call(
        functools.partial(finish_kernel, scaling=scaling),
        out_shape=[
            jax.ShapeDtypeStruct(pieces[0].shape, F32),
            jax.ShapeDtypeStruct((T, width), F32),
            jax.ShapeDtypeStruct((1, width), F32),
        ],
        in_specs=[VMEM] * 5,
        out_specs=[VMEM] * 3,
        compiler_params=PARAMS,
    )(*pieces, sums)


def dense_kernel(*refs, step):
    parts, (grad, weight, offset), rest = refs[:5], refs[5:8], refs[8:]
    hidden, projected, sums = rest[-3:]
    second = len(rest) > 3

    @pl.when(pl.program_id(0) == 0)
    def _():
        sums[...] = rest[1][...] if second else jnp.zeros_like(sums)

    mixed = total_of([ref[...] for ref in parts])
    high = mixed.astype(BF16)
    low = (mixed - high.astype(F32)).astype(BF16)
    w = weight[...]
    pre = jnp.dot(high, w, preferred_element_type=F32)
    pre = pre + jnp.dot(low, w, preferred_element_type=F32) + offset[...]
    s = jax.nn.sigmoid(pre)
    hidden[...] = (pre * s).astype(BF16)
    slope = (grad[...].astype(F32) * s * (1.0 + pre * (1.0 - s))).astype(BF16)
    projected[pl.ds(pl.multiple_of(pl.program_id(0) * step, step), step)] = lax.dot_general(
        slope, w, (((1,), (1,)), ((), ())), preferred_element_type=F32
    ).astype(BF16)
    over_rows = (((0,), (0,)), ((), ()))
    sums[:T] += lax.dot_general(
        high, slope, over_rows, preferred_element_type=F32
    ) + lax.dot_general(low, slope, over_rows, preferred_element_type=F32)
    sums[T:] += jnp.sum(slope.astype(F32).reshape(-1, 8, slope.shape[1]), axis=0)

    @pl.when((pl.program_id(0) == pl.num_programs(0) - 1) & second)
    def _():
        lines = sums.shape[0]
        for k in range(2 if second else 0):
            part = sums[:, k * T : (k + 1) * T].astype(BF16)
            projected[pl.ds(projected.shape[0] - (2 - k) * lines, lines)] = part


def dense(parts, grad, weight, offset, part, before):
    width, rows = weight.shape[1], grad.shape[0]
    step = 512
    steps = rows // 2 // step
    shift = part * steps
    tail = 2 * (T + 8) if before else 0
    half = pl.BlockSpec((step, T), lambda i: (i, 0))
    full = pl.BlockSpec((step, width), lambda i: (i + shift, 0))

    def whole(*shape):
        return pl.BlockSpec(shape, lambda i: (0, 0))

    return pl.pallas_call(
        functools.partial(dense_kernel, step=step),
        grid=(steps,),
        out_shape=[
            jax.ShapeDtypeStruct((rows, width), BF16),
            jax.ShapeDtypeStruct((rows // 2 + tail, T), BF16),
            jax.ShapeDtypeStruct((T + 8, width), F32),
        ],
        in_specs=[half] * 5
        + [full, whole(T, width), whole(1, width)]
        + ([ANY, whole(T + 8, width), ANY] if before else []),
        out_specs=[full, whole(rows // 2 + tail, T), whole(T + 8, width)],
        input_output_aliases={8: 0} if before else {},
        compiler_params=PARAMS,
    )(*parts, grad, weight, offset, *before)


def on_device(features, weight, offset, tile_values, tile_rows, tile_cols, live_tiles, grad_hidden):
    tiles = tile_values.reshape(tile_values.shape[2:])
    nodes_here = features.shape[0]
    scaling = 1.0 / math.sqrt(nodes_here * lax.axis_size("row") * lax.axis_size("col"))
    at_row, at_col = lax.axis_index("row"), lax.axis_index("col")
    live = live_tiles.reshape(1)
    meta, tables = prepare(at_row.reshape(1), at_col.reshape(1), live, tile_rows, tile_cols)

    pieces = ring_gather(features, along_inner)
    *sends, said, lists, counts = pack(pieces, ring_gather(meta, along_outer))
    named = ring_swap([None] + sends, along_outer)[1:]
    full = functools.reduce(jnp.maximum, ring_gather(said, along_inner))[0, 0] > 0.5

    def forward_all(pieces, named):
        whole = jnp.concatenate(pieces)
        whole = ring_gather(whole, along_outer)
        spans = (4 * nodes_here,) * 4
        return products(live, tables, 2, 0, tiles, whole, spans, (32,) * 4, (1,))

    def forward_named(pieces, named):
        spans = (nodes_here,) * 4 + (CAP * T,) * 3
        return products(live, tables, 1, 0, tiles, pieces + named, spans, (32,) * 4, (1,))

    outs = lax.cond(full, forward_all, forward_named, pieces, named)

    part_rows = nodes_here // 2
    halves = []
    for send, keep in zip(outs[:2], outs[2:]):
        got = other_core(send)
        far = []
        for d in (1, 2, 3):
            at = slice(d * part_rows, (d + 1) * part_rows)
            far.append((keep[at].astype(F32) + got[at].astype(F32)).astype(BF16))
        halves.append([keep, got] + ring_swap([None] + far, along_y)[1:])
    before, own, others = (), [], []
    for part, parts in enumerate(halves):
        hidden, projected, sums = dense(
            parts, grad_hidden, weight, offset.reshape(1, -1), part, before
        )
        here = ring_gather(projected, along_y)
        own.append(here)
        others.append([other_core(piece) for piece in here])
        before = (hidden, sums, others[0][0])

    gathered = others[1] + own[1] + others[0] + own[0]
    spans, outs = (part_rows,) * 16, (64,) + (CAP,) * 3
    here, *parts, sums = products(
        live, tables, 3, 1, tiles, gathered, spans, outs, (0,), tailed=8
    )
    sums = total_of(ring_gather(sums, along_outer))
    rounded = jnp.concatenate([sums[:, :T], sums[:, T:]]).astype(BF16)
    parts = ring_swap([None] + parts, along_outer)[1:]

    def backward_all(here, rounded, parts, gathered):
        outs = products(live, tables, 3, 2, tiles, gathered, spans, (64,) * 4, (0,))
        mine = total_of(ring_swap(outs, along_outer)).reshape(4, nodes_here, T)
        far = [jnp.concatenate([mine[d].astype(BF16), rounded]) for d in (1, 2, 3)]
        return [mine[0]] + far

    def backward_named(here, rounded, parts, gathered):
        return list(combine(lists, counts, here, rounded, parts))

    outs = lax.cond(full, backward_all, backward_named, here, rounded, parts, gathered)
    outs = ring_swap(outs, along_inner)
    grad_features, grad_weight, grad_offset = finish(outs, sums, scaling)
    return (hidden, grad_features, grad_weight, grad_offset.reshape(-1))


def solution(mesh):
    in_specs = (
        P(("col", "row"), None),
        P(),
        P(),
        P("row", "col", None, None, None),
        P("row", "col", None),
        P("row", "col", None),
        P("row", "col"),
        P(("row", "col"), None),
    )
    out_specs = (P(("row", "col"), None), P(("col", "row"), None), P(), P())
    return jax.shard_map(
        on_device, mesh=mesh, in_specs=in_specs, out_specs=out_specs, check_vma=False
    )
```

```python
import functools
import itertools
import math

import jax
import jax.numpy as jnp
from jax import lax
from jax.experimental import pallas as pl
from jax.experimental.pallas import tpu as pltpu
from jax.sharding import PartitionSpec as P

T = 128
F32, BF16, I32 = jnp.float32, jnp.bfloat16, jnp.int32
MIB = 1024 * 1024
GROUP = 4
META = 16
CAP = 26
LANES = 32
SMEM = pl.BlockSpec(memory_space=pltpu.SMEM)
VMEM = pl.BlockSpec(memory_space=pltpu.VMEM)
ANY = pl.BlockSpec(memory_space=pl.ANY)


def room(mib):
    return pltpu.CompilerParams(vmem_limit_bytes=mib * MIB)


def along_xz(value, to, x_core):
    pairs = []
    for x, z, y, core in itertools.product(range(4), range(4), range(4), range(2)):
        far = (to(x) % 4, z) if core == x_core else (x, to(z) % 4)
        pairs.append(((x * 4 + z) * 8 + y * 2 + core, (far[0] * 4 + far[1]) * 8 + y * 2 + core))
    return lax.ppermute(value, ("row", "col"), pairs)


def along_inner(value, to):
    return along_xz(value, to, 0)


def along_outer(value, to):
    return along_xz(value, to, 1)


def along_y(value, to):
    pairs = [(y * 2 + k, to(y) % 4 * 2 + k) for y in range(4) for k in range(2)]
    return lax.ppermute(value, "col", pairs)


def other_core(value):
    pairs = [(y * 2 + k, y * 2 + 1 - k) for y in range(4) for k in range(2)]
    return lax.ppermute(value, "col", pairs)


def ahead(step):
    return lambda at: at + step


def ring_gather(value, along):
    across, after, before = [along(value, ahead(step)) for step in (2, -1, 1)]
    return [value, after, across, before]


def ring_swap(pieces, along):
    across = along(pieces[2], ahead(2))
    return [pieces[0], along(pieces[3], ahead(-1)), across, along(pieces[1], ahead(1))]


def total_of(pieces):
    return sum(piece.astype(F32) for piece in pieces)


def block(place):
    return pl.ds(pl.multiple_of(place * T, T), T)


def prepare_kernel(at_row, at_col, live_ref, rows_ref, cols_ref, meta, tables):
    live = live_ref[0]
    x, z = at_row[0] >> 2, at_row[0] & 3
    y, core = at_col[0] >> 1, at_col[0] & 1
    rows, cols = rows_ref[...], cols_ref[...]
    slots = cols.shape[1]

    same_core = jnp.where(((rows >> 4) & 1) == core, 64, 0)
    row_place = same_core + ((rows >> 3) & 1) * 32 + (((rows >> 5) - y) & 3) * 8 + (rows & 7)
    dx, dz = ((cols >> 6) - x) & 3, ((cols >> 4) - z) & 3
    outer, inner = jnp.where(core == 0, dz, dx), jnp.where(core == 0, dx, dz)
    code = inner * 16 + (cols & 15)
    dense_place = outer * 64 + code

    t = lax.broadcasted_iota(I32, (slots, slots), 0)
    s = lax.broadcasted_iota(I32, (slots, slots), 1)
    lane = lax.broadcasted_iota(I32, (slots, T), 1).astype(F32)

    def column(row):
        return jnp.sum(jnp.where(t == s, row, 0.0), axis=1, keepdims=True)

    def count(mask, value=1.0):
        return jnp.sum(jnp.where(mask, value, 0.0), axis=0, keepdims=True)

    valid = lax.broadcasted_iota(I32, (1, slots), 1) < live
    cols_f, outer_f = cols.astype(F32), outer.astype(F32)
    same = column(cols_f) == cols_f
    first = valid & (count(same & (t < s)) == 0.0)
    first_c = column(jnp.where(first, 1.0, 0.0)) > 0.0
    outer_c = column(outer_f)
    rank = count((t < s) & first_c & (outer_c == outer_f))
    over = jnp.where(first & (outer != 0) & (rank >= CAP), 1.0, 0.0)
    over = jnp.max(over, axis=1, keepdims=True)
    far = (64 + (outer - 1) * CAP).astype(F32) + jnp.minimum(rank, CAP - 1.0)
    place = jnp.where(outer == 0, code.astype(F32), far)
    place = count(same & first_c, column(place))
    place = jnp.where(valid, place, 0.0).astype(I32)
    second = (rows >> 3) & 1
    source = (1 - second) * 64 + ((row_place & 64) >> 1) + (row_place & 31)
    pad = jnp.zeros((4, slots), I32)
    tables[...] = jnp.concatenate([row_place, place, dense_place, source, pad], axis=0)

    key = column(jnp.where(first & (rank < CAP), outer_f * LANES + rank, -1.0))
    wanted = count(key == lane, column(code.astype(F32)))
    amounts = jnp.minimum(count((outer_c == lane) & first_c), 1.0 * CAP)
    line = lax.broadcasted_iota(I32, (META, T), 0)
    lines = [wanted, amounts, jnp.broadcast_to(over, (1, T)), jnp.zeros((META - 3, T), F32)]
    meta[...] = jnp.concatenate(lines, axis=0).astype(BF16)


def prepare(at_row, at_col, live, rows, cols):
    slots = cols.shape[-1]
    return pl.pallas_call(
        prepare_kernel,
        out_shape=[
            jax.ShapeDtypeStruct((META, T), BF16),
            jax.ShapeDtypeStruct((8, slots), I32),
        ],
        in_specs=[SMEM] * 3 + [VMEM] * 2,
        out_specs=[VMEM] * 2,
        compiler_params=room(4),
    )(at_row, at_col, live, rows.reshape(1, slots), cols.reshape(1, slots))


def products_kernel(
    live, tables, tiles_ref, *refs, spans, outs, contract, in_row, out_row, tailed
):
    n = len(spans)
    sources, out_refs, (tiles, held, total, tails, sems) = refs[:n], refs[n:-5], refs[-5:]
    copies = [pltpu.make_async_copy(tiles_ref, tiles, sems.at[n])]
    start = 0
    for k, (ref, rows) in enumerate(zip(sources, spans)):
        copies.append(
            pltpu.make_async_copy(
                ref.at[pl.ds(0, rows)], held.at[pl.ds(start, rows)], sems.at[k]
            )
        )
        start += rows
    for k in range(tailed):
        tail = sources[k].at[pl.ds(spans[k], tails.shape[1])]
        copies.append(pltpu.make_async_copy(tail, tails.at[k], sems.at[n + 1 + k]))
    for copy in copies:
        copy.start()

    zeros = jnp.zeros((4, T, T), F32)

    def clear(k, carry):
        total[pl.ds(k * 4, 4)] = zeros
        return carry

    lax.fori_loop(0, total.shape[0] // 4, clear, 0)
    for copy in copies:
        copy.wait()
    if tailed:
        summed = jnp.sum(tails[...].astype(F32), axis=0)
        lines = summed.shape[0] // 2
        out_refs[-1][:, :T] = summed[:lines]
        out_refs[-1][:, T:] = summed[lines:]
        for ref, blocks in zip(out_refs[1:-1], outs[1:]):
            ref[pl.ds(blocks * T, 2 * lines)] = summed.astype(BF16)

    def group(number, carry):
        products = []
        for k in range(GROUP):
            slot = number * GROUP + k
            product = lax.dot_general(
                tiles[slot],
                held[block(tables[in_row, slot])],
                ((contract, (0,)), ((), ())),
                preferred_element_type=F32,
            )
            products.append(jnp.where(slot < live[0], product, 0.0))
        for k, product in enumerate(products):
            total[tables[out_row, number * GROUP + k]] += product
        return carry

    lax.fori_loop(0, (live[0] + GROUP - 1) // GROUP, group, 0)
    start = 0
    for ref, blocks in zip(out_refs, outs):

        def out(k, carry, ref=ref, start=start):
            for at in range(2):
                ref[block(k * 2 + at)] = total[start + k * 2 + at].astype(BF16)
            return carry

        lax.fori_loop(0, blocks // 2, out, 0)
        start += blocks


def products(live, tables, in_row, out_row, tiles, sources, spans, outs, contract, tailed=0):
    lines = sources[0].shape[0] - spans[0] if tailed else 16
    kernel = functools.partial(
        products_kernel,
        spans=spans,
        outs=outs,
        contract=contract,
        in_row=in_row,
        out_row=out_row,
        tailed=tailed,
    )
    need = tiles.size * 2 + sum(spans) * T * 2 + sum(outs) * T * T * 6
    extra = [lines if tailed and n else 0 for n in range(len(outs))]
    return pl.pallas_call(
        kernel,
        out_shape=[jax.ShapeDtypeStruct((n * T + e, T), BF16) for n, e in zip(outs, extra)]
        + ([jax.ShapeDtypeStruct((lines // 2, 2 * T), F32)] if tailed else []),
        in_specs=[SMEM] * 2 + [ANY] * (1 + len(sources)),
        out_specs=[VMEM] * (len(outs) + (tailed > 0)),
        scratch_shapes=[
            pltpu.VMEM(tiles.shape, BF16),
            pltpu.VMEM((sum(spans), T), BF16),
            pltpu.VMEM((sum(outs), T, T), F32),
            pltpu.VMEM((max(tailed, 1), lines, T), BF16),
            pltpu.SemaphoreType.DMA((len(spans) + 1 + tailed,)),
        ],
        compiler_params=room(need // MIB + 5),
    )(live, tables, tiles, *sources)


def pack_kernel(*refs):
    pieces, metas, sends, (said, lists, counts), (held, heard, words, table, sems) = (
        refs[:4],
        refs[4:8],
        refs[8:11],
        refs[11:14],
        refs[14:],
    )
    fetches = [pltpu.make_async_copy(p, heard.at[k], sems.at[k + 4]) for k, p in enumerate(metas)]
    copies = [pltpu.make_async_copy(p, held.at[k], sems.at[k]) for k, p in enumerate(pieces)]
    for copy in fetches + copies:
        copy.start()
    for copy in fetches:
        copy.wait()
    told = [heard[k].astype(F32)[:8] for k in range(4)]
    for n in range(3):
        words[pl.ds(n * 8, 8)] = told[n + 1].astype(I32)
    fetch = pltpu.make_async_copy(words, table, sems.at[8])
    fetch.start()
    over = functools.reduce(jnp.maximum, told)[2:3]
    said[...] = jnp.broadcast_to(over, (8, T))
    fetch.wait()
    for copy in copies:
        copy.wait()
    for n in range(3):
        group = 3 - n
        amount = table[n * 8 + 1, group]
        counts[n] = amount

        def step(k, carry, n=n, group=group):
            code = table[n * 8, group * LANES + k]
            lists[n * CAP + k] = code
            sends[n][block(k)] = held[code >> 4, block(code & 15)]
            return carry

        lax.fori_loop(0, amount, step, 0)


def pack(pieces, metas):
    return pl.pallas_call(
        pack_kernel,
        out_shape=[jax.ShapeDtypeStruct((CAP * T, T), BF16)] * 3
        + [jax.ShapeDtypeStruct((8, T), F32)]
        + [jax.ShapeDtypeStruct((3 * CAP,), I32), jax.ShapeDtypeStruct((3,), I32)],
        in_specs=[ANY] * 8,
        out_specs=[VMEM] * 4 + [SMEM] * 2,
        scratch_shapes=[
            pltpu.VMEM((4,) + pieces[0].shape, BF16),
            pltpu.VMEM((4, META, T), BF16),
            pltpu.VMEM((24, T), I32),
            pltpu.SMEM((24, T), I32),
            pltpu.SemaphoreType.DMA((9,)),
        ],
        compiler_params=room(10),
    )(*pieces, *metas)


def combine_kernel(lists, counts, own_ref, sums, *refs):
    part_refs, outs, summed, (own, parts, total, sems) = refs[:3], refs[3:7], refs[7], refs[8:]
    copies = [pltpu.make_async_copy(own_ref, own, sems.at[3])]
    for n, ref in enumerate(part_refs):
        copies.append(pltpu.make_async_copy(ref, parts.at[n], sems.at[n]))
    for copy in copies:
        copy.start()
    copies[0].wait()

    def widen(k, carry):
        for at in range(4):
            total[k * 4 + at] = own[block(k * 4 + at)].astype(F32)
        return carry

    lax.fori_loop(0, 16, widen, 0)
    for copy in copies[1:]:
        copy.wait()
    lines = sums.shape[0]
    for k in range(2):
        tail = pl.ds(CAP * T + k * lines, lines)
        line = sums[:, k * T : (k + 1) * T] + total_of([parts[n, tail] for n in range(3)])
        summed[:, k * T : (k + 1) * T] = line
        for ref in outs[1:]:
            ref[pl.ds(16 * T + k * lines, lines)] = line.astype(BF16)
    for n in range(3):

        def add(k, carry, n=n):
            total[lists[n * CAP + k]] += parts[n, block(k)].astype(F32)
            return carry

        lax.fori_loop(0, counts[n], add, 0)
    for n, ref in enumerate(outs):

        def out(k, carry, n=n, ref=ref):
            for at in range(4):
                ref[block(k * 4 + at)] = total[n * 16 + k * 4 + at].astype(ref.dtype)
            return carry

        lax.fori_loop(0, 4, out, 0)


def combine(lists, counts, own, sums, parts):
    rows = 16 * T
    return pl.pallas_call(
        combine_kernel,
        out_shape=[jax.ShapeDtypeStruct((rows, T), F32)]
        + [jax.ShapeDtypeStruct((rows + 2 * sums.shape[0], T), BF16)] * 3
        + [jax.ShapeDtypeStruct(sums.shape, F32)],
        in_specs=[SMEM] * 2 + [ANY, VMEM] + [ANY] * 3,
        out_specs=[VMEM] * 5,
        scratch_shapes=[
            pltpu.VMEM(own.shape, BF16),
            pltpu.VMEM((3,) + parts[0].shape, BF16),
            pltpu.VMEM((64, T, T), F32),
            pltpu.SemaphoreType.DMA((4,)),
        ],
        compiler_params=room(16),
    )(lists, counts, own, sums, *parts)


def finish_kernel(*refs, scaling):
    pieces, sums, (nodes, weight, offset) = refs[:4], refs[4], refs[5:]
    rows = nodes.shape[0]
    nodes[...] = total_of([ref[pl.ds(0, rows)] for ref in pieces])
    lines = sums.shape[0]
    for k in range(2):
        part = pl.ds(k * T, T)
        total = sums[:, part]
        for ref in pieces[1:]:
            total = total + ref[pl.ds(rows + k * lines, lines)].astype(F32)
        total = total * scaling
        weight[:, part] = total[:T]
        offset[:, part] = jnp.sum(total[T:], axis=0, keepdims=True)


def finish(pieces, sums, scaling):
    width = sums.shape[-1]
    return pl.pallas_call(
        functools.partial(finish_kernel, scaling=scaling),
        out_shape=[
            jax.ShapeDtypeStruct(pieces[0].shape, F32),
            jax.ShapeDtypeStruct((T, width), F32),
            jax.ShapeDtypeStruct((1, width), F32),
        ],
        in_specs=[VMEM] * 5,
        out_specs=[VMEM] * 3,
        compiler_params=room(10),
    )(*pieces, sums)


def dense_kernel(*refs, step):
    parts, (grad, weight, offset), rest = refs[:5], refs[5:8], refs[8:]
    hidden, projected, sums = rest[-3:]
    second = len(rest) > 3

    @pl.when(pl.program_id(0) == 0)
    def _():
        sums[...] = rest[1][...] if second else jnp.zeros_like(sums)

    mixed = total_of([ref[...] for ref in parts])
    high = mixed.astype(BF16)
    low = (mixed - high.astype(F32)).astype(BF16)
    w = weight[...]
    pre = jnp.dot(high, w, preferred_element_type=F32)
    pre = pre + jnp.dot(low, w, preferred_element_type=F32) + offset[...]
    s = jax.nn.sigmoid(pre)
    hidden[...] = (pre * s).astype(BF16)
    slope = (grad[...].astype(F32) * s * (1.0 + pre * (1.0 - s))).astype(BF16)
    projected[pl.ds(pl.multiple_of(pl.program_id(0) * step, step), step)] = lax.dot_general(
        slope, w, (((1,), (1,)), ((), ())), preferred_element_type=F32
    ).astype(BF16)
    over_rows = (((0,), (0,)), ((), ()))
    sums[:T] += lax.dot_general(
        high, slope, over_rows, preferred_element_type=F32
    ) + lax.dot_general(low, slope, over_rows, preferred_element_type=F32)
    sums[T:] += jnp.sum(slope.astype(F32).reshape(-1, 8, slope.shape[1]), axis=0)

    @pl.when((pl.program_id(0) == pl.num_programs(0) - 1) & second)
    def _():
        lines = sums.shape[0]
        for k in range(2 if second else 0):
            part = sums[:, k * T : (k + 1) * T].astype(BF16)
            projected[pl.ds(projected.shape[0] - (2 - k) * lines, lines)] = part


def dense(parts, grad, weight, offset, part, before):
    width, rows = weight.shape[1], grad.shape[0]
    step = 512
    steps = rows // 2 // step
    shift = part * steps
    tail = 2 * (T + 8) if before else 0
    half = pl.BlockSpec((step, T), lambda i: (i, 0))
    full = pl.BlockSpec((step, width), lambda i: (i + shift, 0))

    def whole(*shape):
        return pl.BlockSpec(shape, lambda i: (0, 0))

    return pl.pallas_call(
        functools.partial(dense_kernel, step=step),
        grid=(steps,),
        out_shape=[
            jax.ShapeDtypeStruct((rows, width), BF16),
            jax.ShapeDtypeStruct((rows // 2 + tail, T), BF16),
            jax.ShapeDtypeStruct((T + 8, width), F32),
        ],
        in_specs=[half] * 5
        + [full, whole(T, width), whole(1, width)]
        + ([ANY, whole(T + 8, width), ANY] if before else []),
        out_specs=[full, whole(rows // 2 + tail, T), whole(T + 8, width)],
        input_output_aliases={8: 0} if before else {},
        compiler_params=room(14),
    )(*parts, grad, weight, offset, *before)


def on_device(features, weight, offset, tile_values, tile_rows, tile_cols, live_tiles, grad_hidden):
    tiles = tile_values.reshape(tile_values.shape[2:])
    nodes_here = features.shape[0]
    scaling = 1.0 / math.sqrt(nodes_here * lax.axis_size("row") * lax.axis_size("col"))
    at_row, at_col = lax.axis_index("row"), lax.axis_index("col")
    live = live_tiles.reshape(1)
    meta, tables = prepare(at_row.reshape(1), at_col.reshape(1), live, tile_rows, tile_cols)

    pieces = ring_gather(features, along_inner)
    *sends, said, lists, counts = pack(pieces, ring_gather(meta, along_outer))
    named = ring_swap([None] + sends, along_outer)[1:]
    full = functools.reduce(jnp.maximum, ring_gather(said, along_inner))[0, 0] > 0.5

    def forward_all(pieces, named):
        whole = jnp.concatenate(pieces)
        whole = ring_gather(whole, along_outer)
        spans = (4 * nodes_here,) * 4
        return products(live, tables, 2, 0, tiles, whole, spans, (32,) * 4, (1,))

    def forward_named(pieces, named):
        spans = (nodes_here,) * 4 + (CAP * T,) * 3
        return products(live, tables, 1, 0, tiles, pieces + named, spans, (32,) * 4, (1,))

    outs = lax.cond(full, forward_all, forward_named, pieces, named)

    part_rows = nodes_here // 2
    halves = []
    for send, keep in zip(outs[:2], outs[2:]):
        got = other_core(send)
        far = []
        for d in (1, 2, 3):
            at = slice(d * part_rows, (d + 1) * part_rows)
            far.append((keep[at].astype(F32) + got[at].astype(F32)).astype(BF16))
        halves.append([keep, got] + ring_swap([None] + far, along_y)[1:])
    before, own, others = (), [], []
    for part, parts in enumerate(halves):
        hidden, projected, sums = dense(
            parts, grad_hidden, weight, offset.reshape(1, -1), part, before
        )
        here = ring_gather(projected, along_y)
        own.append(here)
        others.append([other_core(piece) for piece in here])
        before = (hidden, sums, others[0][0])

    gathered = others[1] + own[1] + others[0] + own[0]
    spans, outs = (part_rows,) * 16, (64,) + (CAP,) * 3
    here, *parts, sums = products(
        live, tables, 3, 1, tiles, gathered, spans, outs, (0,), tailed=8
    )
    parts = ring_swap([None] + parts, along_outer)[1:]

    def backward_all(here, sums, parts, gathered):
        outs = products(live, tables, 3, 2, tiles, gathered, spans, (64,) * 4, (0,))
        mine = total_of(ring_swap(outs, along_outer)).reshape(4, nodes_here, T)
        tail = total_of([p[CAP * T :] for p in parts])
        lines = sums.shape[0]
        sums = sums + jnp.concatenate([tail[:lines], tail[lines:]], axis=1)
        tail = jnp.concatenate([sums[:, :T], sums[:, T:]]).astype(BF16)
        far = [jnp.concatenate([mine[d].astype(BF16), tail]) for d in (1, 2, 3)]
        return [mine[0]] + far + [sums]

    def backward_named(here, sums, parts, gathered):
        return list(combine(lists, counts, here, sums, parts))

    *outs, sums = lax.cond(full, backward_all, backward_named, here, sums, parts, gathered)
    outs = ring_swap(outs, along_inner)
    grad_features, grad_weight, grad_offset = finish(outs, sums, scaling)
    return (hidden, grad_features, grad_weight, grad_offset.reshape(-1))


def solution(mesh):
    in_specs = (
        P(("col", "row"), None),
        P(),
        P(),
        P("row", "col", None, None, None),
        P("row", "col", None),
        P("row", "col", None),
        P("row", "col"),
        P(("row", "col"), None),
    )
    out_specs = (P(("row", "col"), None), P(("col", "row"), None), P(), P())
    return jax.shard_map(
        on_device, mesh=mesh, in_specs=in_specs, out_specs=out_specs, check_vma=False
    )
```

```python
import functools
import itertools
import math

import jax
import jax.numpy as jnp
from jax import lax
from jax.experimental import pallas as pl
from jax.experimental.pallas import tpu as pltpu
from jax.sharding import PartitionSpec as P

T = 128
F32, BF16, I32 = jnp.float32, jnp.bfloat16, jnp.int32
MIB = 1024 * 1024
GROUP = 16
META = 16
CAP = 26
LANES = 32
SMEM = pl.BlockSpec(memory_space=pltpu.SMEM)
VMEM = pl.BlockSpec(memory_space=pltpu.VMEM)
ANY = pl.BlockSpec(memory_space=pl.ANY)


def room(mib):
    return pltpu.CompilerParams(vmem_limit_bytes=mib * MIB)


def along_xz(value, to, x_core):
    pairs = []
    for x, z, y, core in itertools.product(range(4), range(4), range(4), range(2)):
        far = (to(x) % 4, z) if core == x_core else (x, to(z) % 4)
        pairs.append(((x * 4 + z) * 8 + y * 2 + core, (far[0] * 4 + far[1]) * 8 + y * 2 + core))
    return lax.ppermute(value, ("row", "col"), pairs)


def along_inner(value, to):
    return along_xz(value, to, 0)


def along_outer(value, to):
    return along_xz(value, to, 1)


def along_y(value, to):
    pairs = []
    for y in range(4):
        pairs.append((y * 2, to(y) % 4 * 2))
        pairs.append((y * 2 + 1, (2 * y - to(y)) % 4 * 2 + 1))
    return lax.ppermute(value, "col", pairs)


def other_core(value):
    pairs = [(y * 2 + k, y * 2 + 1 - k) for y in range(4) for k in range(2)]
    return lax.ppermute(value, "col", pairs)


def ahead(step):
    return lambda at: at + step


def ring_gather(value, along):
    across, after, before = [along(value, ahead(step)) for step in (2, -1, 1)]
    return [value, after, across, before]


def ring_swap(pieces, along):
    across = along(pieces[2], ahead(2))
    return [pieces[0], along(pieces[3], ahead(-1)), across, along(pieces[1], ahead(1))]


def total_of(pieces):
    return sum(piece.astype(F32) for piece in pieces)


def block(place):
    return pl.ds(pl.multiple_of(place * T, T), T)


def prepare_kernel(at_row, at_col, live_ref, rows_ref, cols_ref, meta, tables):
    live = live_ref[0]
    x, z = at_row[0] >> 2, at_row[0] & 3
    y, core = at_col[0] >> 1, at_col[0] & 1
    rows, cols = rows_ref[...], cols_ref[...]
    slots = cols.shape[1]

    far_core = (rows >> 4) & 1
    same_core = jnp.where(far_core == core, 64, 0)
    dy = (rows >> 5) - y
    dy = jnp.where(far_core == 0, dy, -dy) & 3
    row_place = same_core + ((rows >> 3) & 1) * 32 + dy * 8 + (rows & 7)
    dx, dz = ((cols >> 6) - x) & 3, ((cols >> 4) - z) & 3
    outer, inner = jnp.where(core == 0, dz, dx), jnp.where(core == 0, dx, dz)
    code = inner * 16 + (cols & 15)
    dense_place = outer * 64 + code

    t = lax.broadcasted_iota(I32, (slots, slots), 0)
    s = lax.broadcasted_iota(I32, (slots, slots), 1)
    lane = lax.broadcasted_iota(I32, (slots, T), 1).astype(F32)

    def column(row):
        return jnp.sum(jnp.where(t == s, row, 0.0), axis=1, keepdims=True)

    def count(mask, value=1.0):
        return jnp.sum(jnp.where(mask, value, 0.0), axis=0, keepdims=True)

    valid = lax.broadcasted_iota(I32, (1, slots), 1) < live
    cols_f, outer_f = cols.astype(F32), outer.astype(F32)
    same = column(cols_f) == cols_f
    first = valid & (count(same & (t < s)) == 0.0)
    first_c = column(jnp.where(first, 1.0, 0.0)) > 0.0
    outer_c = column(outer_f)
    rank = count((t < s) & first_c & (outer_c == outer_f))
    over = jnp.where(first & (outer != 0) & (rank >= CAP), 1.0, 0.0)
    over = jnp.max(over, axis=1, keepdims=True)
    far = (64 + (outer - 1) * CAP).astype(F32) + jnp.minimum(rank, CAP - 1.0)
    place = jnp.where(outer == 0, code.astype(F32), far)
    place = count(same & first_c, column(place))
    place = jnp.where(valid, place, 0.0).astype(I32)
    second = (rows >> 3) & 1
    source = (1 - second) * 64 + ((row_place & 64) >> 1) + (row_place & 31)
    pad = jnp.zeros((4, slots), I32)
    tables[...] = jnp.concatenate([row_place, place, dense_place, source, pad], axis=0)

    key = column(jnp.where(first & (rank < CAP), outer_f * LANES + rank, -1.0))
    wanted = count(key == lane, column(code.astype(F32)))
    amounts = jnp.minimum(count((outer_c == lane) & first_c), 1.0 * CAP)
    line = lax.broadcasted_iota(I32, (META, T), 0)
    lines = [wanted, amounts, jnp.broadcast_to(over, (1, T)), jnp.zeros((META - 3, T), F32)]
    meta[...] = jnp.concatenate(lines, axis=0).astype(BF16)


def prepare(at_row, at_col, live, rows, cols):
    slots = cols.shape[-1]
    return pl.pallas_call(
        prepare_kernel,
        out_shape=[
            jax.ShapeDtypeStruct((META, T), BF16),
            jax.ShapeDtypeStruct((8, slots), I32),
        ],
        in_specs=[SMEM] * 3 + [VMEM] * 2,
        out_specs=[VMEM] * 2,
        compiler_params=room(4),
    )(at_row, at_col, live, rows.reshape(1, slots), cols.reshape(1, slots))


def products_kernel(
    live, tables, tiles_ref, *refs, spans, outs, contract, in_row, out_row, tailed
):
    n = len(spans)
    sources, out_refs, (tiles, held, total, tails, sems) = refs[:n], refs[n:-5], refs[-5:]
    copies = [pltpu.make_async_copy(tiles_ref, tiles, sems.at[n])]
    start = 0
    for k, (ref, rows) in enumerate(zip(sources, spans)):
        copies.append(
            pltpu.make_async_copy(
                ref.at[pl.ds(0, rows)], held.at[pl.ds(start, rows)], sems.at[k]
            )
        )
        start += rows
    for k in range(tailed):
        tail = sources[k].at[pl.ds(spans[k], tails.shape[1])]
        copies.append(pltpu.make_async_copy(tail, tails.at[k], sems.at[n + 1 + k]))
    for copy in copies:
        copy.start()

    zeros = jnp.zeros((4, T, T), F32)

    def clear(k, carry):
        total[pl.ds(k * 4, 4)] = zeros
        return carry

    lax.fori_loop(0, total.shape[0] // 4, clear, 0)
    for copy in copies:
        copy.wait()
    if tailed:
        summed = jnp.sum(tails[...].astype(F32), axis=0)
        lines = summed.shape[0] // 2
        out_refs[-1][:, :T] = summed[:lines]
        out_refs[-1][:, T:] = summed[lines:]
        for ref, blocks in zip(out_refs[1:-1], outs[1:]):
            ref[pl.ds(blocks * T, 2 * lines)] = summed.astype(BF16)

    def group(number, carry):
        products = []
        for k in range(GROUP):
            slot = number * GROUP + k
            product = lax.dot_general(
                tiles[slot],
                held[block(tables[in_row, slot])],
                ((contract, (0,)), ((), ())),
                preferred_element_type=F32,
            )
            products.append(jnp.where(slot < live[0], product, 0.0))
        for k, product in enumerate(products):
            total[tables[out_row, number * GROUP + k]] += product
        return carry

    lax.fori_loop(0, (live[0] + GROUP - 1) // GROUP, group, 0)
    start = 0
    for ref, blocks in zip(out_refs, outs):

        def out(k, carry, ref=ref, start=start):
            for at in range(2):
                ref[block(k * 2 + at)] = total[start + k * 2 + at].astype(BF16)
            return carry

        lax.fori_loop(0, blocks // 2, out, 0)
        start += blocks


def products(live, tables, in_row, out_row, tiles, sources, spans, outs, contract, tailed=0):
    lines = sources[0].shape[0] - spans[0] if tailed else 16
    kernel = functools.partial(
        products_kernel,
        spans=spans,
        outs=outs,
        contract=contract,
        in_row=in_row,
        out_row=out_row,
        tailed=tailed,
    )
    need = tiles.size * 2 + sum(spans) * T * 2 + sum(outs) * T * T * 6
    extra = [lines if tailed and n else 0 for n in range(len(outs))]
    return pl.pallas_call(
        kernel,
        out_shape=[jax.ShapeDtypeStruct((n * T + e, T), BF16) for n, e in zip(outs, extra)]
        + ([jax.ShapeDtypeStruct((lines // 2, 2 * T), F32)] if tailed else []),
        in_specs=[SMEM] * 2 + [ANY] * (1 + len(sources)),
        out_specs=[VMEM] * (len(outs) + (tailed > 0)),
        scratch_shapes=[
            pltpu.VMEM(tiles.shape, BF16),
            pltpu.VMEM((sum(spans), T), BF16),
            pltpu.VMEM((sum(outs), T, T), F32),
            pltpu.VMEM((max(tailed, 1), lines, T), BF16),
            pltpu.SemaphoreType.DMA((len(spans) + 1 + tailed,)),
        ],
        compiler_params=room(need // MIB + 5),
    )(live, tables, tiles, *sources)


def pack_kernel(*refs):
    pieces, metas, sends, (said, lists, counts), (held, heard, words, table, sems) = (
        refs[:4],
        refs[4:8],
        refs[8:11],
        refs[11:14],
        refs[14:],
    )
    fetches = [pltpu.make_async_copy(p, heard.at[k], sems.at[k + 4]) for k, p in enumerate(metas)]
    copies = [pltpu.make_async_copy(p, held.at[k], sems.at[k]) for k, p in enumerate(pieces)]
    for copy in fetches + copies:
        copy.start()
    for copy in fetches:
        copy.wait()
    told = [heard[k].astype(F32)[:8] for k in range(4)]
    for n in range(3):
        words[pl.ds(n * 8, 8)] = told[n + 1].astype(I32)
    fetch = pltpu.make_async_copy(words, table, sems.at[8])
    fetch.start()
    over = functools.reduce(jnp.maximum, told)[2:3]
    said[...] = jnp.broadcast_to(over, (8, T))
    fetch.wait()
    for copy in copies:
        copy.wait()
    for n in range(3):
        group = 3 - n
        amount = table[n * 8 + 1, group]
        counts[n] = amount
        for k in range(4):
            lists[n * LANES + amount + k] = 64

        def step(k, carry, n=n, group=group):
            code = table[n * 8, group * LANES + k]
            lists[n * LANES + k] = code
            sends[n][block(k)] = held[code >> 4, block(code & 15)]
            return carry

        lax.fori_loop(0, amount, step, 0)


def pack(pieces, metas):
    return pl.pallas_call(
        pack_kernel,
        out_shape=[jax.ShapeDtypeStruct((CAP * T, T), BF16)] * 3
        + [jax.ShapeDtypeStruct((8, T), F32)]
        + [jax.ShapeDtypeStruct((3 * LANES,), I32), jax.ShapeDtypeStruct((3,), I32)],
        in_specs=[ANY] * 8,
        out_specs=[VMEM] * 4 + [SMEM] * 2,
        scratch_shapes=[
            pltpu.VMEM((4,) + pieces[0].shape, BF16),
            pltpu.VMEM((4, META, T), BF16),
            pltpu.VMEM((24, T), I32),
            pltpu.SMEM((24, T), I32),
            pltpu.SemaphoreType.DMA((9,)),
        ],
        compiler_params=room(10),
    )(*pieces, *metas)


def combine_kernel(lists, counts, own_ref, sums, *refs):
    part_refs, outs, summed, (own, parts, total, sems) = refs[:3], refs[3:7], refs[7], refs[8:]
    copies = [pltpu.make_async_copy(own_ref, own, sems.at[3])]
    for n, ref in enumerate(part_refs):
        copies.append(pltpu.make_async_copy(ref, parts.at[n], sems.at[n]))
    for copy in copies:
        copy.start()
    copies[0].wait()

    def widen(k, carry):
        for at in range(4):
            total[k * 4 + at] = own[block(k * 4 + at)].astype(F32)
        return carry

    lax.fori_loop(0, 16, widen, 0)
    for copy in copies[1:]:
        copy.wait()
    lines = sums.shape[0]
    for k in range(2):
        tail = pl.ds(CAP * T + k * lines, lines)
        line = sums[:, k * T : (k + 1) * T] + total_of([parts[n, tail] for n in range(3)])
        summed[:, k * T : (k + 1) * T] = line
        for ref in outs[1:]:
            ref[pl.ds(16 * T + k * lines, lines)] = line.astype(BF16)
    for n in range(3):

        def add(k, carry, n=n):
            for at in range(4):
                slot = k * 4 + at
                total[lists[n * LANES + slot]] += parts[n, block(slot)].astype(F32)
            return carry

        lax.fori_loop(0, (counts[n] + 3) // 4, add, 0)
    for n, ref in enumerate(outs):

        def out(k, carry, n=n, ref=ref):
            for at in range(4):
                ref[block(k * 4 + at)] = total[n * 16 + k * 4 + at].astype(ref.dtype)
            return carry

        lax.fori_loop(0, 4, out, 0)


def combine(lists, counts, own, sums, parts):
    rows = 16 * T
    return pl.pallas_call(
        combine_kernel,
        out_shape=[jax.ShapeDtypeStruct((rows, T), F32)]
        + [jax.ShapeDtypeStruct((rows + 2 * sums.shape[0], T), BF16)] * 3
        + [jax.ShapeDtypeStruct(sums.shape, F32)],
        in_specs=[SMEM] * 2 + [ANY, VMEM] + [ANY] * 3,
        out_specs=[VMEM] * 5,
        scratch_shapes=[
            pltpu.VMEM(own.shape, BF16),
            pltpu.VMEM((3,) + parts[0].shape, BF16),
            pltpu.VMEM((65, T, T), F32),
            pltpu.SemaphoreType.DMA((4,)),
        ],
        compiler_params=room(16),
    )(lists, counts, own, sums, *parts)


def finish_kernel(*refs, scaling):
    pieces, sums, (nodes, weight, offset), (held, sems) = refs[:4], refs[4], refs[5:8], refs[8:]
    rows = nodes.shape[0]
    copies = []
    for k in range(4):
        part = pl.ds(k * rows // 4, rows // 4)
        held[part] = total_of([ref[part] for ref in pieces])
        copies.append(pltpu.make_async_copy(held.at[part], nodes.at[part], sems.at[k]))
        copies[k].start()
    lines = sums.shape[0]
    for k in range(2):
        part = pl.ds(k * T, T)
        total = sums[:, part]
        for ref in pieces[1:]:
            total = total + ref[pl.ds(rows + k * lines, lines)].astype(F32)
        total = total * scaling
        weight[:, part] = total[:T]
        offset[:, part] = jnp.sum(total[T:], axis=0, keepdims=True)
    for copy in copies:
        copy.wait()


def finish(pieces, sums, scaling):
    width = sums.shape[-1]
    return pl.pallas_call(
        functools.partial(finish_kernel, scaling=scaling),
        out_shape=[
            jax.ShapeDtypeStruct(pieces[0].shape, F32),
            jax.ShapeDtypeStruct((T, width), F32),
            jax.ShapeDtypeStruct((1, width), F32),
        ],
        in_specs=[VMEM] * 5,
        out_specs=[ANY] + [VMEM] * 2,
        scratch_shapes=[pltpu.VMEM(pieces[0].shape, F32), pltpu.SemaphoreType.DMA((4,))],
        compiler_params=room(10),
    )(*pieces, sums)


def dense_kernel(*refs, step):
    parts, (grad, weight, offset), rest = refs[:5], refs[5:8], refs[8:]
    hidden, projected, sums = rest[-3:]
    second = len(rest) > 3

    @pl.when(pl.program_id(0) == 0)
    def _():
        sums[...] = rest[1][...] if second else jnp.zeros_like(sums)

    mixed = total_of([ref[...] for ref in parts])
    high = mixed.astype(BF16)
    low = (mixed - high.astype(F32)).astype(BF16)
    w = weight[...]
    pre = jnp.dot(high, w, preferred_element_type=F32)
    pre = pre + jnp.dot(low, w, preferred_element_type=F32) + offset[...]
    s = jax.nn.sigmoid(pre)
    hidden[...] = (pre * s).astype(BF16)
    slope = (grad[...].astype(F32) * s * (1.0 + pre * (1.0 - s))).astype(BF16)
    projected[pl.ds(pl.multiple_of(pl.program_id(0) * step, step), step)] = lax.dot_general(
        slope, w, (((1,), (1,)), ((), ())), preferred_element_type=F32
    ).astype(BF16)
    over_rows = (((0,), (0,)), ((), ()))
    sums[:T] += lax.dot_general(
        high, slope, over_rows, preferred_element_type=F32
    ) + lax.dot_general(low, slope, over_rows, preferred_element_type=F32)
    sums[T:] += jnp.sum(slope.astype(F32).reshape(-1, 8, slope.shape[1]), axis=0)

    @pl.when((pl.program_id(0) == pl.num_programs(0) - 1) & second)
    def _():
        lines = sums.shape[0]
        for k in range(2 if second else 0):
            part = sums[:, k * T : (k + 1) * T].astype(BF16)
            projected[pl.ds(projected.shape[0] - (2 - k) * lines, lines)] = part


def dense(parts, grad, weight, offset, part, before):
    width, rows = weight.shape[1], grad.shape[0]
    step = 512
    steps = rows // 2 // step
    shift = part * steps
    tail = 2 * (T + 8) if before else 0
    half = pl.BlockSpec((step, T), lambda i: (i, 0))
    full = pl.BlockSpec((step, width), lambda i: (i + shift, 0))

    def whole(*shape):
        return pl.BlockSpec(shape, lambda i: (0, 0))

    return pl.pallas_call(
        functools.partial(dense_kernel, step=step),
        grid=(steps,),
        out_shape=[
            jax.ShapeDtypeStruct((rows, width), BF16),
            jax.ShapeDtypeStruct((rows // 2 + tail, T), BF16),
            jax.ShapeDtypeStruct((T + 8, width), F32),
        ],
        in_specs=[half] * 5
        + [full, whole(T, width), whole(1, width)]
        + ([ANY, whole(T + 8, width), ANY] if before else []),
        out_specs=[full, whole(rows // 2 + tail, T), whole(T + 8, width)],
        input_output_aliases={8: 0} if before else {},
        compiler_params=room(14),
    )(*parts, grad, weight, offset, *before)


def on_device(features, weight, offset, tile_values, tile_rows, tile_cols, live_tiles, grad_hidden):
    tiles = tile_values.reshape(tile_values.shape[2:])
    nodes_here = features.shape[0]
    scaling = 1.0 / math.sqrt(nodes_here * lax.axis_size("row") * lax.axis_size("col"))
    at_row, at_col = lax.axis_index("row"), lax.axis_index("col")
    live = live_tiles.reshape(1)
    meta, tables = prepare(at_row.reshape(1), at_col.reshape(1), live, tile_rows, tile_cols)

    pieces = ring_gather(features, along_inner)
    *sends, said, lists, counts = pack(pieces, ring_gather(meta, along_outer))
    named = ring_swap([None] + sends, along_outer)[1:]
    full = functools.reduce(jnp.maximum, ring_gather(said, along_inner))[0, 0] > 0.5

    def forward_all(pieces, named):
        whole = jnp.concatenate(pieces)
        whole = ring_gather(whole, along_outer)
        spans = (4 * nodes_here,) * 4
        return products(live, tables, 2, 0, tiles, whole, spans, (32,) * 4, (1,))

    def forward_named(pieces, named):
        spans = (nodes_here,) * 4 + (CAP * T,) * 3
        return products(live, tables, 1, 0, tiles, pieces + named, spans, (32,) * 4, (1,))

    outs = lax.cond(full, forward_all, forward_named, pieces, named)

    part_rows = nodes_here // 2
    halves = []
    for send, keep in zip(outs[:2], outs[2:]):
        got = other_core(send)
        far = []
        for d in (1, 2, 3):
            at = slice(d * part_rows, (d + 1) * part_rows)
            far.append((keep[at].astype(F32) + got[at].astype(F32)).astype(BF16))
        halves.append([keep, got] + ring_swap([None] + far, along_y)[1:])
    before, own, others = (), [], []
    for part, parts in enumerate(halves):
        hidden, projected, sums = dense(
            parts, grad_hidden, weight, offset.reshape(1, -1), part, before
        )
        here = ring_gather(projected, along_y)
        own.append(here)
        others.append([other_core(piece) for piece in here])
        before = (hidden, sums, others[0][0])

    gathered = others[1] + own[1] + others[0] + own[0]
    spans, outs = (part_rows,) * 16, (64,) + (CAP,) * 3
    here, *parts, sums = products(
        live, tables, 3, 1, tiles, gathered, spans, outs, (0,), tailed=8
    )
    parts = ring_swap([None] + parts, along_outer)[1:]

    def backward_all(here, sums, parts, gathered):
        outs = products(live, tables, 3, 2, tiles, gathered, spans, (64,) * 4, (0,))
        mine = total_of(ring_swap(outs, along_outer)).reshape(4, nodes_here, T)
        tail = total_of([p[CAP * T :] for p in parts])
        lines = sums.shape[0]
        sums = sums + jnp.concatenate([tail[:lines], tail[lines:]], axis=1)
        tail = jnp.concatenate([sums[:, :T], sums[:, T:]]).astype(BF16)
        far = [jnp.concatenate([mine[d].astype(BF16), tail]) for d in (1, 2, 3)]
        return [mine[0]] + far + [sums]

    def backward_named(here, sums, parts, gathered):
        return list(combine(lists, counts, here, sums, parts))

    *outs, sums = lax.cond(full, backward_all, backward_named, here, sums, parts, gathered)
    outs = ring_swap(outs, along_inner)
    grad_features, grad_weight, grad_offset = finish(outs, sums, scaling)
    return (hidden, grad_features, grad_weight, grad_offset.reshape(-1))


def solution(mesh):
    in_specs = (
        P(("col", "row"), None),
        P(),
        P(),
        P("row", "col", None, None, None),
        P("row", "col", None),
        P("row", "col", None),
        P("row", "col"),
        P(("row", "col"), None),
    )
    out_specs = (P(("row", "col"), None), P(("col", "row"), None), P(), P())
    return jax.shard_map(
        on_device, mesh=mesh, in_specs=in_specs, out_specs=out_specs, check_vma=False
    )
```

```python
import functools
import itertools
import math

import jax
import jax.numpy as jnp
from jax import lax
from jax.experimental import pallas as pl
from jax.experimental.pallas import tpu as pltpu
from jax.sharding import PartitionSpec as P

T = 128
F32, BF16, I32 = jnp.float32, jnp.bfloat16, jnp.int32
MIB = 1024 * 1024
GROUP = 16
META = 16
CAP = 26
LANES = 32
SMEM = pl.BlockSpec(memory_space=pltpu.SMEM)
VMEM = pl.BlockSpec(memory_space=pltpu.VMEM)
ANY = pl.BlockSpec(memory_space=pl.ANY)


def room(mib):
    return pltpu.CompilerParams(vmem_limit_bytes=mib * MIB)


def along_xz(value, to, x_core):
    pairs = []
    for x, z, y, core in itertools.product(range(4), range(4), range(4), range(2)):
        far = (to(x) % 4, z) if core == x_core else (x, to(z) % 4)
        pairs.append(((x * 4 + z) * 8 + y * 2 + core, (far[0] * 4 + far[1]) * 8 + y * 2 + core))
    return lax.ppermute(value, ("row", "col"), pairs)


def along_inner(value, to):
    return along_xz(value, to, 0)


def along_outer(value, to):
    return along_xz(value, to, 1)


def along_y(value, to):
    pairs = []
    for y in range(4):
        pairs.append((y * 2, to(y) % 4 * 2))
        pairs.append((y * 2 + 1, (2 * y - to(y)) % 4 * 2 + 1))
    return lax.ppermute(value, "col", pairs)


def other_core(value):
    pairs = [(y * 2 + k, y * 2 + 1 - k) for y in range(4) for k in range(2)]
    return lax.ppermute(value, "col", pairs)


def ahead(step):
    return lambda at: at + step


def ring_gather(value, along):
    across, after, before = [along(value, ahead(step)) for step in (2, -1, 1)]
    return [value, after, across, before]


def ring_swap(pieces, along):
    across = along(pieces[2], ahead(2))
    return [pieces[0], along(pieces[3], ahead(-1)), across, along(pieces[1], ahead(1))]


def total_of(pieces):
    return sum(piece.astype(F32) for piece in pieces)


def block(place):
    return pl.ds(pl.multiple_of(place * T, T), T)


def prepare_kernel(at_row, at_col, live_ref, rows_ref, cols_ref, meta, tables):
    live = live_ref[0]
    x, z = at_row[0] >> 2, at_row[0] & 3
    y, core = at_col[0] >> 1, at_col[0] & 1
    rows, cols = rows_ref[...], cols_ref[...]
    slots = cols.shape[1]

    far_core = (rows >> 4) & 1
    same_core = jnp.where(far_core == core, 64, 0)
    dy = (rows >> 5) - y
    dy = jnp.where(far_core == 0, dy, -dy) & 3
    row_place = same_core + ((rows >> 3) & 1) * 32 + dy * 8 + (rows & 7)
    dx, dz = ((cols >> 6) - x) & 3, ((cols >> 4) - z) & 3
    outer, inner = jnp.where(core == 0, dz, dx), jnp.where(core == 0, dx, dz)
    code = inner * 16 + (cols & 15)
    dense_place = outer * 64 + code

    t = lax.broadcasted_iota(I32, (slots, slots), 0)
    s = lax.broadcasted_iota(I32, (slots, slots), 1)
    lane = lax.broadcasted_iota(I32, (slots, T), 1).astype(F32)

    def column(row):
        return jnp.sum(jnp.where(t == s, row, 0.0), axis=1, keepdims=True)

    def count(mask, value=1.0):
        return jnp.sum(jnp.where(mask, value, 0.0), axis=0, keepdims=True)

    valid = lax.broadcasted_iota(I32, (1, slots), 1) < live
    cols_f, outer_f = cols.astype(F32), outer.astype(F32)
    same = column(cols_f) == cols_f
    first = valid & (count(same & (t < s)) == 0.0)
    first_c = column(jnp.where(first, 1.0, 0.0)) > 0.0
    outer_c = column(outer_f)
    rank = count((t < s) & first_c & (outer_c == outer_f))
    over = jnp.where(first & (outer != 0) & (rank >= CAP), 1.0, 0.0)
    over = jnp.max(over, axis=1, keepdims=True)
    far = (64 + (outer - 1) * CAP).astype(F32) + jnp.minimum(rank, CAP - 1.0)
    place = jnp.where(outer == 0, code.astype(F32), far)
    place = count(same & first_c, column(place))
    place = jnp.where(valid, place, 0.0).astype(I32)
    second = (rows >> 3) & 1
    source = (1 - second) * 64 + ((row_place & 64) >> 1) + (row_place & 31)
    pad = jnp.zeros((4, slots), I32)
    tables[...] = jnp.concatenate([row_place, place, dense_place, source, pad], axis=0)

    key = column(jnp.where(first & (rank < CAP), outer_f * LANES + rank, -1.0))
    wanted = count(key == lane, column(code.astype(F32)))
    amounts = jnp.minimum(count((outer_c == lane) & first_c), 1.0 * CAP)
    line = lax.broadcasted_iota(I32, (META, T), 0)
    lines = [wanted, amounts, jnp.broadcast_to(over, (1, T)), jnp.zeros((META - 3, T), F32)]
    meta[...] = jnp.concatenate(lines, axis=0).astype(BF16)


def prepare(at_row, at_col, live, rows, cols):
    slots = cols.shape[-1]
    return pl.pallas_call(
        prepare_kernel,
        out_shape=[
            jax.ShapeDtypeStruct((META, T), BF16),
            jax.ShapeDtypeStruct((8, slots), I32),
        ],
        in_specs=[SMEM] * 3 + [VMEM] * 2,
        out_specs=[VMEM] * 2,
        compiler_params=room(4),
    )(at_row, at_col, live, rows.reshape(1, slots), cols.reshape(1, slots))


def products_kernel(
    live, tables, tiles_ref, *refs, spans, outs, contract, in_row, out_row, tailed
):
    n = len(spans)
    sources, out_refs, (tiles, held, total, tails, sems) = refs[:n], refs[n:-5], refs[-5:]
    copies = [pltpu.make_async_copy(tiles_ref, tiles, sems.at[n])]
    start = 0
    for k, (ref, rows) in enumerate(zip(sources, spans)):
        copies.append(
            pltpu.make_async_copy(
                ref.at[pl.ds(0, rows)], held.at[pl.ds(start, rows)], sems.at[k]
            )
        )
        start += rows
    for k in range(tailed):
        tail = sources[k].at[pl.ds(spans[k], tails.shape[1])]
        copies.append(pltpu.make_async_copy(tail, tails.at[k], sems.at[n + 1 + k]))
    for copy in copies:
        copy.start()

    zeros = jnp.zeros((4, T, T), F32)

    def clear(k, carry):
        total[pl.ds(k * 4, 4)] = zeros
        return carry

    lax.fori_loop(0, total.shape[0] // 4, clear, 0)
    for copy in copies:
        copy.wait()
    if tailed:
        summed = jnp.sum(tails[...].astype(F32), axis=0)
        lines = summed.shape[0] // 2
        out_refs[-1][:, :T] = summed[:lines]
        out_refs[-1][:, T:] = summed[lines:]
        for ref, blocks in zip(out_refs[1:-1], outs[1:]):
            ref[pl.ds(blocks * T, 2 * lines)] = summed.astype(BF16)

    def group(number, carry):
        products = []
        for k in range(GROUP):
            slot = number * GROUP + k
            product = lax.dot_general(
                tiles[slot],
                held[block(tables[in_row, slot])],
                ((contract, (0,)), ((), ())),
                preferred_element_type=F32,
            )
            products.append(jnp.where(slot < live[0], product, 0.0))
        for k, product in enumerate(products):
            total[tables[out_row, number * GROUP + k]] += product
        return carry

    lax.fori_loop(0, (live[0] + GROUP - 1) // GROUP, group, 0)
    start = 0
    for ref, blocks in zip(out_refs, outs):

        def out(k, carry, ref=ref, start=start):
            for at in range(2):
                ref[block(k * 2 + at)] = total[start + k * 2 + at].astype(BF16)
            return carry

        lax.fori_loop(0, blocks // 2, out, 0)
        start += blocks


def products(live, tables, in_row, out_row, tiles, sources, spans, outs, contract, tailed=0):
    lines = sources[0].shape[0] - spans[0] if tailed else 16
    kernel = functools.partial(
        products_kernel,
        spans=spans,
        outs=outs,
        contract=contract,
        in_row=in_row,
        out_row=out_row,
        tailed=tailed,
    )
    need = tiles.size * 2 + sum(spans) * T * 2 + sum(outs) * T * T * 6
    extra = [lines if tailed and n else 0 for n in range(len(outs))]
    return pl.pallas_call(
        kernel,
        out_shape=[jax.ShapeDtypeStruct((n * T + e, T), BF16) for n, e in zip(outs, extra)]
        + ([jax.ShapeDtypeStruct((lines // 2, 2 * T), F32)] if tailed else []),
        in_specs=[SMEM] * 2 + [ANY] * (1 + len(sources)),
        out_specs=[VMEM] * (len(outs) + (tailed > 0)),
        scratch_shapes=[
            pltpu.VMEM(tiles.shape, BF16),
            pltpu.VMEM((sum(spans), T), BF16),
            pltpu.VMEM((sum(outs), T, T), F32),
            pltpu.VMEM((max(tailed, 1), lines, T), BF16),
            pltpu.SemaphoreType.DMA((len(spans) + 1 + tailed,)),
        ],
        compiler_params=room(need // MIB + 5),
    )(live, tables, tiles, *sources)


def pack_kernel(*refs):
    pieces, metas, sends, (said, lists, counts), (held, heard, words, table, sems) = (
        refs[:4],
        refs[4:8],
        refs[8:11],
        refs[11:14],
        refs[14:],
    )
    fetches = [pltpu.make_async_copy(p, heard.at[k], sems.at[k + 4]) for k, p in enumerate(metas)]
    copies = [pltpu.make_async_copy(p, held.at[k], sems.at[k]) for k, p in enumerate(pieces)]
    for copy in fetches + copies:
        copy.start()
    for copy in fetches:
        copy.wait()
    told = [heard[k].astype(F32)[:8] for k in range(4)]
    for n in range(3):
        words[pl.ds(n * 8, 8)] = told[n + 1].astype(I32)
    fetch = pltpu.make_async_copy(words, table, sems.at[8])
    fetch.start()
    over = functools.reduce(jnp.maximum, told)[2:3]
    said[...] = jnp.broadcast_to(over, (8, T))
    fetch.wait()
    for copy in copies:
        copy.wait()
    for n in range(3):
        group = 3 - n
        amount = table[n * 8 + 1, group]
        counts[n] = amount
        for k in range(4):
            lists[n * LANES + amount + k] = 64

        def step(k, carry, n=n, group=group):
            code = table[n * 8, group * LANES + k]
            lists[n * LANES + k] = code
            sends[n][block(k)] = held[code >> 4, block(code & 15)]
            return carry

        lax.fori_loop(0, amount, step, 0)


def pack(pieces, metas):
    return pl.pallas_call(
        pack_kernel,
        out_shape=[jax.ShapeDtypeStruct((CAP * T, T), BF16)] * 3
        + [jax.ShapeDtypeStruct((8, T), F32)]
        + [jax.ShapeDtypeStruct((3 * LANES,), I32), jax.ShapeDtypeStruct((3,), I32)],
        in_specs=[ANY] * 8,
        out_specs=[VMEM] * 4 + [SMEM] * 2,
        scratch_shapes=[
            pltpu.VMEM((4,) + pieces[0].shape, BF16),
            pltpu.VMEM((4, META, T), BF16),
            pltpu.VMEM((24, T), I32),
            pltpu.SMEM((24, T), I32),
            pltpu.SemaphoreType.DMA((9,)),
        ],
        compiler_params=room(10),
    )(*pieces, *metas)


def combine_kernel(lists, counts, own_ref, sums, *refs):
    part_refs, outs, summed, (own, parts, total, sems) = refs[:3], refs[3:7], refs[7], refs[8:]
    copies = [pltpu.make_async_copy(own_ref, own, sems.at[3])]
    for n, ref in enumerate(part_refs):
        copies.append(pltpu.make_async_copy(ref, parts.at[n], sems.at[n]))
    for copy in copies:
        copy.start()
    copies[0].wait()

    def widen(k, carry):
        for at in range(4):
            total[k * 4 + at] = own[block(k * 4 + at)].astype(F32)
        return carry

    lax.fori_loop(0, 16, widen, 0)
    for copy in copies[1:]:
        copy.wait()
    lines = sums.shape[0]
    for k in range(2):
        tail = pl.ds(CAP * T + k * lines, lines)
        line = sums[:, k * T : (k + 1) * T] + total_of([parts[n, tail] for n in range(3)])
        summed[:, k * T : (k + 1) * T] = line
        for ref in outs[1:]:
            ref[pl.ds(16 * T + k * lines, lines)] = line.astype(BF16)
    for n in range(3):

        def add(k, carry, n=n):
            for at in range(4):
                slot = k * 4 + at
                total[lists[n * LANES + slot]] += parts[n, block(slot)].astype(F32)
            return carry

        lax.fori_loop(0, (counts[n] + 3) // 4, add, 0)
    for n, ref in enumerate(outs):

        def out(k, carry, n=n, ref=ref):
            for at in range(4):
                ref[block(k * 4 + at)] = total[n * 16 + k * 4 + at].astype(ref.dtype)
            return carry

        lax.fori_loop(0, 4, out, 0)


def combine(lists, counts, own, sums, parts):
    rows = 16 * T
    return pl.pallas_call(
        combine_kernel,
        out_shape=[jax.ShapeDtypeStruct((rows, T), F32)]
        + [jax.ShapeDtypeStruct((rows + 2 * sums.shape[0], T), BF16)] * 3
        + [jax.ShapeDtypeStruct(sums.shape, F32)],
        in_specs=[SMEM] * 2 + [ANY, VMEM] + [ANY] * 3,
        out_specs=[VMEM] * 5,
        scratch_shapes=[
            pltpu.VMEM(own.shape, BF16),
            pltpu.VMEM((3,) + parts[0].shape, BF16),
            pltpu.VMEM((65, T, T), F32),
            pltpu.SemaphoreType.DMA((4,)),
        ],
        compiler_params=room(16),
    )(lists, counts, own, sums, *parts)


def finish_kernel(*refs, scaling):
    pieces, sums, (nodes, weight, offset) = refs[:4], refs[4], refs[5:]
    rows = nodes.shape[0]
    nodes[...] = total_of([ref[pl.ds(0, rows)] for ref in pieces])
    lines = sums.shape[0]
    for k in range(2):
        part = pl.ds(k * T, T)
        total = sums[:, part]
        for ref in pieces[1:]:
            total = total + ref[pl.ds(rows + k * lines, lines)].astype(F32)
        total = total * scaling
        weight[:, part] = total[:T]
        offset[:, part] = jnp.sum(total[T:], axis=0, keepdims=True)


def finish(pieces, sums, scaling):
    width = sums.shape[-1]
    return pl.pallas_call(
        functools.partial(finish_kernel, scaling=scaling),
        out_shape=[
            jax.ShapeDtypeStruct(pieces[0].shape, F32),
            jax.ShapeDtypeStruct((T, width), F32),
            jax.ShapeDtypeStruct((1, width), F32),
        ],
        in_specs=[VMEM] * 5,
        out_specs=[VMEM] * 3,
        compiler_params=room(10),
    )(*pieces, sums)


def dense_kernel(*refs, step):
    parts, (grad, weight, offset), rest = refs[:5], refs[5:8], refs[8:]
    hidden, projected, sums = rest[-3:]
    second = len(rest) > 3

    @pl.when(pl.program_id(0) == 0)
    def _():
        sums[...] = rest[1][...] if second else jnp.zeros_like(sums)

    mixed = total_of([ref[...] for ref in parts])
    high = mixed.astype(BF16)
    low = (mixed - high.astype(F32)).astype(BF16)
    w = weight[...]
    pre = jnp.dot(high, w, preferred_element_type=F32)
    pre = pre + jnp.dot(low, w, preferred_element_type=F32) + offset[...]
    s = jax.nn.sigmoid(pre)
    hidden[...] = (pre * s).astype(BF16)
    slope = (grad[...].astype(F32) * s * (1.0 + pre * (1.0 - s))).astype(BF16)
    projected[pl.ds(pl.multiple_of(pl.program_id(0) * step, step), step)] = lax.dot_general(
        slope, w, (((1,), (1,)), ((), ())), preferred_element_type=F32
    ).astype(BF16)
    over_rows = (((0,), (0,)), ((), ()))
    sums[:T] += lax.dot_general(
        high, slope, over_rows, preferred_element_type=F32
    ) + lax.dot_general(low, slope, over_rows, preferred_element_type=F32)
    sums[T:] += jnp.sum(slope.astype(F32).reshape(-1, 8, slope.shape[1]), axis=0)

    @pl.when((pl.program_id(0) == pl.num_programs(0) - 1) & second)
    def _():
        lines = sums.shape[0]
        for k in range(2 if second else 0):
            part = sums[:, k * T : (k + 1) * T].astype(BF16)
            projected[pl.ds(projected.shape[0] - (2 - k) * lines, lines)] = part


def dense(parts, grad, weight, offset, part, before):
    width, rows = weight.shape[1], grad.shape[0]
    step = 512
    steps = rows // 2 // step
    shift = part * steps
    tail = 2 * (T + 8) if before else 0
    half = pl.BlockSpec((step, T), lambda i: (i, 0))
    full = pl.BlockSpec((step, width), lambda i: (i + shift, 0))

    def whole(*shape):
        return pl.BlockSpec(shape, lambda i: (0, 0))

    return pl.pallas_call(
        functools.partial(dense_kernel, step=step),
        grid=(steps,),
        out_shape=[
            jax.ShapeDtypeStruct((rows, width), BF16),
            jax.ShapeDtypeStruct((rows // 2 + tail, T), BF16),
            jax.ShapeDtypeStruct((T + 8, width), F32),
        ],
        in_specs=[half] * 5
        + [full, whole(T, width), whole(1, width)]
        + ([ANY, whole(T + 8, width), ANY] if before else []),
        out_specs=[full, whole(rows // 2 + tail, T), whole(T + 8, width)],
        input_output_aliases={8: 0} if before else {},
        compiler_params=room(14),
    )(*parts, grad, weight, offset, *before)


def on_device(features, weight, offset, tile_values, tile_rows, tile_cols, live_tiles, grad_hidden):
    tiles = tile_values.reshape(tile_values.shape[2:])
    nodes_here = features.shape[0]
    scaling = 1.0 / math.sqrt(nodes_here * lax.axis_size("row") * lax.axis_size("col"))
    at_row, at_col = lax.axis_index("row"), lax.axis_index("col")
    live = live_tiles.reshape(1)
    meta, tables = prepare(at_row.reshape(1), at_col.reshape(1), live, tile_rows, tile_cols)

    pieces = ring_gather(features, along_inner)
    *sends, said, lists, counts = pack(pieces, ring_gather(meta, along_outer))
    named = ring_swap([None] + sends, along_outer)[1:]
    full = functools.reduce(jnp.maximum, ring_gather(said, along_inner))[0, 0] > 0.5

    def forward_all(outs, pieces):
        whole = ring_gather(jnp.concatenate(pieces), along_outer)
        spans = (4 * nodes_here,) * 4
        return products(live, tables, 2, 0, tiles, whole, spans, (32,) * 4, (1,))

    spans = (nodes_here,) * 4 + (CAP * T,) * 3
    outs = products(live, tables, 1, 0, tiles, pieces + named, spans, (32,) * 4, (1,))
    outs = lax.cond(full, forward_all, lambda outs, pieces: outs, outs, pieces)

    part_rows = nodes_here // 2
    halves = []
    for send, keep in zip(outs[:2], outs[2:]):
        got = other_core(send)
        far = []
        for d in (1, 2, 3):
            at = slice(d * part_rows, (d + 1) * part_rows)
            far.append((keep[at].astype(F32) + got[at].astype(F32)).astype(BF16))
        halves.append([keep, got] + ring_swap([None] + far, along_y)[1:])
    before, own, others = (), [], []
    for part, parts in enumerate(halves):
        hidden, projected, sums = dense(
            parts, grad_hidden, weight, offset.reshape(1, -1), part, before
        )
        here = ring_gather(projected, along_y)
        own.append(here)
        others.append([other_core(piece) for piece in here])
        before = (hidden, sums, others[0][0])

    gathered = others[1] + own[1] + others[0] + own[0]
    spans, outs = (part_rows,) * 16, (64,) + (CAP,) * 3
    here, *parts, sums = products(
        live, tables, 3, 1, tiles, gathered, spans, outs, (0,), tailed=8
    )
    parts = ring_swap([None] + parts, along_outer)[1:]

    def backward_all(outs, gathered):
        mine = products(live, tables, 3, 2, tiles, gathered, spans, (64,) * 4, (0,))
        mine = total_of(ring_swap(mine, along_outer)).reshape(4, nodes_here, T)
        far = [outs[d].at[:nodes_here].set(mine[d].astype(BF16)) for d in (1, 2, 3)]
        return [mine[0]] + far

    *outs, sums = combine(lists, counts, here, sums, parts)
    outs = lax.cond(full, backward_all, lambda outs, gathered: outs, outs, gathered)
    outs = ring_swap(outs, along_inner)
    grad_features, grad_weight, grad_offset = finish(outs, sums, scaling)
    return (hidden, grad_features, grad_weight, grad_offset.reshape(-1))


def solution(mesh):
    in_specs = (
        P(("col", "row"), None),
        P(),
        P(),
        P("row", "col", None, None, None),
        P("row", "col", None),
        P("row", "col", None),
        P("row", "col"),
        P(("row", "col"), None),
    )
    out_specs = (P(("row", "col"), None), P(("col", "row"), None), P(), P())
    return jax.shard_map(
        on_device, mesh=mesh, in_specs=in_specs, out_specs=out_specs, check_vma=False
    )
```

```python
import functools
import itertools
import math

import jax
import jax.numpy as jnp
from jax import lax
from jax.experimental import pallas as pl
from jax.experimental.pallas import tpu as pltpu
from jax.sharding import PartitionSpec as P

T = 128
F32, BF16, I32 = jnp.float32, jnp.bfloat16, jnp.int32
MIB = 1024 * 1024
GROUP = 16
META = 16
CAP = 26
LANES = 32
SMEM = pl.BlockSpec(memory_space=pltpu.SMEM)
VMEM = pl.BlockSpec(memory_space=pltpu.VMEM)
ANY = pl.BlockSpec(memory_space=pl.ANY)


def room(mib):
    return pltpu.CompilerParams(vmem_limit_bytes=mib * MIB)


def along_xz(value, to, x_core):
    pairs = []
    for x, z, y, core in itertools.product(range(4), range(4), range(4), range(2)):
        far = (to(x) % 4, z) if core == x_core else (x, to(z) % 4)
        pairs.append(((x * 4 + z) * 8 + y * 2 + core, (far[0] * 4 + far[1]) * 8 + y * 2 + core))
    return lax.ppermute(value, ("row", "col"), pairs)


def along_inner(value, to):
    return along_xz(value, to, 0)


def along_outer(value, to):
    return along_xz(value, to, 1)


def along_y(value, to):
    pairs = []
    for y in range(4):
        pairs.append((y * 2, to(y) % 4 * 2))
        pairs.append((y * 2 + 1, (2 * y - to(y)) % 4 * 2 + 1))
    return lax.ppermute(value, "col", pairs)


def other_core(value):
    pairs = [(y * 2 + k, y * 2 + 1 - k) for y in range(4) for k in range(2)]
    return lax.ppermute(value, "col", pairs)


def ahead(step):
    return lambda at: at + step


def ring_gather(value, along):
    across, after, before = [along(value, ahead(step)) for step in (2, -1, 1)]
    return [value, after, across, before]


def ring_swap(pieces, along):
    after, before = along(pieces[3], ahead(-1)), along(pieces[1], ahead(1))
    return [pieces[0], after, along(pieces[2], ahead(2)), before]


def total_of(pieces):
    return sum(piece.astype(F32) for piece in pieces)


def block(place):
    return pl.ds(pl.multiple_of(place * T, T), T)


def prepare_kernel(at_row, at_col, live_ref, rows_ref, cols_ref, meta, tables, slots_held, sems):
    copies = [
        pltpu.make_async_copy(ref, slots_held.at[k], sems.at[k])
        for k, ref in enumerate((rows_ref, cols_ref))
    ]
    for copy in copies:
        copy.start()
    for copy in copies:
        copy.wait()
    live = live_ref[0]
    x, z = at_row[0] >> 2, at_row[0] & 3
    y, core = at_col[0] >> 1, at_col[0] & 1
    rows, cols = slots_held[0], slots_held[1]
    slots = cols.shape[1]

    far_core = (rows >> 4) & 1
    same_core = jnp.where(far_core == core, 64, 0)
    dy = (rows >> 5) - y
    dy = jnp.where(far_core == 0, dy, -dy) & 3
    row_place = same_core + ((rows >> 3) & 1) * 32 + dy * 8 + (rows & 7)
    dx, dz = ((cols >> 6) - x) & 3, ((cols >> 4) - z) & 3
    outer, inner = jnp.where(core == 0, dz, dx), jnp.where(core == 0, dx, dz)
    code = inner * 16 + (cols & 15)
    dense_place = outer * 64 + code

    t = lax.broadcasted_iota(I32, (slots, slots), 0)
    s = lax.broadcasted_iota(I32, (slots, slots), 1)
    lane = lax.broadcasted_iota(I32, (slots, T), 1).astype(F32)

    def column(row):
        return jnp.sum(jnp.where(t == s, row, 0.0), axis=1, keepdims=True)

    def count(mask, value=1.0):
        return jnp.sum(jnp.where(mask, value, 0.0), axis=0, keepdims=True)

    valid = lax.broadcasted_iota(I32, (1, slots), 1) < live
    cols_f, outer_f = cols.astype(F32), outer.astype(F32)
    same = column(cols_f) == cols_f
    first = valid & (count(same & (t < s)) == 0.0)
    first_c = column(jnp.where(first, 1.0, 0.0)) > 0.0
    outer_c = column(outer_f)
    rank = count((t < s) & first_c & (outer_c == outer_f))
    over = jnp.where(first & (outer != 0) & (rank >= CAP), 1.0, 0.0)
    over = jnp.max(over, axis=1, keepdims=True)
    far = (64 + (outer - 1) * CAP).astype(F32) + jnp.minimum(rank, CAP - 1.0)
    place = jnp.where(outer == 0, code.astype(F32), far)
    place = count(same & first_c, column(place))
    place = jnp.where(valid, place, 0.0).astype(I32)
    second = (rows >> 3) & 1
    source = (1 - second) * 64 + ((row_place & 64) >> 1) + (row_place & 31)
    pad = jnp.zeros((4, slots), I32)
    tables[...] = jnp.concatenate([row_place, place, dense_place, source, pad], axis=0)

    key = column(jnp.where(first & (rank < CAP), outer_f * LANES + rank, -1.0))
    wanted = count(key == lane, column(code.astype(F32)))
    amounts = jnp.minimum(count((outer_c == lane) & first_c), 1.0 * CAP)
    line = lax.broadcasted_iota(I32, (META, T), 0)
    lines = [wanted, amounts, jnp.broadcast_to(over, (1, T)), jnp.zeros((META - 3, T), F32)]
    meta[...] = jnp.concatenate(lines, axis=0).astype(BF16)


def prepare(at_row, at_col, live, rows, cols):
    slots = cols.shape[-1]
    return pl.pallas_call(
        prepare_kernel,
        out_shape=[
            jax.ShapeDtypeStruct((META, T), BF16),
            jax.ShapeDtypeStruct((8, slots), I32),
        ],
        in_specs=[SMEM] * 3 + [ANY] * 2,
        out_specs=[VMEM] * 2,
        scratch_shapes=[pltpu.VMEM((2, 1, slots), I32), pltpu.SemaphoreType.DMA((2,))],
        compiler_params=room(4),
    )(at_row, at_col, live, rows.reshape(1, slots), cols.reshape(1, slots))


def products_kernel(
    live, tables, tiles_ref, *refs, spans, outs, contract, in_row, out_row, tailed
):
    n = len(spans)
    sources, out_refs, (tiles, held, total, tails, sems) = refs[:n], refs[n:-5], refs[-5:]
    copies = [pltpu.make_async_copy(tiles_ref, tiles, sems.at[n])]
    start = 0
    for k, (ref, rows) in enumerate(zip(sources, spans)):
        copies.append(
            pltpu.make_async_copy(
                ref.at[pl.ds(0, rows)], held.at[pl.ds(start, rows)], sems.at[k]
            )
        )
        start += rows
    for k in range(tailed):
        tail = sources[k].at[pl.ds(spans[k], tails.shape[1])]
        copies.append(pltpu.make_async_copy(tail, tails.at[k], sems.at[n + 1 + k]))
    for copy in copies:
        copy.start()

    zeros = jnp.zeros((4, T, T), F32)

    def clear(k, carry):
        total[pl.ds(k * 4, 4)] = zeros
        return carry

    lax.fori_loop(0, total.shape[0] // 4, clear, 0)
    for copy in copies:
        copy.wait()
    if tailed:
        summed = jnp.sum(tails[...].astype(F32), axis=0)
        lines = summed.shape[0] // 2
        out_refs[-1][:, :T] = summed[:lines]
        out_refs[-1][:, T:] = summed[lines:]
        for ref, blocks in zip(out_refs[1:-1], outs[1:]):
            ref[pl.ds(blocks * T, 2 * lines)] = summed.astype(BF16)

    def group(number, carry):
        products = []
        for k in range(GROUP):
            slot = number * GROUP + k
            product = lax.dot_general(
                tiles[slot],
                held[block(tables[in_row, slot])],
                ((contract, (0,)), ((), ())),
                preferred_element_type=F32,
            )
            products.append(jnp.where(slot < live[0], product, 0.0))
        for k, product in enumerate(products):
            total[tables[out_row, number * GROUP + k]] += product
        return carry

    lax.fori_loop(0, (live[0] + GROUP - 1) // GROUP, group, 0)
    start = 0
    for ref, blocks in zip(out_refs, outs):

        def out(k, carry, ref=ref, start=start):
            for at in range(2):
                ref[block(k * 2 + at)] = total[start + k * 2 + at].astype(BF16)
            return carry

        lax.fori_loop(0, blocks // 2, out, 0)
        start += blocks


def products(live, tables, in_row, out_row, tiles, sources, spans, outs, contract, tailed=0):
    lines = sources[0].shape[0] - spans[0] if tailed else 16
    kernel = functools.partial(
        products_kernel,
        spans=spans,
        outs=outs,
        contract=contract,
        in_row=in_row,
        out_row=out_row,
        tailed=tailed,
    )
    need = tiles.size * 2 + sum(spans) * T * 2 + sum(outs) * T * T * 6
    extra = [lines if tailed and n else 0 for n in range(len(outs))]
    return pl.pallas_call(
        kernel,
        out_shape=[jax.ShapeDtypeStruct((n * T + e, T), BF16) for n, e in zip(outs, extra)]
        + ([jax.ShapeDtypeStruct((lines // 2, 2 * T), F32)] if tailed else []),
        in_specs=[SMEM] * 2 + [ANY] * (1 + len(sources)),
        out_specs=[VMEM] * (len(outs) + (tailed > 0)),
        scratch_shapes=[
            pltpu.VMEM(tiles.shape, BF16),
            pltpu.VMEM((sum(spans), T), BF16),
            pltpu.VMEM((sum(outs), T, T), F32),
            pltpu.VMEM((max(tailed, 1), lines, T), BF16),
            pltpu.SemaphoreType.DMA((len(spans) + 1 + tailed,)),
        ],
        compiler_params=room(need // MIB + 5),
    )(live, tables, tiles, *sources)


def pack_kernel(*refs):
    pieces, metas, sends, (said, lists, counts), (held, heard, words, table, sems) = (
        refs[:4],
        refs[4:8],
        refs[8:11],
        refs[11:14],
        refs[14:],
    )
    fetches = [pltpu.make_async_copy(p, heard.at[k], sems.at[k + 4]) for k, p in enumerate(metas)]
    copies = [pltpu.make_async_copy(p, held.at[k], sems.at[k]) for k, p in enumerate(pieces)]
    for copy in fetches + copies:
        copy.start()
    for copy in fetches:
        copy.wait()
    told = [heard[k].astype(F32)[:8] for k in range(4)]
    for n in range(3):
        words[pl.ds(n * 8, 8)] = told[n + 1].astype(I32)
    fetch = pltpu.make_async_copy(words, table, sems.at[8])
    fetch.start()
    over = functools.reduce(jnp.maximum, told)[2:3]
    said[...] = jnp.broadcast_to(over, (8, T))
    fetch.wait()
    for copy in copies:
        copy.wait()
    for n in range(3):
        group = 3 - n
        amount = table[n * 8 + 1, group]
        counts[n] = amount
        for k in range(4):
            lists[n * LANES + amount + k] = 64

        def step(k, carry, n=n, group=group):
            code = table[n * 8, group * LANES + k]
            lists[n * LANES + k] = code
            sends[n][block(k)] = held[code >> 4, block(code & 15)]
            return carry

        lax.fori_loop(0, amount, step, 0)


def pack(pieces, metas):
    return pl.pallas_call(
        pack_kernel,
        out_shape=[jax.ShapeDtypeStruct((CAP * T, T), BF16)] * 3
        + [jax.ShapeDtypeStruct((8, T), F32)]
        + [jax.ShapeDtypeStruct((3 * LANES,), I32), jax.ShapeDtypeStruct((3,), I32)],
        in_specs=[ANY] * 8,
        out_specs=[VMEM] * 4 + [SMEM] * 2,
        scratch_shapes=[
            pltpu.VMEM((4,) + pieces[0].shape, BF16),
            pltpu.VMEM((4, META, T), BF16),
            pltpu.VMEM((24, T), I32),
            pltpu.SMEM((24, T), I32),
            pltpu.SemaphoreType.DMA((9,)),
        ],
        compiler_params=room(10),
    )(*pieces, *metas)


def combine_kernel(lists, counts, own, sums, *refs):
    parts, outs, summed, total = refs[:3], refs[3:7], refs[7], refs[8]

    def widen(k, carry):
        for at in range(4):
            total[k * 4 + at] = own[block(k * 4 + at)].astype(F32)
        return carry

    lax.fori_loop(0, 16, widen, 0)
    lines = sums.shape[0]
    for k in range(2):
        tail = pl.ds(CAP * T + k * lines, lines)
        line = sums[:, k * T : (k + 1) * T] + total_of([part[tail] for part in parts])
        summed[:, k * T : (k + 1) * T] = line
        for ref in outs[1:]:
            ref[pl.ds(16 * T + k * lines, lines)] = line.astype(BF16)
    for n in range(3):

        def add(k, carry, n=n):
            for at in range(4):
                slot = k * 4 + at
                total[lists[n * LANES + slot]] += parts[n][block(slot)].astype(F32)
            return carry

        lax.fori_loop(0, (counts[n] + 3) // 4, add, 0)
    for n, ref in enumerate(outs):

        def out(k, carry, n=n, ref=ref):
            for at in range(4):
                ref[block(k * 4 + at)] = total[n * 16 + k * 4 + at].astype(ref.dtype)
            return carry

        lax.fori_loop(0, 4, out, 0)


def combine(lists, counts, own, sums, parts):
    rows = 16 * T
    return pl.pallas_call(
        combine_kernel,
        out_shape=[jax.ShapeDtypeStruct((rows, T), F32)]
        + [jax.ShapeDtypeStruct((rows + 2 * sums.shape[0], T), BF16)] * 3
        + [jax.ShapeDtypeStruct(sums.shape, F32)],
        in_specs=[SMEM] * 2 + [VMEM] * 5,
        out_specs=[VMEM] * 5,
        scratch_shapes=[pltpu.VMEM((65, T, T), F32)],
        compiler_params=room(16),
    )(lists, counts, own, sums, *parts)


def finish_kernel(*refs, scaling):
    pieces, sums, (nodes, weight, offset) = refs[:4], refs[4], refs[5:]
    rows = nodes.shape[0]
    nodes[...] = total_of([ref[pl.ds(0, rows)] for ref in pieces])
    lines = sums.shape[0]
    for k in range(2):
        part = pl.ds(k * T, T)
        total = sums[:, part]
        for ref in pieces[1:]:
            total = total + ref[pl.ds(rows + k * lines, lines)].astype(F32)
        total = total * scaling
        weight[:, part] = total[:T]
        offset[:, part] = jnp.sum(total[T:], axis=0, keepdims=True)


def finish(pieces, sums, scaling):
    width = sums.shape[-1]
    return pl.pallas_call(
        functools.partial(finish_kernel, scaling=scaling),
        out_shape=[
            jax.ShapeDtypeStruct(pieces[0].shape, F32),
            jax.ShapeDtypeStruct((T, width), F32),
            jax.ShapeDtypeStruct((1, width), F32),
        ],
        in_specs=[VMEM] * 5,
        out_specs=[VMEM] * 3,
        compiler_params=room(10),
    )(*pieces, sums)


def dense_kernel(*refs, step):
    parts, (grad, weight, offset), rest = refs[:5], refs[5:8], refs[8:]
    hidden, projected, sums = rest[-3:]
    second = len(rest) > 3

    @pl.when(pl.program_id(0) == 0)
    def _():
        sums[...] = rest[1][...] if second else jnp.zeros_like(sums)

    mixed = total_of([ref[...] for ref in parts])
    high = mixed.astype(BF16)
    low = (mixed - high.astype(F32)).astype(BF16)
    w = weight[...]
    pre = jnp.dot(high, w, preferred_element_type=F32)
    pre = pre + jnp.dot(low, w, preferred_element_type=F32) + offset[...]
    s = jax.nn.sigmoid(pre)
    hidden[...] = (pre * s).astype(BF16)
    slope = (grad[...].astype(F32) * s * (1.0 + pre * (1.0 - s))).astype(BF16)
    projected[pl.ds(pl.multiple_of(pl.program_id(0) * step, step), step)] = lax.dot_general(
        slope, w, (((1,), (1,)), ((), ())), preferred_element_type=F32
    ).astype(BF16)
    over_rows = (((0,), (0,)), ((), ()))
    sums[:T] += lax.dot_general(
        high, slope, over_rows, preferred_element_type=F32
    ) + lax.dot_general(low, slope, over_rows, preferred_element_type=F32)
    sums[T:] += jnp.sum(slope.astype(F32).reshape(-1, 8, slope.shape[1]), axis=0)

    @pl.when((pl.program_id(0) == pl.num_programs(0) - 1) & second)
    def _():
        lines = sums.shape[0]
        for k in range(2 if second else 0):
            part = sums[:, k * T : (k + 1) * T].astype(BF16)
            projected[pl.ds(projected.shape[0] - (2 - k) * lines, lines)] = part


def dense(parts, grad, weight, offset, part, before):
    width, rows = weight.shape[1], grad.shape[0]
    step = 1024
    steps = rows // 2 // step
    shift = part * steps
    tail = 2 * (T + 8) if before else 0
    half = pl.BlockSpec((step, T), lambda i: (i, 0))
    full = pl.BlockSpec((step, width), lambda i: (i + shift, 0))

    def whole(*shape):
        return pl.BlockSpec(shape, lambda i: (0, 0))

    return pl.pallas_call(
        functools.partial(dense_kernel, step=step),
        grid=(steps,),
        out_shape=[
            jax.ShapeDtypeStruct((rows, width), BF16),
            jax.ShapeDtypeStruct((rows // 2 + tail, T), BF16),
            jax.ShapeDtypeStruct((T + 8, width), F32),
        ],
        in_specs=[half] * 5
        + [full, whole(T, width), whole(1, width)]
        + ([ANY, whole(T + 8, width), ANY] if before else []),
        out_specs=[full, whole(rows // 2 + tail, T), whole(T + 8, width)],
        input_output_aliases={8: 0} if before else {},
        compiler_params=room(20),
    )(*parts, grad, weight, offset, *before)


def on_device(features, weight, offset, tile_values, tile_rows, tile_cols, live_tiles, grad_hidden):
    tiles = tile_values.reshape(tile_values.shape[2:])
    nodes_here = features.shape[0]
    scaling = 1.0 / math.sqrt(nodes_here * lax.axis_size("row") * lax.axis_size("col"))
    at_row, at_col = lax.axis_index("row"), lax.axis_index("col")
    live = live_tiles.reshape(1)
    meta, tables = prepare(at_row.reshape(1), at_col.reshape(1), live, tile_rows, tile_cols)

    pieces = ring_gather(features, along_inner)
    *sends, said, lists, counts = pack(pieces, ring_gather(meta, along_outer))
    named = ring_swap([None] + sends, along_outer)[1:]
    full = functools.reduce(jnp.maximum, ring_gather(said, along_inner))[0, 0] > 0.5

    def forward_all(outs, pieces):
        whole = ring_gather(jnp.concatenate(pieces), along_outer)
        spans = (4 * nodes_here,) * 4
        return products(live, tables, 2, 0, tiles, whole, spans, (32,) * 4, (1,))

    spans = (nodes_here,) * 4 + (CAP * T,) * 3
    outs = products(live, tables, 1, 0, tiles, pieces + named, spans, (32,) * 4, (1,))
    outs = lax.cond(full, forward_all, lambda outs, pieces: outs, outs, pieces)

    part_rows = nodes_here // 2
    halves = []
    for send, keep in zip(outs[:2], outs[2:]):
        got = other_core(send)
        far = []
        for d in (1, 2, 3):
            at = slice(d * part_rows, (d + 1) * part_rows)
            far.append((keep[at].astype(F32) + got[at].astype(F32)).astype(BF16))
        halves.append([keep, got] + ring_swap([None] + far, along_y)[1:])
    before, own, others = (), [], []
    for part, parts in enumerate(halves):
        hidden, projected, sums = dense(
            parts, grad_hidden, weight, offset.reshape(1, -1), part, before
        )
        here = ring_gather(projected, along_y)
        own.append(here)
        others.append([other_core(piece) for piece in here])
        before = (hidden, sums, others[0][0])

    gathered = others[1] + own[1] + others[0] + own[0]
    spans, outs = (part_rows,) * 16, (64,) + (CAP,) * 3
    here, *parts, sums = products(
        live, tables, 3, 1, tiles, gathered, spans, outs, (0,), tailed=8
    )
    parts = ring_swap([None] + parts, along_outer)[1:]

    def backward_all(outs, gathered):
        mine = products(live, tables, 3, 2, tiles, gathered, spans, (64,) * 4, (0,))
        mine = total_of(ring_swap(mine, along_outer)).reshape(4, nodes_here, T)
        far = [outs[d].at[:nodes_here].set(mine[d].astype(BF16)) for d in (1, 2, 3)]
        return [mine[0]] + far

    *outs, sums = combine(lists, counts, here, sums, parts)
    outs = lax.cond(full, backward_all, lambda outs, gathered: outs, outs, gathered)
    outs = ring_swap(outs, along_inner)
    grad_features, grad_weight, grad_offset = finish(outs, sums, scaling)
    return (hidden, grad_features, grad_weight, grad_offset.reshape(-1))


def solution(mesh):
    in_specs = (
        P(("col", "row"), None),
        P(),
        P(),
        P("row", "col", None, None, None),
        P("row", "col", None),
        P("row", "col", None),
        P("row", "col"),
        P(("row", "col"), None),
    )
    out_specs = (P(("row", "col"), None), P(("col", "row"), None), P(), P())
    return jax.shard_map(
        on_device, mesh=mesh, in_specs=in_specs, out_specs=out_specs, check_vma=False
    )
```

```python
import functools
import itertools
import math

import jax
import jax.numpy as jnp
from jax import lax
from jax.experimental import pallas as pl
from jax.experimental.pallas import tpu as pltpu
from jax.sharding import PartitionSpec as P

T = 128
F32, BF16, I32 = jnp.float32, jnp.bfloat16, jnp.int32
MIB = 1024 * 1024
GROUP = 16
META = 16
CAP = 24
LANES = 32
SMEM = pl.BlockSpec(memory_space=pltpu.SMEM)
VMEM = pl.BlockSpec(memory_space=pltpu.VMEM)
ANY = pl.BlockSpec(memory_space=pl.ANY)


def room(mib):
    return pltpu.CompilerParams(vmem_limit_bytes=mib * MIB)


def along_xz(value, to, x_core):
    pairs = []
    for x, z, y, core in itertools.product(range(4), range(4), range(4), range(2)):
        far = (to(x) % 4, z) if core == x_core else (x, to(z) % 4)
        pairs.append(((x * 4 + z) * 8 + y * 2 + core, (far[0] * 4 + far[1]) * 8 + y * 2 + core))
    return lax.ppermute(value, ("row", "col"), pairs)


def along_inner(value, to):
    return along_xz(value, to, 0)


def along_outer(value, to):
    return along_xz(value, to, 1)


def along_y(value, to):
    pairs = []
    for y in range(4):
        pairs.append((y * 2, to(y) % 4 * 2))
        pairs.append((y * 2 + 1, (2 * y - to(y)) % 4 * 2 + 1))
    return lax.ppermute(value, "col", pairs)


def other_core(value):
    pairs = [(y * 2 + k, y * 2 + 1 - k) for y in range(4) for k in range(2)]
    return lax.ppermute(value, "col", pairs)


def ahead(step):
    return lambda at: at + step


def ring_gather(value, along):
    across, after, before = [along(value, ahead(step)) for step in (2, -1, 1)]
    return [value, after, across, before]


def ring_swap(pieces, along):
    after, before = along(pieces[3], ahead(-1)), along(pieces[1], ahead(1))
    return [pieces[0], after, along(pieces[2], ahead(2)), before]


def total_of(pieces):
    return sum(piece.astype(F32) for piece in pieces)


def block(place):
    return pl.ds(pl.multiple_of(place * T, T), T)


def prepare_kernel(at_row, at_col, live_ref, rows_ref, cols_ref, meta, tables, slots_held, sems):
    copies = [
        pltpu.make_async_copy(ref, slots_held.at[k], sems.at[k])
        for k, ref in enumerate((rows_ref, cols_ref))
    ]
    for copy in copies:
        copy.start()
    for copy in copies:
        copy.wait()
    live = live_ref[0]
    x, z = at_row[0] >> 2, at_row[0] & 3
    y, core = at_col[0] >> 1, at_col[0] & 1
    rows, cols = slots_held[0], slots_held[1]
    slots = cols.shape[1]

    far_core = (rows >> 4) & 1
    same_core = jnp.where(far_core == core, 64, 0)
    dy = (rows >> 5) - y
    dy = jnp.where(far_core == 0, dy, -dy) & 3
    row_place = same_core + ((rows >> 3) & 1) * 32 + dy * 8 + (rows & 7)
    dx, dz = ((cols >> 6) - x) & 3, ((cols >> 4) - z) & 3
    outer, inner = jnp.where(core == 0, dz, dx), jnp.where(core == 0, dx, dz)
    code = inner * 16 + (cols & 15)
    dense_place = outer * 64 + code

    t = lax.broadcasted_iota(I32, (slots, slots), 0)
    s = lax.broadcasted_iota(I32, (slots, slots), 1)
    lane = lax.broadcasted_iota(I32, (slots, T), 1).astype(F32)

    def column(row):
        return jnp.sum(jnp.where(t == s, row, 0.0), axis=1, keepdims=True)

    def count(mask, value=1.0):
        return jnp.sum(jnp.where(mask, value, 0.0), axis=0, keepdims=True)

    valid = lax.broadcasted_iota(I32, (1, slots), 1) < live
    cols_f, outer_f = cols.astype(F32), outer.astype(F32)
    same = column(cols_f) == cols_f
    first = valid & (count(same & (t < s)) == 0.0)
    first_c = column(jnp.where(first, 1.0, 0.0)) > 0.0
    outer_c = column(outer_f)
    rank = count((t < s) & first_c & (outer_c == outer_f))
    over = jnp.where(first & (outer != 0) & (rank >= CAP), 1.0, 0.0)
    over = jnp.max(over, axis=1, keepdims=True)
    far = (64 + (outer - 1) * CAP).astype(F32) + jnp.minimum(rank, CAP - 1.0)
    place = jnp.where(outer == 0, code.astype(F32), far)
    place = count(same & first_c, column(place))
    place = jnp.where(valid, place, 0.0).astype(I32)
    second = (rows >> 3) & 1
    source = (1 - second) * 64 + ((row_place & 64) >> 1) + (row_place & 31)
    pad = jnp.zeros((4, slots), I32)
    tables[...] = jnp.concatenate([row_place, place, dense_place, source, pad], axis=0)

    key = column(jnp.where(first & (rank < CAP), outer_f * LANES + rank, -1.0))
    wanted = count(key == lane, column(code.astype(F32)))
    amounts = jnp.minimum(count((outer_c == lane) & first_c), 1.0 * CAP)
    line = lax.broadcasted_iota(I32, (META, T), 0)
    lines = [wanted, amounts, jnp.broadcast_to(over, (1, T)), jnp.zeros((META - 3, T), F32)]
    meta[...] = jnp.concatenate(lines, axis=0).astype(BF16)


def prepare(at_row, at_col, live, rows, cols):
    slots = cols.shape[-1]
    return pl.pallas_call(
        prepare_kernel,
        out_shape=[
            jax.ShapeDtypeStruct((META, T), BF16),
            jax.ShapeDtypeStruct((8, slots), I32),
        ],
        in_specs=[SMEM] * 3 + [ANY] * 2,
        out_specs=[VMEM] * 2,
        scratch_shapes=[pltpu.VMEM((2, 1, slots), I32), pltpu.SemaphoreType.DMA((2,))],
        compiler_params=room(4),
    )(at_row, at_col, live, rows.reshape(1, slots), cols.reshape(1, slots))


def products_kernel(
    live, tables, tiles_ref, *refs, spans, outs, contract, in_row, out_row, tailed
):
    n = len(spans)
    sources, out_refs, (tiles, held, total, tails, sems) = refs[:n], refs[n:-5], refs[-5:]
    copies = [pltpu.make_async_copy(tiles_ref, tiles, sems.at[n])]
    start = 0
    for k, (ref, rows) in enumerate(zip(sources, spans)):
        copies.append(
            pltpu.make_async_copy(
                ref.at[pl.ds(0, rows)], held.at[pl.ds(start, rows)], sems.at[k]
            )
        )
        start += rows
    for k in range(tailed):
        tail = sources[k].at[pl.ds(spans[k], tails.shape[1])]
        copies.append(pltpu.make_async_copy(tail, tails.at[k], sems.at[n + 1 + k]))
    for copy in copies:
        copy.start()

    zeros = jnp.zeros((4, T, T), F32)

    def clear(k, carry):
        total[pl.ds(k * 4, 4)] = zeros
        return carry

    lax.fori_loop(0, total.shape[0] // 4, clear, 0)
    for copy in copies:
        copy.wait()
    if tailed:
        summed = jnp.sum(tails[...].astype(F32), axis=0)
        lines = summed.shape[0] // 2
        out_refs[-1][:, :T] = summed[:lines]
        out_refs[-1][:, T:] = summed[lines:]
        for ref, blocks in zip(out_refs[1:-1], outs[1:]):
            ref[pl.ds(blocks * T, 2 * lines)] = summed.astype(BF16)

    def group(number, carry):
        products = []
        for k in range(GROUP):
            slot = number * GROUP + k
            product = lax.dot_general(
                tiles[slot],
                held[block(tables[in_row, slot])],
                ((contract, (0,)), ((), ())),
                preferred_element_type=F32,
            )
            products.append(jnp.where(slot < live[0], product, 0.0))
        for k, product in enumerate(products):
            total[tables[out_row, number * GROUP + k]] += product
        return carry

    lax.fori_loop(0, (live[0] + GROUP - 1) // GROUP, group, 0)
    start = 0
    for ref, blocks in zip(out_refs, outs):

        def out(k, carry, ref=ref, start=start):
            for at in range(2):
                ref[block(k * 2 + at)] = total[start + k * 2 + at].astype(BF16)
            return carry

        lax.fori_loop(0, blocks // 2, out, 0)
        start += blocks


def products(live, tables, in_row, out_row, tiles, sources, spans, outs, contract, tailed=0):
    lines = sources[0].shape[0] - spans[0] if tailed else 16
    kernel = functools.partial(
        products_kernel,
        spans=spans,
        outs=outs,
        contract=contract,
        in_row=in_row,
        out_row=out_row,
        tailed=tailed,
    )
    need = tiles.size * 2 + sum(spans) * T * 2 + sum(outs) * T * T * 6
    extra = [lines if tailed and n else 0 for n in range(len(outs))]
    return pl.pallas_call(
        kernel,
        out_shape=[jax.ShapeDtypeStruct((n * T + e, T), BF16) for n, e in zip(outs, extra)]
        + ([jax.ShapeDtypeStruct((lines // 2, 2 * T), F32)] if tailed else []),
        in_specs=[SMEM] * 2 + [ANY] * (1 + len(sources)),
        out_specs=[VMEM] * (len(outs) + (tailed > 0)),
        scratch_shapes=[
            pltpu.VMEM(tiles.shape, BF16),
            pltpu.VMEM((sum(spans), T), BF16),
            pltpu.VMEM((sum(outs), T, T), F32),
            pltpu.VMEM((max(tailed, 1), lines, T), BF16),
            pltpu.SemaphoreType.DMA((len(spans) + 1 + tailed,)),
        ],
        compiler_params=room(need // MIB + 5),
    )(live, tables, tiles, *sources)


def pack_kernel(*refs):
    pieces, metas, sends, (said, lists, counts), (held, heard, words, table, sems) = (
        refs[:4],
        refs[4:8],
        refs[8:11],
        refs[11:14],
        refs[14:],
    )
    fetches = [pltpu.make_async_copy(p, heard.at[k], sems.at[k + 4]) for k, p in enumerate(metas)]
    copies = [pltpu.make_async_copy(p, held.at[k], sems.at[k]) for k, p in enumerate(pieces)]
    for copy in fetches + copies:
        copy.start()
    for copy in fetches:
        copy.wait()
    told = [heard[k].astype(F32)[:8] for k in range(4)]
    for n in range(3):
        words[pl.ds(n * 8, 8)] = told[n + 1].astype(I32)
    fetch = pltpu.make_async_copy(words, table, sems.at[8])
    fetch.start()
    over = functools.reduce(jnp.maximum, told)[2:3]
    said[...] = jnp.broadcast_to(over, (8, T))
    fetch.wait()
    for copy in copies:
        copy.wait()
    for n in range(3):
        group = 3 - n
        amount = table[n * 8 + 1, group]
        counts[n] = amount
        for k in range(4):
            lists[n * LANES + amount + k] = 64

        def step(k, carry, n=n, group=group):
            code = table[n * 8, group * LANES + k]
            lists[n * LANES + k] = code
            sends[n][block(k)] = held[code >> 4, block(code & 15)]
            return carry

        lax.fori_loop(0, amount, step, 0)


def pack(pieces, metas):
    return pl.pallas_call(
        pack_kernel,
        out_shape=[jax.ShapeDtypeStruct((CAP * T, T), BF16)] * 3
        + [jax.ShapeDtypeStruct((8, T), F32)]
        + [jax.ShapeDtypeStruct((3 * LANES,), I32), jax.ShapeDtypeStruct((3,), I32)],
        in_specs=[ANY] * 8,
        out_specs=[VMEM] * 4 + [SMEM] * 2,
        scratch_shapes=[
            pltpu.VMEM((4,) + pieces[0].shape, BF16),
            pltpu.VMEM((4, META, T), BF16),
            pltpu.VMEM((24, T), I32),
            pltpu.SMEM((24, T), I32),
            pltpu.SemaphoreType.DMA((9,)),
        ],
        compiler_params=room(10),
    )(*pieces, *metas)


def combine_kernel(lists, counts, own, sums, *refs):
    parts, outs, summed, total = refs[:3], refs[3:7], refs[7], refs[8]

    def widen(k, carry):
        for at in range(4):
            total[k * 4 + at] = own[block(k * 4 + at)].astype(F32)
        return carry

    lax.fori_loop(0, 16, widen, 0)
    lines = sums.shape[0]
    for k in range(2):
        tail = pl.ds(CAP * T + k * lines, lines)
        line = sums[:, k * T : (k + 1) * T] + total_of([part[tail] for part in parts])
        summed[:, k * T : (k + 1) * T] = line
        for ref in outs[1:]:
            ref[pl.ds(16 * T + k * lines, lines)] = line.astype(BF16)
    for n in range(3):

        def add(k, carry, n=n):
            for at in range(4):
                slot = k * 4 + at
                total[lists[n * LANES + slot]] += parts[n][block(slot)].astype(F32)
            return carry

        lax.fori_loop(0, (counts[n] + 3) // 4, add, 0)
    for n, ref in enumerate(outs):

        def out(k, carry, n=n, ref=ref):
            for at in range(4):
                ref[block(k * 4 + at)] = total[n * 16 + k * 4 + at].astype(ref.dtype)
            return carry

        lax.fori_loop(0, 4, out, 0)


def combine(lists, counts, own, sums, parts):
    rows = 16 * T
    return pl.pallas_call(
        combine_kernel,
        out_shape=[jax.ShapeDtypeStruct((rows, T), F32)]
        + [jax.ShapeDtypeStruct((rows + 2 * sums.shape[0], T), BF16)] * 3
        + [jax.ShapeDtypeStruct(sums.shape, F32)],
        in_specs=[SMEM] * 2 + [VMEM] * 5,
        out_specs=[VMEM] * 5,
        scratch_shapes=[pltpu.VMEM((65, T, T), F32)],
        compiler_params=room(16),
    )(lists, counts, own, sums, *parts)


def finish_kernel(*refs, scaling):
    pieces, sums, (nodes, weight, offset) = refs[:4], refs[4], refs[5:]
    rows = nodes.shape[0]
    nodes[...] = total_of([ref[pl.ds(0, rows)] for ref in pieces])
    lines = sums.shape[0]
    for k in range(2):
        part = pl.ds(k * T, T)
        total = sums[:, part]
        for ref in pieces[1:]:
            total = total + ref[pl.ds(rows + k * lines, lines)].astype(F32)
        total = total * scaling
        weight[:, part] = total[:T]
        offset[:, part] = jnp.sum(total[T:], axis=0, keepdims=True)


def finish(pieces, sums, scaling):
    width = sums.shape[-1]
    return pl.pallas_call(
        functools.partial(finish_kernel, scaling=scaling),
        out_shape=[
            jax.ShapeDtypeStruct(pieces[0].shape, F32),
            jax.ShapeDtypeStruct((T, width), F32),
            jax.ShapeDtypeStruct((1, width), F32),
        ],
        in_specs=[VMEM] * 5,
        out_specs=[VMEM] * 3,
        compiler_params=room(10),
    )(*pieces, sums)


def dense_kernel(*refs, step):
    parts, (grad, weight, offset), rest = refs[:5], refs[5:8], refs[8:]
    hidden, projected, sums = rest[-3:]
    second = len(rest) > 3

    @pl.when(pl.program_id(0) == 0)
    def _():
        sums[...] = rest[1][...] if second else jnp.zeros_like(sums)

    mixed = total_of([ref[...] for ref in parts])
    high = mixed.astype(BF16)
    low = (mixed - high.astype(F32)).astype(BF16)
    w = weight[...]
    pre = jnp.dot(high, w, preferred_element_type=F32)
    pre = pre + jnp.dot(low, w, preferred_element_type=F32) + offset[...]
    s = jax.nn.sigmoid(pre)
    hidden[...] = (pre * s).astype(BF16)
    slope = (grad[...].astype(F32) * s * (1.0 + pre * (1.0 - s))).astype(BF16)
    projected[pl.ds(pl.multiple_of(pl.program_id(0) * step, step), step)] = lax.dot_general(
        slope, w, (((1,), (1,)), ((), ())), preferred_element_type=F32
    ).astype(BF16)
    over_rows = (((0,), (0,)), ((), ()))
    sums[:T] += lax.dot_general(
        high, slope, over_rows, preferred_element_type=F32
    ) + lax.dot_general(low, slope, over_rows, preferred_element_type=F32)
    sums[T:] += jnp.sum(slope.astype(F32).reshape(-1, 8, slope.shape[1]), axis=0)

    @pl.when((pl.program_id(0) == pl.num_programs(0) - 1) & second)
    def _():
        lines = sums.shape[0]
        for k in range(2 if second else 0):
            part = sums[:, k * T : (k + 1) * T].astype(BF16)
            projected[pl.ds(projected.shape[0] - (2 - k) * lines, lines)] = part


def dense(parts, grad, weight, offset, part, before):
    width, rows = weight.shape[1], grad.shape[0]
    step = 1024
    steps = rows // 2 // step
    shift = part * steps
    tail = 2 * (T + 8) if before else 0
    half = pl.BlockSpec((step, T), lambda i: (i, 0))
    full = pl.BlockSpec((step, width), lambda i: (i + shift, 0))

    def whole(*shape):
        return pl.BlockSpec(shape, lambda i: (0, 0))

    return pl.pallas_call(
        functools.partial(dense_kernel, step=step),
        grid=(steps,),
        out_shape=[
            jax.ShapeDtypeStruct((rows, width), BF16),
            jax.ShapeDtypeStruct((rows // 2 + tail, T), BF16),
            jax.ShapeDtypeStruct((T + 8, width), F32),
        ],
        in_specs=[half] * 5
        + [full, whole(T, width), whole(1, width)]
        + ([ANY, whole(T + 8, width), ANY] if before else []),
        out_specs=[full, whole(rows // 2 + tail, T), whole(T + 8, width)],
        input_output_aliases={8: 0} if before else {},
        compiler_params=room(20),
    )(*parts, grad, weight, offset, *before)


def on_device(features, weight, offset, tile_values, tile_rows, tile_cols, live_tiles, grad_hidden):
    tiles = tile_values.reshape(tile_values.shape[2:])
    nodes_here = features.shape[0]
    scaling = 1.0 / math.sqrt(nodes_here * lax.axis_size("row") * lax.axis_size("col"))
    at_row, at_col = lax.axis_index("row"), lax.axis_index("col")
    live = live_tiles.reshape(1)
    meta, tables = prepare(at_row.reshape(1), at_col.reshape(1), live, tile_rows, tile_cols)

    pieces = ring_gather(features, along_inner)
    *sends, said, lists, counts = pack(pieces, ring_gather(meta, along_outer))
    named = ring_swap([None] + sends, along_outer)[1:]
    full = functools.reduce(jnp.maximum, ring_gather(said, along_inner))[0, 0] > 0.5

    def forward_all(outs, pieces):
        whole = ring_gather(jnp.concatenate(pieces), along_outer)
        spans = (4 * nodes_here,) * 4
        return products(live, tables, 2, 0, tiles, whole, spans, (32,) * 4, (1,))

    spans = (nodes_here,) * 4 + (CAP * T,) * 3
    outs = products(live, tables, 1, 0, tiles, pieces + named, spans, (32,) * 4, (1,))
    outs = lax.cond(full, forward_all, lambda outs, pieces: outs, outs, pieces)

    part_rows = nodes_here // 2
    halves = []
    for send, keep in zip(outs[:2], outs[2:]):
        got = other_core(send)
        far = []
        for d in (1, 2, 3):
            at = slice(d * part_rows, (d + 1) * part_rows)
            far.append((keep[at].astype(F32) + got[at].astype(F32)).astype(BF16))
        halves.append([keep, got] + ring_swap([None] + far, along_y)[1:])
    before, own, others = (), [], []
    for part, parts in enumerate(halves):
        hidden, projected, sums = dense(
            parts, grad_hidden, weight, offset.reshape(1, -1), part, before
        )
        here = ring_gather(projected, along_y)
        own.append(here)
        others.append([other_core(piece) for piece in here])
        before = (hidden, sums, others[0][0])

    gathered = others[1] + own[1] + others[0] + own[0]
    spans, outs = (part_rows,) * 16, (64,) + (CAP,) * 3
    here, *parts, sums = products(
        live, tables, 3, 1, tiles, gathered, spans, outs, (0,), tailed=8
    )
    parts = ring_swap([None] + parts, along_outer)[1:]

    def backward_all(outs, gathered):
        mine = products(live, tables, 3, 2, tiles, gathered, spans, (64,) * 4, (0,))
        mine = total_of(ring_swap(mine, along_outer)).reshape(4, nodes_here, T)
        far = [outs[d].at[:nodes_here].set(mine[d].astype(BF16)) for d in (1, 2, 3)]
        return [mine[0]] + far

    *outs, sums = combine(lists, counts, here, sums, parts)
    outs = lax.cond(full, backward_all, lambda outs, gathered: outs, outs, gathered)
    outs = ring_swap(outs, along_inner)
    grad_features, grad_weight, grad_offset = finish(outs, sums, scaling)
    return (hidden, grad_features, grad_weight, grad_offset.reshape(-1))


def solution(mesh):
    in_specs = (
        P(("col", "row"), None),
        P(),
        P(),
        P("row", "col", None, None, None),
        P("row", "col", None),
        P("row", "col", None),
        P("row", "col"),
        P(("row", "col"), None),
    )
    out_specs = (P(("row", "col"), None), P(("col", "row"), None), P(), P())
    return jax.shard_map(
        on_device, mesh=mesh, in_specs=in_specs, out_specs=out_specs, check_vma=False
    )
```

```python
import functools
import itertools
import math

import jax
import jax.numpy as jnp
from jax import lax
from jax.experimental import pallas as pl
from jax.experimental.pallas import tpu as pltpu
from jax.sharding import PartitionSpec as P

T = 128
F32, BF16, I32 = jnp.float32, jnp.bfloat16, jnp.int32
MIB = 1024 * 1024
GROUP = 16
META = 16
CAP = 24
LANES = 32
SMEM = pl.BlockSpec(memory_space=pltpu.SMEM)
VMEM = pl.BlockSpec(memory_space=pltpu.VMEM)
ANY = pl.BlockSpec(memory_space=pl.ANY)


def room(mib):
    return pltpu.CompilerParams(vmem_limit_bytes=mib * MIB)


def along_xz(value, to, x_core):
    pairs = []
    for x, z, y, core in itertools.product(range(4), range(4), range(4), range(2)):
        far = (to(x) % 4, z) if core == x_core else (x, to(z) % 4)
        pairs.append(((x * 4 + z) * 8 + y * 2 + core, (far[0] * 4 + far[1]) * 8 + y * 2 + core))
    return lax.ppermute(value, ("row", "col"), pairs)


def along_inner(value, to):
    return along_xz(value, to, 0)


def along_outer(value, to):
    return along_xz(value, to, 1)


def along_y(value, to):
    pairs = []
    for y in range(4):
        pairs.append((y * 2, to(y) % 4 * 2))
        pairs.append((y * 2 + 1, (2 * y - to(y)) % 4 * 2 + 1))
    return lax.ppermute(value, "col", pairs)


def other_core(value):
    pairs = [(y * 2 + k, y * 2 + 1 - k) for y in range(4) for k in range(2)]
    return lax.ppermute(value, "col", pairs)


def ahead(step):
    return lambda at: at + step


def ring_gather(value, along):
    across, after, before = [along(value, ahead(step)) for step in (2, -1, 1)]
    return [value, after, across, before]


def ring_swap(pieces, along):
    after, before = along(pieces[3], ahead(-1)), along(pieces[1], ahead(1))
    return [pieces[0], after, along(pieces[2], ahead(2)), before]


def total_of(pieces):
    return sum(piece.astype(F32) for piece in pieces)


def block(place):
    return pl.ds(pl.multiple_of(place * T, T), T)


def prepare_kernel(at_row, at_col, live_ref, rows_ref, cols_ref, meta, tables, slots_held, sems):
    copies = [
        pltpu.make_async_copy(ref, slots_held.at[k], sems.at[k])
        for k, ref in enumerate((rows_ref, cols_ref))
    ]
    for copy in copies:
        copy.start()
    for copy in copies:
        copy.wait()
    live = live_ref[0]
    x, z = at_row[0] >> 2, at_row[0] & 3
    y, core = at_col[0] >> 1, at_col[0] & 1
    rows, cols = slots_held[0], slots_held[1]
    slots = cols.shape[1]

    far_core = (rows >> 4) & 1
    same_core = jnp.where(far_core == core, 64, 0)
    dy = (rows >> 5) - y
    dy = jnp.where(far_core == 0, dy, -dy) & 3
    row_place = same_core + ((rows >> 3) & 1) * 32 + dy * 8 + (rows & 7)
    dx, dz = ((cols >> 6) - x) & 3, ((cols >> 4) - z) & 3
    outer, inner = jnp.where(core == 0, dz, dx), jnp.where(core == 0, dx, dz)
    code = inner * 16 + (cols & 15)
    dense_place = outer * 64 + code

    t = lax.broadcasted_iota(I32, (slots, slots), 0)
    s = lax.broadcasted_iota(I32, (slots, slots), 1)
    lane = lax.broadcasted_iota(I32, (slots, T), 1).astype(F32)

    def column(row):
        return jnp.sum(jnp.where(t == s, row, 0.0), axis=1, keepdims=True)

    def count(mask, value=1.0):
        return jnp.sum(jnp.where(mask, value, 0.0), axis=0, keepdims=True)

    valid = lax.broadcasted_iota(I32, (1, slots), 1) < live
    cols_f, outer_f = cols.astype(F32), outer.astype(F32)
    same = column(cols_f) == cols_f
    first = valid & (count(same & (t < s)) == 0.0)
    first_c = column(jnp.where(first, 1.0, 0.0)) > 0.0
    outer_c = column(outer_f)
    rank = count((t < s) & first_c & (outer_c == outer_f))
    over = jnp.where(first & (outer != 0) & (rank >= CAP), 1.0, 0.0)
    over = jnp.max(over, axis=1, keepdims=True)
    far = (64 + (outer - 1) * CAP).astype(F32) + jnp.minimum(rank, CAP - 1.0)
    place = jnp.where(outer == 0, code.astype(F32), far)
    place = count(same & first_c, column(place))
    place = jnp.where(valid, place, 0.0).astype(I32)
    second = (rows >> 3) & 1
    source = (1 - second) * 64 + ((row_place & 64) >> 1) + (row_place & 31)
    pad = jnp.zeros((4, slots), I32)
    tables[...] = jnp.concatenate([row_place, place, dense_place, source, pad], axis=0)

    key = column(jnp.where(first & (rank < CAP), outer_f * LANES + rank, -1.0))
    wanted = count(key == lane, column(code.astype(F32)))
    amounts = jnp.minimum(count((outer_c == lane) & first_c), 1.0 * CAP)
    line = lax.broadcasted_iota(I32, (META, T), 0)
    lines = [wanted, amounts, jnp.broadcast_to(over, (1, T)), jnp.zeros((META - 3, T), F32)]
    meta[...] = jnp.concatenate(lines, axis=0).astype(BF16)


def prepare(at_row, at_col, live, rows, cols):
    slots = cols.shape[-1]
    return pl.pallas_call(
        prepare_kernel,
        out_shape=[
            jax.ShapeDtypeStruct((META, T), BF16),
            jax.ShapeDtypeStruct((8, slots), I32),
        ],
        in_specs=[SMEM] * 3 + [ANY] * 2,
        out_specs=[VMEM] * 2,
        scratch_shapes=[pltpu.VMEM((2, 1, slots), I32), pltpu.SemaphoreType.DMA((2,))],
        compiler_params=room(4),
    )(at_row, at_col, live, rows.reshape(1, slots), cols.reshape(1, slots))


def products_kernel(
    live, tables, tiles_ref, *refs, spans, outs, contract, in_row, out_row, tailed
):
    n = len(spans)
    sources, out_refs, (tiles, held, total, tails, sems) = refs[:n], refs[n:-5], refs[-5:]
    copies = [pltpu.make_async_copy(tiles_ref, tiles, sems.at[n])]
    start = 0
    for k, (ref, rows) in enumerate(zip(sources, spans)):
        copies.append(
            pltpu.make_async_copy(
                ref.at[pl.ds(0, rows)], held.at[pl.ds(start, rows)], sems.at[k]
            )
        )
        start += rows
    for k in range(tailed):
        tail = sources[k].at[pl.ds(spans[k], tails.shape[1])]
        copies.append(pltpu.make_async_copy(tail, tails.at[k], sems.at[n + 1 + k]))
    for copy in copies:
        copy.start()

    zeros = jnp.zeros((4, T, T), F32)

    def clear(k, carry):
        total[pl.ds(k * 4, 4)] = zeros
        return carry

    lax.fori_loop(0, total.shape[0] // 4, clear, 0)
    for copy in copies:
        copy.wait()
    if tailed:
        summed = jnp.sum(tails[...].astype(F32), axis=0)
        lines = summed.shape[0] // 2
        out_refs[-1][:, :T] = summed[:lines]
        out_refs[-1][:, T:] = summed[lines:]
        for ref, blocks in zip(out_refs[1:-1], outs[1:]):
            ref[pl.ds(blocks * T, 2 * lines)] = summed.astype(BF16)

    def group(number, carry):
        products = []
        for k in range(GROUP):
            slot = number * GROUP + k
            product = lax.dot_general(
                tiles[slot],
                held[block(tables[in_row, slot])],
                ((contract, (0,)), ((), ())),
                preferred_element_type=F32,
            )
            products.append(jnp.where(slot < live[0], product, 0.0))
        for k, product in enumerate(products):
            total[tables[out_row, number * GROUP + k]] += product
        return carry

    lax.fori_loop(0, (live[0] + GROUP - 1) // GROUP, group, 0)
    start = 0
    for ref, blocks in zip(out_refs, outs):

        def out(k, carry, ref=ref, start=start):
            for at in range(2):
                ref[block(k * 2 + at)] = total[start + k * 2 + at].astype(BF16)
            return carry

        lax.fori_loop(0, blocks // 2, out, 0)
        start += blocks


def products(live, tables, in_row, out_row, tiles, sources, spans, outs, contract, tailed=0):
    lines = sources[0].shape[0] - spans[0] if tailed else 16
    kernel = functools.partial(
        products_kernel,
        spans=spans,
        outs=outs,
        contract=contract,
        in_row=in_row,
        out_row=out_row,
        tailed=tailed,
    )
    need = tiles.size * 2 + sum(spans) * T * 2 + sum(outs) * T * T * 6
    extra = [lines if tailed and n else 0 for n in range(len(outs))]
    return pl.pallas_call(
        kernel,
        out_shape=[jax.ShapeDtypeStruct((n * T + e, T), BF16) for n, e in zip(outs, extra)]
        + ([jax.ShapeDtypeStruct((lines // 2, 2 * T), F32)] if tailed else []),
        in_specs=[SMEM] * 2 + [ANY] * (1 + len(sources)),
        out_specs=[VMEM] * (len(outs) + (tailed > 0)),
        scratch_shapes=[
            pltpu.VMEM(tiles.shape, BF16),
            pltpu.VMEM((sum(spans), T), BF16),
            pltpu.VMEM((sum(outs), T, T), F32),
            pltpu.VMEM((max(tailed, 1), lines, T), BF16),
            pltpu.SemaphoreType.DMA((len(spans) + 1 + tailed,)),
        ],
        compiler_params=room(need // MIB + 5),
    )(live, tables, tiles, *sources)


def pack_kernel(*refs):
    pieces, metas, sends, (said, lists, counts), (held, heard, words, table, sems) = (
        refs[:4],
        refs[4:8],
        refs[8:11],
        refs[11:14],
        refs[14:],
    )
    fetches = [pltpu.make_async_copy(p, heard.at[k], sems.at[k + 4]) for k, p in enumerate(metas)]
    copies = [pltpu.make_async_copy(p, held.at[k], sems.at[k]) for k, p in enumerate(pieces)]
    for copy in fetches + copies:
        copy.start()
    for copy in fetches:
        copy.wait()
    told = [heard[k].astype(F32)[:8] for k in range(4)]
    for n in range(3):
        words[pl.ds(n * 8, 8)] = told[n + 1].astype(I32)
    fetch = pltpu.make_async_copy(words, table, sems.at[8])
    fetch.start()
    over = functools.reduce(jnp.maximum, told)[2:3]
    said[...] = jnp.broadcast_to(over, (8, T))
    fetch.wait()
    for copy in copies:
        copy.wait()
    for n in range(3):
        group = 3 - n
        amount = table[n * 8 + 1, group]
        counts[n] = amount
        for k in range(4):
            lists[n * LANES + amount + k] = 64

        def step(k, carry, n=n, group=group):
            code = table[n * 8, group * LANES + k]
            lists[n * LANES + k] = code
            sends[n][block(k)] = held[code >> 4, block(code & 15)]
            return carry

        lax.fori_loop(0, amount, step, 0)


def pack(pieces, metas):
    return pl.pallas_call(
        pack_kernel,
        out_shape=[jax.ShapeDtypeStruct((CAP * T, T), BF16)] * 3
        + [jax.ShapeDtypeStruct((8, T), F32)]
        + [jax.ShapeDtypeStruct((3 * LANES,), I32), jax.ShapeDtypeStruct((3,), I32)],
        in_specs=[ANY] * 8,
        out_specs=[VMEM] * 4 + [SMEM] * 2,
        scratch_shapes=[
            pltpu.VMEM((4,) + pieces[0].shape, BF16),
            pltpu.VMEM((4, META, T), BF16),
            pltpu.VMEM((24, T), I32),
            pltpu.SMEM((24, T), I32),
            pltpu.SemaphoreType.DMA((9,)),
        ],
        compiler_params=room(10),
    )(*pieces, *metas)


def combine_kernel(lists, counts, own, sums, *refs):
    parts, outs, summed, total = refs[:3], refs[3:7], refs[7], refs[8]

    def widen(k, carry):
        for at in range(4):
            total[k * 4 + at] = own[block(k * 4 + at)].astype(F32)
        return carry

    lax.fori_loop(0, 16, widen, 0)
    lines = sums.shape[0]
    for k in range(2):
        tail = pl.ds(CAP * T + k * lines, lines)
        line = sums[:, k * T : (k + 1) * T] + total_of([part[tail] for part in parts])
        summed[:, k * T : (k + 1) * T] = line
        for ref in outs[1:]:
            ref[pl.ds(16 * T + k * lines, lines)] = line.astype(BF16)
    for n in range(3):

        def add(k, carry, n=n):
            for at in range(4):
                slot = k * 4 + at
                total[lists[n * LANES + slot]] += parts[n][block(slot)].astype(F32)
            return carry

        lax.fori_loop(0, (counts[n] + 3) // 4, add, 0)
    for n, ref in enumerate(outs):

        def out(k, carry, n=n, ref=ref):
            for at in range(4):
                ref[block(k * 4 + at)] = total[n * 16 + k * 4 + at].astype(ref.dtype)
            return carry

        lax.fori_loop(0, 4, out, 0)


def combine(lists, counts, own, sums, parts):
    rows = 16 * T
    return pl.pallas_call(
        combine_kernel,
        out_shape=[jax.ShapeDtypeStruct((rows, T), F32)]
        + [jax.ShapeDtypeStruct((rows + 2 * sums.shape[0], T), BF16)] * 3
        + [jax.ShapeDtypeStruct(sums.shape, F32)],
        in_specs=[SMEM] * 2 + [VMEM] * 5,
        out_specs=[VMEM] * 5,
        scratch_shapes=[pltpu.VMEM((65, T, T), F32)],
        compiler_params=room(16),
    )(lists, counts, own, sums, *parts)


def finish_kernel(*refs, scaling):
    pieces, sums, (nodes, weight, offset) = refs[:4], refs[4], refs[5:]
    rows = nodes.shape[0]
    nodes[...] = total_of([ref[pl.ds(0, rows)] for ref in pieces])
    lines = sums.shape[0]
    for k in range(2):
        part = pl.ds(k * T, T)
        total = sums[:, part]
        for ref in pieces[1:]:
            total = total + ref[pl.ds(rows + k * lines, lines)].astype(F32)
        total = total * scaling
        weight[:, part] = total[:T]
        offset[:, part] = jnp.sum(total[T:], axis=0, keepdims=True)


def finish(pieces, sums, scaling):
    width = sums.shape[-1]
    return pl.pallas_call(
        functools.partial(finish_kernel, scaling=scaling),
        out_shape=[
            jax.ShapeDtypeStruct(pieces[0].shape, F32),
            jax.ShapeDtypeStruct((T, width), F32),
            jax.ShapeDtypeStruct((1, width), F32),
        ],
        in_specs=[VMEM] * 5,
        out_specs=[VMEM] * 3,
        compiler_params=room(10),
    )(*pieces, sums)


def dense_kernel(*refs, step):
    parts, (grad, weight, offset), rest = refs[:5], refs[5:8], refs[8:]
    hidden, projected, sums = rest[-3:]
    second = len(rest) > 3

    @pl.when(pl.program_id(0) == 0)
    def _():
        sums[...] = rest[1][...] if second else jnp.zeros_like(sums)

    mixed = total_of([ref[...] for ref in parts])
    high = mixed.astype(BF16)
    low = (mixed - high.astype(F32)).astype(BF16)
    w = weight[...]
    pre = jnp.dot(high, w, preferred_element_type=F32)
    pre = pre + jnp.dot(low, w, preferred_element_type=F32) + offset[...]
    s = jax.nn.sigmoid(pre)
    hidden[...] = (pre * s).astype(BF16)
    slope = (grad[...].astype(F32) * s * (1.0 + pre * (1.0 - s))).astype(BF16)
    projected[pl.ds(pl.multiple_of(pl.program_id(0) * step, step), step)] = lax.dot_general(
        slope, w, (((1,), (1,)), ((), ())), preferred_element_type=F32
    ).astype(BF16)
    over_rows = (((0,), (0,)), ((), ()))
    sums[:T] += lax.dot_general(
        high, slope, over_rows, preferred_element_type=F32
    ) + lax.dot_general(low, slope, over_rows, preferred_element_type=F32)
    sums[T:] += jnp.sum(slope.astype(F32).reshape(-1, 16, slope.shape[1]), axis=0)

    @pl.when((pl.program_id(0) == pl.num_programs(0) - 1) & second)
    def _():
        lines = sums.shape[0]
        for k in range(2 if second else 0):
            part = sums[:, k * T : (k + 1) * T].astype(BF16)
            projected[pl.ds(projected.shape[0] - (2 - k) * lines, lines)] = part


def dense(parts, grad, weight, offset, part, before):
    width, rows = weight.shape[1], grad.shape[0]
    step = 1024
    steps = rows // 2 // step
    shift = part * steps
    tail = 2 * (T + 16) if before else 0
    half = pl.BlockSpec((step, T), lambda i: (i, 0))
    full = pl.BlockSpec((step, width), lambda i: (i + shift, 0))

    def whole(*shape):
        return pl.BlockSpec(shape, lambda i: (0, 0))

    return pl.pallas_call(
        functools.partial(dense_kernel, step=step),
        grid=(steps,),
        out_shape=[
            jax.ShapeDtypeStruct((rows, width), BF16),
            jax.ShapeDtypeStruct((rows // 2 + tail, T), BF16),
            jax.ShapeDtypeStruct((T + 16, width), F32),
        ],
        in_specs=[half] * 5
        + [full, whole(T, width), whole(1, width)]
        + ([ANY, whole(T + 16, width), ANY] if before else []),
        out_specs=[full, whole(rows // 2 + tail, T), whole(T + 16, width)],
        input_output_aliases={8: 0} if before else {},
        compiler_params=room(20),
    )(*parts, grad, weight, offset, *before)


def on_device(features, weight, offset, tile_values, tile_rows, tile_cols, live_tiles, grad_hidden):
    tiles = tile_values.reshape(tile_values.shape[2:])
    nodes_here = features.shape[0]
    scaling = 1.0 / math.sqrt(nodes_here * lax.axis_size("row") * lax.axis_size("col"))
    at_row, at_col = lax.axis_index("row"), lax.axis_index("col")
    live = live_tiles.reshape(1)
    meta, tables = prepare(at_row.reshape(1), at_col.reshape(1), live, tile_rows, tile_cols)

    pieces = ring_gather(features, along_inner)
    *sends, said, lists, counts = pack(pieces, ring_gather(meta, along_outer))
    named = ring_swap([None] + sends, along_outer)[1:]
    full = functools.reduce(jnp.maximum, ring_gather(said, along_inner))[0, 0] > 0.5

    def forward_all(outs, pieces):
        whole = ring_gather(jnp.concatenate(pieces), along_outer)
        spans = (4 * nodes_here,) * 4
        return products(live, tables, 2, 0, tiles, whole, spans, (32,) * 4, (1,))

    spans = (nodes_here,) * 4 + (CAP * T,) * 3
    outs = products(live, tables, 1, 0, tiles, pieces + named, spans, (32,) * 4, (1,))
    outs = lax.cond(full, forward_all, lambda outs, pieces: outs, outs, pieces)

    part_rows = nodes_here // 2
    halves = []
    for send, keep in zip(outs[:2], outs[2:]):
        got = other_core(send)
        far = []
        for d in (1, 2, 3):
            at = slice(d * part_rows, (d + 1) * part_rows)
            far.append((keep[at].astype(F32) + got[at].astype(F32)).astype(BF16))
        halves.append([keep, got] + ring_swap([None] + far, along_y)[1:])
    before, own, others = (), [], []
    for part, parts in enumerate(halves):
        hidden, projected, sums = dense(
            parts, grad_hidden, weight, offset.reshape(1, -1), part, before
        )
        here = ring_gather(projected, along_y)
        own.append(here)
        others.append([other_core(piece) for piece in here])
        before = (hidden, sums, others[0][0])

    gathered = others[1] + own[1] + others[0] + own[0]
    spans, outs = (part_rows,) * 16, (64,) + (CAP,) * 3
    here, *parts, sums = products(
        live, tables, 3, 1, tiles, gathered, spans, outs, (0,), tailed=8
    )
    parts = ring_swap([None] + parts, along_outer)[1:]

    def backward_all(outs, gathered):
        mine = products(live, tables, 3, 2, tiles, gathered, spans, (64,) * 4, (0,))
        mine = total_of(ring_swap(mine, along_outer)).reshape(4, nodes_here, T)
        far = [outs[d].at[:nodes_here].set(mine[d].astype(BF16)) for d in (1, 2, 3)]
        return [mine[0]] + far

    *outs, sums = combine(lists, counts, here, sums, parts)
    outs = lax.cond(full, backward_all, lambda outs, gathered: outs, outs, gathered)
    outs = ring_swap(outs, along_inner)
    grad_features, grad_weight, grad_offset = finish(outs, sums, scaling)
    return (hidden, grad_features, grad_weight, grad_offset.reshape(-1))


def solution(mesh):
    in_specs = (
        P(("col", "row"), None),
        P(),
        P(),
        P("row", "col", None, None, None),
        P("row", "col", None),
        P("row", "col", None),
        P("row", "col"),
        P(("row", "col"), None),
    )
    out_specs = (P(("row", "col"), None), P(("col", "row"), None), P(), P())
    return jax.shard_map(
        on_device, mesh=mesh, in_specs=in_specs, out_specs=out_specs, check_vma=False
    )
```

```python
import functools
import itertools
import math

import jax
import jax.numpy as jnp
from jax import lax
from jax.experimental import pallas as pl
from jax.experimental.pallas import tpu as pltpu
from jax.sharding import PartitionSpec as P

T = 128
F32, BF16, I32 = jnp.float32, jnp.bfloat16, jnp.int32
MIB = 1024 * 1024
GROUP = 16
META = 16
CAP = 24
LANES = 32
SMEM = pl.BlockSpec(memory_space=pltpu.SMEM)
VMEM = pl.BlockSpec(memory_space=pltpu.VMEM)
ANY = pl.BlockSpec(memory_space=pl.ANY)


def room(mib):
    return pltpu.CompilerParams(vmem_limit_bytes=mib * MIB)


def along_xz(value, to, x_core):
    pairs = []
    for x, z, y, core in itertools.product(range(4), range(4), range(4), range(2)):
        far = (to(x) % 4, z) if core == x_core else (x, to(z) % 4)
        pairs.append(((x * 4 + z) * 8 + y * 2 + core, (far[0] * 4 + far[1]) * 8 + y * 2 + core))
    return lax.ppermute(value, ("row", "col"), pairs)


def along_inner(value, to):
    return along_xz(value, to, 0)


def along_outer(value, to):
    return along_xz(value, to, 1)


def along_y(value, to):
    pairs = []
    for y in range(4):
        pairs.append((y * 2, to(y) % 4 * 2))
        pairs.append((y * 2 + 1, (2 * y - to(y)) % 4 * 2 + 1))
    return lax.ppermute(value, "col", pairs)


def other_core(value):
    pairs = [(y * 2 + k, y * 2 + 1 - k) for y in range(4) for k in range(2)]
    return lax.ppermute(value, "col", pairs)


def ahead(step):
    return lambda at: at + step


def ring_gather(value, along):
    across, after, before = [along(value, ahead(step)) for step in (2, -1, 1)]
    return [value, after, across, before]


def ring_swap(pieces, along):
    after, before = along(pieces[3], ahead(-1)), along(pieces[1], ahead(1))
    return [pieces[0], after, along(pieces[2], ahead(2)), before]


def total_of(pieces):
    return sum(piece.astype(F32) for piece in pieces)


def block(place):
    return pl.ds(pl.multiple_of(place * T, T), T)


def prepare_kernel(at_row, at_col, live_ref, rows_ref, cols_ref, meta, tables, slots_held, sems):
    copies = [
        pltpu.make_async_copy(ref, slots_held.at[k], sems.at[k])
        for k, ref in enumerate((rows_ref, cols_ref))
    ]
    for copy in copies:
        copy.start()
    for copy in copies:
        copy.wait()
    live = live_ref[0]
    x, z = at_row[0] >> 2, at_row[0] & 3
    y, core = at_col[0] >> 1, at_col[0] & 1
    rows, cols = slots_held[0], slots_held[1]
    slots = cols.shape[1]

    far_core = (rows >> 4) & 1
    same_core = jnp.where(far_core == core, 64, 0)
    dy = (rows >> 5) - y
    dy = jnp.where(far_core == 0, dy, -dy) & 3
    row_place = same_core + ((rows >> 3) & 1) * 32 + dy * 8 + (rows & 7)
    dx, dz = ((cols >> 6) - x) & 3, ((cols >> 4) - z) & 3
    outer, inner = jnp.where(core == 0, dz, dx), jnp.where(core == 0, dx, dz)
    code = inner * 16 + (cols & 15)
    dense_place = outer * 64 + code

    t = lax.broadcasted_iota(I32, (slots, slots), 0)
    s = lax.broadcasted_iota(I32, (slots, slots), 1)
    lane = lax.broadcasted_iota(I32, (slots, T), 1).astype(F32)

    def column(row):
        return jnp.sum(jnp.where(t == s, row, 0.0), axis=1, keepdims=True)

    def count(mask, value=1.0):
        return jnp.sum(jnp.where(mask, value, 0.0), axis=0, keepdims=True)

    valid = lax.broadcasted_iota(I32, (1, slots), 1) < live
    cols_f, outer_f = cols.astype(F32), outer.astype(F32)
    same = column(cols_f) == cols_f
    first = valid & (count(same & (t < s)) == 0.0)
    first_c = column(jnp.where(first, 1.0, 0.0)) > 0.0
    outer_c = column(outer_f)
    rank = count((t < s) & first_c & (outer_c == outer_f))
    over = jnp.where(first & (outer != 0) & (rank >= CAP), 1.0, 0.0)
    over = jnp.max(over, axis=1, keepdims=True)
    far = (64 + (outer - 1) * CAP).astype(F32) + jnp.minimum(rank, CAP - 1.0)
    place = jnp.where(outer == 0, code.astype(F32), far)
    place = count(same & first_c, column(place))
    place = jnp.where(valid, place, 0.0).astype(I32)
    second = (rows >> 3) & 1
    source = (1 - second) * 64 + ((row_place & 64) >> 1) + (row_place & 31)
    pad = jnp.zeros((4, slots), I32)
    tables[...] = jnp.concatenate([row_place, place, dense_place, source, pad], axis=0)

    key = column(jnp.where(first & (rank < CAP), outer_f * LANES + rank, -1.0))
    wanted = count(key == lane, column(code.astype(F32)))
    amounts = jnp.minimum(count((outer_c == lane) & first_c), 1.0 * CAP)
    line = lax.broadcasted_iota(I32, (META, T), 0)
    lines = [wanted, amounts, jnp.broadcast_to(over, (1, T)), jnp.zeros((META - 3, T), F32)]
    meta[...] = jnp.concatenate(lines, axis=0).astype(BF16)


def prepare(at_row, at_col, live, rows, cols):
    slots = cols.shape[-1]
    return pl.pallas_call(
        prepare_kernel,
        out_shape=[
            jax.ShapeDtypeStruct((META, T), BF16),
            jax.ShapeDtypeStruct((8, slots), I32),
        ],
        in_specs=[SMEM] * 3 + [ANY] * 2,
        out_specs=[VMEM] * 2,
        scratch_shapes=[pltpu.VMEM((2, 1, slots), I32), pltpu.SemaphoreType.DMA((2,))],
        compiler_params=room(4),
    )(at_row, at_col, live, rows.reshape(1, slots), cols.reshape(1, slots))


def products_kernel(
    live, tables, tiles, *refs, spans, outs, contract, in_row, out_row, tailed
):
    n = len(spans)
    sources, out_refs, (held, total, tails, sems) = refs[:n], refs[n:-4], refs[-4:]
    copies = []
    start = 0
    for k, (ref, rows) in enumerate(zip(sources, spans)):
        copies.append(
            pltpu.make_async_copy(
                ref.at[pl.ds(0, rows)], held.at[pl.ds(start, rows)], sems.at[k]
            )
        )
        start += rows
    for k in range(tailed):
        tail = sources[k].at[pl.ds(spans[k], tails.shape[1])]
        copies.append(pltpu.make_async_copy(tail, tails.at[k], sems.at[n + k]))
    for copy in copies:
        copy.start()

    zeros = jnp.zeros((4, T, T), F32)

    def clear(k, carry):
        total[pl.ds(k * 4, 4)] = zeros
        return carry

    lax.fori_loop(0, total.shape[0] // 4, clear, 0)
    for copy in copies:
        copy.wait()
    if tailed:
        summed = jnp.sum(tails[...].astype(F32), axis=0)
        lines = summed.shape[0] // 2
        out_refs[-1][:, :T] = summed[:lines]
        out_refs[-1][:, T:] = summed[lines:]
        for ref, blocks in zip(out_refs[1:-1], outs[1:]):
            ref[pl.ds(blocks * T, 2 * lines)] = summed.astype(BF16)

    def group(number, carry):
        products = []
        for k in range(GROUP):
            slot = number * GROUP + k
            product = lax.dot_general(
                tiles[slot],
                held[block(tables[in_row, slot])],
                ((contract, (0,)), ((), ())),
                preferred_element_type=F32,
            )
            products.append(jnp.where(slot < live[0], product, 0.0))
        for k, product in enumerate(products):
            total[tables[out_row, number * GROUP + k]] += product
        return carry

    lax.fori_loop(0, (live[0] + GROUP - 1) // GROUP, group, 0)
    start = 0
    for ref, blocks in zip(out_refs, outs):

        def out(k, carry, ref=ref, start=start):
            for at in range(4):
                ref[block(k * 4 + at)] = total[start + k * 4 + at].astype(BF16)
            return carry

        lax.fori_loop(0, blocks // 4, out, 0)
        start += blocks


def products(live, tables, in_row, out_row, tiles, sources, spans, outs, contract, tailed=0):
    lines = sources[0].shape[0] - spans[0] if tailed else 16
    kernel = functools.partial(
        products_kernel,
        spans=spans,
        outs=outs,
        contract=contract,
        in_row=in_row,
        out_row=out_row,
        tailed=tailed,
    )
    need = tiles.size * 2 + sum(spans) * T * 2 + sum(outs) * T * T * 6
    extra = [lines if tailed and n else 0 for n in range(len(outs))]
    return pl.pallas_call(
        kernel,
        out_shape=[jax.ShapeDtypeStruct((n * T + e, T), BF16) for n, e in zip(outs, extra)]
        + ([jax.ShapeDtypeStruct((lines // 2, 2 * T), F32)] if tailed else []),
        in_specs=[SMEM] * 2 + [VMEM] + [ANY] * len(sources),
        out_specs=[VMEM] * (len(outs) + (tailed > 0)),
        scratch_shapes=[
            pltpu.VMEM((sum(spans), T), BF16),
            pltpu.VMEM((sum(outs), T, T), F32),
            pltpu.VMEM((max(tailed, 1), lines, T), BF16),
            pltpu.SemaphoreType.DMA((len(spans) + tailed,)),
        ],
        compiler_params=room(need // MIB + 5),
    )(live, tables, tiles, *sources)


def pack_kernel(*refs):
    pieces, metas, sends, (said, lists, counts), (held, heard, words, table, sems) = (
        refs[:4],
        refs[4:8],
        refs[8:11],
        refs[11:14],
        refs[14:],
    )
    fetches = [pltpu.make_async_copy(p, heard.at[k], sems.at[k + 4]) for k, p in enumerate(metas)]
    copies = [pltpu.make_async_copy(p, held.at[k], sems.at[k]) for k, p in enumerate(pieces)]
    for copy in fetches + copies:
        copy.start()
    for copy in fetches:
        copy.wait()
    told = [heard[k].astype(F32)[:8] for k in range(4)]
    for n in range(3):
        words[pl.ds(n * 8, 8)] = told[n + 1].astype(I32)
    fetch = pltpu.make_async_copy(words, table, sems.at[8])
    fetch.start()
    over = functools.reduce(jnp.maximum, told)[2:3]
    said[...] = jnp.broadcast_to(over, (8, T))
    fetch.wait()
    for copy in copies:
        copy.wait()
    for n in range(3):
        group = 3 - n
        amount = table[n * 8 + 1, group]
        counts[n] = amount
        for k in range(4):
            lists[n * LANES + amount + k] = 64

        def step(k, carry, n=n, group=group):
            code = table[n * 8, group * LANES + k]
            lists[n * LANES + k] = code
            sends[n][block(k)] = held[code >> 4, block(code & 15)]
            return carry

        lax.fori_loop(0, amount, step, 0)


def pack(pieces, metas):
    return pl.pallas_call(
        pack_kernel,
        out_shape=[jax.ShapeDtypeStruct((CAP * T, T), BF16)] * 3
        + [jax.ShapeDtypeStruct((8, T), F32)]
        + [jax.ShapeDtypeStruct((3 * LANES,), I32), jax.ShapeDtypeStruct((3,), I32)],
        in_specs=[ANY] * 8,
        out_specs=[VMEM] * 4 + [SMEM] * 2,
        scratch_shapes=[
            pltpu.VMEM((4,) + pieces[0].shape, BF16),
            pltpu.VMEM((4, META, T), BF16),
            pltpu.VMEM((24, T), I32),
            pltpu.SMEM((24, T), I32),
            pltpu.SemaphoreType.DMA((9,)),
        ],
        compiler_params=room(10),
    )(*pieces, *metas)


def combine_kernel(lists, counts, own, sums, *refs):
    parts, outs, summed, total = refs[:3], refs[3:7], refs[7], refs[8]

    def widen(k, carry):
        for at in range(4):
            total[k * 4 + at] = own[block(k * 4 + at)].astype(F32)
        return carry

    lax.fori_loop(0, 16, widen, 0)
    lines = sums.shape[0]
    for k in range(2):
        tail = pl.ds(CAP * T + k * lines, lines)
        line = sums[:, k * T : (k + 1) * T] + total_of([part[tail] for part in parts])
        summed[:, k * T : (k + 1) * T] = line
        for ref in outs[1:]:
            ref[pl.ds(16 * T + k * lines, lines)] = line.astype(BF16)
    for n in range(3):

        def add(k, carry, n=n):
            for at in range(4):
                slot = k * 4 + at
                total[lists[n * LANES + slot]] += parts[n][block(slot)].astype(F32)
            return carry

        lax.fori_loop(0, (counts[n] + 3) // 4, add, 0)
    for n, ref in enumerate(outs):

        def out(k, carry, n=n, ref=ref):
            for at in range(4):
                ref[block(k * 4 + at)] = total[n * 16 + k * 4 + at].astype(ref.dtype)
            return carry

        lax.fori_loop(0, 4, out, 0)


def combine(lists, counts, own, sums, parts):
    rows = 16 * T
    return pl.pallas_call(
        combine_kernel,
        out_shape=[jax.ShapeDtypeStruct((rows, T), F32)]
        + [jax.ShapeDtypeStruct((rows + 2 * sums.shape[0], T), BF16)] * 3
        + [jax.ShapeDtypeStruct(sums.shape, F32)],
        in_specs=[SMEM] * 2 + [VMEM] * 5,
        out_specs=[VMEM] * 5,
        scratch_shapes=[pltpu.VMEM((65, T, T), F32)],
        compiler_params=room(16),
    )(lists, counts, own, sums, *parts)


def finish_kernel(*refs, scaling):
    pieces, sums, (nodes, weight, offset) = refs[:4], refs[4], refs[5:]
    rows = nodes.shape[0]
    nodes[...] = total_of([ref[pl.ds(0, rows)] for ref in pieces])
    lines = sums.shape[0]
    for k in range(2):
        part = pl.ds(k * T, T)
        total = sums[:, part]
        for ref in pieces[1:]:
            total = total + ref[pl.ds(rows + k * lines, lines)].astype(F32)
        total = total * scaling
        weight[:, part] = total[:T]
        offset[:, part] = jnp.sum(total[T:], axis=0, keepdims=True)


def finish(pieces, sums, scaling):
    width = sums.shape[-1]
    return pl.pallas_call(
        functools.partial(finish_kernel, scaling=scaling),
        out_shape=[
            jax.ShapeDtypeStruct(pieces[0].shape, F32),
            jax.ShapeDtypeStruct((T, width), F32),
            jax.ShapeDtypeStruct((1, width), F32),
        ],
        in_specs=[VMEM] * 5,
        out_specs=[VMEM] * 3,
        compiler_params=room(10),
    )(*pieces, sums)


def dense_kernel(*refs, step):
    parts, (grad, weight, offset), rest = refs[:5], refs[5:8], refs[8:]
    hidden, projected, sums = rest[-3:]
    second = len(rest) > 3

    @pl.when(pl.program_id(0) == 0)
    def _():
        sums[...] = rest[1][...] if second else jnp.zeros_like(sums)

    mixed = total_of([ref[...] for ref in parts])
    high = mixed.astype(BF16)
    low = (mixed - high.astype(F32)).astype(BF16)
    w = weight[...]
    pre = jnp.dot(high, w, preferred_element_type=F32)
    pre = pre + jnp.dot(low, w, preferred_element_type=F32) + offset[...]
    s = jax.nn.sigmoid(pre)
    hidden[...] = (pre * s).astype(BF16)
    slope = (grad[...].astype(F32) * s * (1.0 + pre * (1.0 - s))).astype(BF16)
    projected[pl.ds(pl.multiple_of(pl.program_id(0) * step, step), step)] = lax.dot_general(
        slope, w, (((1,), (1,)), ((), ())), preferred_element_type=F32
    ).astype(BF16)
    over_rows = (((0,), (0,)), ((), ()))
    sums[:T] += lax.dot_general(
        high, slope, over_rows, preferred_element_type=F32
    ) + lax.dot_general(low, slope, over_rows, preferred_element_type=F32)
    sums[T:] += jnp.sum(slope.astype(F32).reshape(-1, 16, slope.shape[1]), axis=0)

    @pl.when((pl.program_id(0) == pl.num_programs(0) - 1) & second)
    def _():
        lines = sums.shape[0]
        for k in range(2 if second else 0):
            part = sums[:, k * T : (k + 1) * T].astype(BF16)
            projected[pl.ds(projected.shape[0] - (2 - k) * lines, lines)] = part


def dense(parts, grad, weight, offset, part, before):
    width, rows = weight.shape[1], grad.shape[0]
    step = 1024
    steps = rows // 2 // step
    shift = part * steps
    tail = 2 * (T + 16) if before else 0
    half = pl.BlockSpec((step, T), lambda i: (i, 0))
    full = pl.BlockSpec((step, width), lambda i: (i + shift, 0))

    def whole(*shape):
        return pl.BlockSpec(shape, lambda i: (0, 0))

    return pl.pallas_call(
        functools.partial(dense_kernel, step=step),
        grid=(steps,),
        out_shape=[
            jax.ShapeDtypeStruct((rows, width), BF16),
            jax.ShapeDtypeStruct((rows // 2 + tail, T), BF16),
            jax.ShapeDtypeStruct((T + 16, width), F32),
        ],
        in_specs=[half] * 5
        + [full, whole(T, width), whole(1, width)]
        + ([ANY, whole(T + 16, width), ANY] if before else []),
        out_specs=[full, whole(rows // 2 + tail, T), whole(T + 16, width)],
        input_output_aliases={8: 0} if before else {},
        compiler_params=room(20),
    )(*parts, grad, weight, offset, *before)


def on_device(features, weight, offset, tile_values, tile_rows, tile_cols, live_tiles, grad_hidden):
    tiles = tile_values.reshape(tile_values.shape[2:])
    nodes_here = features.shape[0]
    scaling = 1.0 / math.sqrt(nodes_here * lax.axis_size("row") * lax.axis_size("col"))
    at_row, at_col = lax.axis_index("row"), lax.axis_index("col")
    live = live_tiles.reshape(1)
    meta, tables = prepare(at_row.reshape(1), at_col.reshape(1), live, tile_rows, tile_cols)

    pieces = ring_gather(features, along_inner)
    *sends, said, lists, counts = pack(pieces, ring_gather(meta, along_outer))
    named = ring_swap([None] + sends, along_outer)[1:]
    full = functools.reduce(jnp.maximum, ring_gather(said, along_inner))[0, 0] > 0.5

    def forward_all(outs, pieces):
        whole = ring_gather(jnp.concatenate(pieces), along_outer)
        spans = (4 * nodes_here,) * 4
        return products(live, tables, 2, 0, tiles, whole, spans, (32,) * 4, (1,))

    spans = (nodes_here,) * 4 + (CAP * T,) * 3
    outs = products(live, tables, 1, 0, tiles, pieces + named, spans, (32,) * 4, (1,))
    outs = lax.cond(full, forward_all, lambda outs, pieces: outs, outs, pieces)

    part_rows = nodes_here // 2
    halves = []
    for send, keep in zip(outs[:2], outs[2:]):
        got = other_core(send)
        far = []
        for d in (1, 2, 3):
            at = slice(d * part_rows, (d + 1) * part_rows)
            far.append((keep[at].astype(F32) + got[at].astype(F32)).astype(BF16))
        halves.append([keep, got] + ring_swap([None] + far, along_y)[1:])
    before, own, others = (), [], []
    for part, parts in enumerate(halves):
        hidden, projected, sums = dense(
            parts, grad_hidden, weight, offset.reshape(1, -1), part, before
        )
        here = ring_gather(projected, along_y)
        own.append(here)
        others.append([other_core(piece) for piece in here])
        before = (hidden, sums, others[0][0])

    gathered = others[1] + own[1] + others[0] + own[0]
    spans, outs = (part_rows,) * 16, (64,) + (CAP,) * 3
    here, *parts, sums = products(
        live, tables, 3, 1, tiles, gathered, spans, outs, (0,), tailed=8
    )
    parts = ring_swap([None] + parts, along_outer)[1:]

    def backward_all(outs, gathered):
        mine = products(live, tables, 3, 2, tiles, gathered, spans, (64,) * 4, (0,))
        mine = total_of(ring_swap(mine, along_outer)).reshape(4, nodes_here, T)
        far = [outs[d].at[:nodes_here].set(mine[d].astype(BF16)) for d in (1, 2, 3)]
        return [mine[0]] + far

    *outs, sums = combine(lists, counts, here, sums, parts)
    outs = lax.cond(full, backward_all, lambda outs, gathered: outs, outs, gathered)
    outs = ring_swap(outs, along_inner)
    grad_features, grad_weight, grad_offset = finish(outs, sums, scaling)
    return (hidden, grad_features, grad_weight, grad_offset.reshape(-1))


def solution(mesh):
    in_specs = (
        P(("col", "row"), None),
        P(),
        P(),
        P("row", "col", None, None, None),
        P("row", "col", None),
        P("row", "col", None),
        P("row", "col"),
        P(("row", "col"), None),
    )
    out_specs = (P(("row", "col"), None), P(("col", "row"), None), P(), P())
    return jax.shard_map(
        on_device, mesh=mesh, in_specs=in_specs, out_specs=out_specs, check_vma=False
    )
```

```python
import functools
import itertools
import math

import jax
import jax.numpy as jnp
from jax import lax
from jax.experimental import pallas as pl
from jax.experimental.pallas import tpu as pltpu
from jax.sharding import PartitionSpec as P

T = 128
F32, BF16, I32 = jnp.float32, jnp.bfloat16, jnp.int32
MIB = 1024 * 1024
GROUP = 32
META = 16
CAP = 24
LANES = 32
SMEM = pl.BlockSpec(memory_space=pltpu.SMEM)
VMEM = pl.BlockSpec(memory_space=pltpu.VMEM)
ANY = pl.BlockSpec(memory_space=pl.ANY)


def room(mib):
    return pltpu.CompilerParams(vmem_limit_bytes=mib * MIB)


def along_xz(value, to, x_core):
    pairs = []
    for x, z, y, core in itertools.product(range(4), range(4), range(4), range(2)):
        far = (to(x) % 4, z) if core == x_core else (x, to(z) % 4)
        pairs.append(((x * 4 + z) * 8 + y * 2 + core, (far[0] * 4 + far[1]) * 8 + y * 2 + core))
    return lax.ppermute(value, ("row", "col"), pairs)


def along_inner(value, to):
    return along_xz(value, to, 0)


def along_outer(value, to):
    return along_xz(value, to, 1)


def along_y(value, to):
    pairs = []
    for y in range(4):
        pairs.append((y * 2, to(y) % 4 * 2))
        pairs.append((y * 2 + 1, (2 * y - to(y)) % 4 * 2 + 1))
    return lax.ppermute(value, "col", pairs)


def other_core(value):
    pairs = [(y * 2 + k, y * 2 + 1 - k) for y in range(4) for k in range(2)]
    return lax.ppermute(value, "col", pairs)


def ahead(step):
    return lambda at: at + step


def ring_gather(value, along):
    across, after, before = [along(value, ahead(step)) for step in (2, -1, 1)]
    return [value, after, across, before]


def ring_swap(pieces, along):
    after, before = along(pieces[3], ahead(-1)), along(pieces[1], ahead(1))
    return [pieces[0], after, along(pieces[2], ahead(2)), before]


def total_of(pieces):
    return sum(piece.astype(F32) for piece in pieces)


def block(place):
    return pl.ds(pl.multiple_of(place * T, T), T)


def prepare_kernel(at_row, at_col, live_ref, rows_ref, cols_ref, meta, tables, slots_held, sems):
    copies = [
        pltpu.make_async_copy(ref, slots_held.at[k], sems.at[k])
        for k, ref in enumerate((rows_ref, cols_ref))
    ]
    for copy in copies:
        copy.start()
    for copy in copies:
        copy.wait()
    live = live_ref[0]
    x, z = at_row[0] >> 2, at_row[0] & 3
    y, core = at_col[0] >> 1, at_col[0] & 1
    rows, cols = slots_held[0], slots_held[1]
    slots = cols.shape[1]

    far_core = (rows >> 4) & 1
    same_core = jnp.where(far_core == core, 64, 0)
    dy = (rows >> 5) - y
    dy = jnp.where(far_core == 0, dy, -dy) & 3
    row_place = same_core + ((rows >> 3) & 1) * 32 + dy * 8 + (rows & 7)
    dx, dz = ((cols >> 6) - x) & 3, ((cols >> 4) - z) & 3
    outer, inner = jnp.where(core == 0, dz, dx), jnp.where(core == 0, dx, dz)
    code = inner * 16 + (cols & 15)
    dense_place = outer * 64 + code

    t = lax.broadcasted_iota(I32, (slots, slots), 0)
    s = lax.broadcasted_iota(I32, (slots, slots), 1)
    lane = lax.broadcasted_iota(I32, (slots, T), 1).astype(F32)

    def column(row):
        return jnp.sum(jnp.where(t == s, row, 0.0), axis=1, keepdims=True)

    def count(mask, value=1.0):
        return jnp.sum(jnp.where(mask, value, 0.0), axis=0, keepdims=True)

    valid = lax.broadcasted_iota(I32, (1, slots), 1) < live
    cols_f, outer_f = cols.astype(F32), outer.astype(F32)
    same = column(cols_f) == cols_f
    first = valid & (count(same & (t < s)) == 0.0)
    first_c = column(jnp.where(first, 1.0, 0.0)) > 0.0
    outer_c = column(outer_f)
    rank = count((t < s) & first_c & (outer_c == outer_f))
    over = jnp.where(first & (outer != 0) & (rank >= CAP), 1.0, 0.0)
    over = jnp.max(over, axis=1, keepdims=True)
    far = (64 + (outer - 1) * CAP).astype(F32) + jnp.minimum(rank, CAP - 1.0)
    place = jnp.where(outer == 0, code.astype(F32), far)
    place = count(same & first_c, column(place))
    place = jnp.where(valid, place, 0.0).astype(I32)
    second = (rows >> 3) & 1
    source = (1 - second) * 64 + ((row_place & 64) >> 1) + (row_place & 31)
    pad = jnp.zeros((4, slots), I32)
    tables[...] = jnp.concatenate([row_place, place, dense_place, source, pad], axis=0)

    key = column(jnp.where(first & (rank < CAP), outer_f * LANES + rank, -1.0))
    wanted = count(key == lane, column(code.astype(F32)))
    amounts = jnp.minimum(count((outer_c == lane) & first_c), 1.0 * CAP)
    line = lax.broadcasted_iota(I32, (META, T), 0)
    lines = [wanted, amounts, jnp.broadcast_to(over, (1, T)), jnp.zeros((META - 3, T), F32)]
    meta[...] = jnp.concatenate(lines, axis=0).astype(BF16)


def prepare(at_row, at_col, live, rows, cols):
    slots = cols.shape[-1]
    return pl.pallas_call(
        prepare_kernel,
        out_shape=[
            jax.ShapeDtypeStruct((META, T), BF16),
            jax.ShapeDtypeStruct((8, slots), I32),
        ],
        in_specs=[SMEM] * 3 + [ANY] * 2,
        out_specs=[VMEM] * 2,
        scratch_shapes=[pltpu.VMEM((2, 1, slots), I32), pltpu.SemaphoreType.DMA((2,))],
        compiler_params=room(4),
    )(at_row, at_col, live, rows.reshape(1, slots), cols.reshape(1, slots))


def products_kernel(
    live, tables, tiles, *refs, spans, outs, contract, in_row, out_row, tailed
):
    n = len(spans)
    sources, out_refs, (held, total, tails, sems) = refs[:n], refs[n:-4], refs[-4:]
    copies = []
    start = 0
    for k, (ref, rows) in enumerate(zip(sources, spans)):
        copies.append(
            pltpu.make_async_copy(
                ref.at[pl.ds(0, rows)], held.at[pl.ds(start, rows)], sems.at[k]
            )
        )
        start += rows
    for k in range(tailed):
        tail = sources[k].at[pl.ds(spans[k], tails.shape[1])]
        copies.append(pltpu.make_async_copy(tail, tails.at[k], sems.at[n + k]))
    for copy in copies:
        copy.start()

    zeros = jnp.zeros((4, T, T), F32)

    def clear(k, carry):
        total[pl.ds(k * 4, 4)] = zeros
        return carry

    lax.fori_loop(0, total.shape[0] // 4, clear, 0)
    for copy in copies:
        copy.wait()
    if tailed:
        summed = jnp.sum(tails[...].astype(F32), axis=0)
        lines = summed.shape[0] // 2
        out_refs[-1][:, :T] = summed[:lines]
        out_refs[-1][:, T:] = summed[lines:]
        for ref, blocks in zip(out_refs[1:-1], outs[1:]):
            ref[pl.ds(blocks * T, 2 * lines)] = summed.astype(BF16)

    def group(number, carry):
        products = []
        for k in range(GROUP):
            slot = number * GROUP + k
            product = lax.dot_general(
                tiles[slot],
                held[block(tables[in_row, slot])],
                ((contract, (0,)), ((), ())),
                preferred_element_type=F32,
            )
            products.append(jnp.where(slot < live[0], product, 0.0))
        for k, product in enumerate(products):
            total[tables[out_row, number * GROUP + k]] += product
        return carry

    lax.fori_loop(0, (live[0] + GROUP - 1) // GROUP, group, 0)
    start = 0
    for ref, blocks in zip(out_refs, outs):

        def out(k, carry, ref=ref, start=start):
            for at in range(4):
                ref[block(k * 4 + at)] = total[start + k * 4 + at].astype(BF16)
            return carry

        lax.fori_loop(0, blocks // 4, out, 0)
        start += blocks


def products(live, tables, in_row, out_row, tiles, sources, spans, outs, contract, tailed=0):
    lines = sources[0].shape[0] - spans[0] if tailed else 16
    kernel = functools.partial(
        products_kernel,
        spans=spans,
        outs=outs,
        contract=contract,
        in_row=in_row,
        out_row=out_row,
        tailed=tailed,
    )
    need = tiles.size * 2 + sum(spans) * T * 2 + sum(outs) * T * T * 6
    extra = [lines if tailed and n else 0 for n in range(len(outs))]
    return pl.pallas_call(
        kernel,
        out_shape=[jax.ShapeDtypeStruct((n * T + e, T), BF16) for n, e in zip(outs, extra)]
        + ([jax.ShapeDtypeStruct((lines // 2, 2 * T), F32)] if tailed else []),
        in_specs=[SMEM] * 2 + [VMEM] + [ANY] * len(sources),
        out_specs=[VMEM] * (len(outs) + (tailed > 0)),
        scratch_shapes=[
            pltpu.VMEM((sum(spans), T), BF16),
            pltpu.VMEM((sum(outs), T, T), F32),
            pltpu.VMEM((max(tailed, 1), lines, T), BF16),
            pltpu.SemaphoreType.DMA((len(spans) + tailed,)),
        ],
        compiler_params=room(need // MIB + 5),
    )(live, tables, tiles, *sources)


def pack_kernel(*refs):
    pieces, metas, sends, (said, lists, counts), (held, heard, words, table, sems) = (
        refs[:4],
        refs[4:8],
        refs[8:11],
        refs[11:14],
        refs[14:],
    )
    fetches = [pltpu.make_async_copy(p, heard.at[k], sems.at[k + 4]) for k, p in enumerate(metas)]
    copies = [pltpu.make_async_copy(p, held.at[k], sems.at[k]) for k, p in enumerate(pieces)]
    for copy in fetches + copies:
        copy.start()
    for copy in fetches:
        copy.wait()
    told = [heard[k].astype(F32)[:8] for k in range(4)]
    for n in range(3):
        words[pl.ds(n * 8, 8)] = told[n + 1].astype(I32)
    fetch = pltpu.make_async_copy(words, table, sems.at[8])
    fetch.start()
    over = functools.reduce(jnp.maximum, told)[2:3]
    said[...] = jnp.broadcast_to(over, (8, T))
    fetch.wait()
    for copy in copies:
        copy.wait()
    for n in range(3):
        group = 3 - n
        amount = table[n * 8 + 1, group]
        counts[n] = amount
        for k in range(4):
            lists[n * LANES + amount + k] = 64

        def step(k, carry, n=n, group=group):
            code = table[n * 8, group * LANES + k]
            lists[n * LANES + k] = code
            sends[n][block(k)] = held[code >> 4, block(code & 15)]
            return carry

        lax.fori_loop(0, amount, step, 0)


def pack(pieces, metas):
    return pl.pallas_call(
        pack_kernel,
        out_shape=[jax.ShapeDtypeStruct((CAP * T, T), BF16)] * 3
        + [jax.ShapeDtypeStruct((8, T), F32)]
        + [jax.ShapeDtypeStruct((3 * LANES,), I32), jax.ShapeDtypeStruct((3,), I32)],
        in_specs=[ANY] * 8,
        out_specs=[VMEM] * 4 + [SMEM] * 2,
        scratch_shapes=[
            pltpu.VMEM((4,) + pieces[0].shape, BF16),
            pltpu.VMEM((4, META, T), BF16),
            pltpu.VMEM((24, T), I32),
            pltpu.SMEM((24, T), I32),
            pltpu.SemaphoreType.DMA((9,)),
        ],
        compiler_params=room(10),
    )(*pieces, *metas)


def combine_kernel(lists, counts, own, sums, *refs):
    parts, outs, summed, total = refs[:3], refs[3:7], refs[7], refs[8]

    def widen(k, carry):
        for at in range(4):
            total[k * 4 + at] = own[block(k * 4 + at)].astype(F32)
        return carry

    lax.fori_loop(0, 16, widen, 0)
    lines = sums.shape[0]
    for k in range(2):
        tail = pl.ds(CAP * T + k * lines, lines)
        line = sums[:, k * T : (k + 1) * T] + total_of([part[tail] for part in parts])
        summed[:, k * T : (k + 1) * T] = line
        for ref in outs[1:]:
            ref[pl.ds(16 * T + k * lines, lines)] = line.astype(BF16)
    for n in range(3):

        def add(k, carry, n=n):
            for at in range(4):
                slot = k * 4 + at
                total[lists[n * LANES + slot]] += parts[n][block(slot)].astype(F32)
            return carry

        lax.fori_loop(0, (counts[n] + 3) // 4, add, 0)
    for n, ref in enumerate(outs):

        def out(k, carry, n=n, ref=ref):
            for at in range(4):
                ref[block(k * 4 + at)] = total[n * 16 + k * 4 + at].astype(ref.dtype)
            return carry

        lax.fori_loop(0, 4, out, 0)


def combine(lists, counts, own, sums, parts):
    rows = 16 * T
    return pl.pallas_call(
        combine_kernel,
        out_shape=[jax.ShapeDtypeStruct((rows, T), F32)]
        + [jax.ShapeDtypeStruct((rows + 2 * sums.shape[0], T), BF16)] * 3
        + [jax.ShapeDtypeStruct(sums.shape, F32)],
        in_specs=[SMEM] * 2 + [VMEM] * 5,
        out_specs=[VMEM] * 5,
        scratch_shapes=[pltpu.VMEM((65, T, T), F32)],
        compiler_params=room(16),
    )(lists, counts, own, sums, *parts)


def finish_kernel(*refs, scaling):
    pieces, sums, (nodes, weight, offset) = refs[:4], refs[4], refs[5:]
    rows = nodes.shape[0]
    nodes[...] = total_of([ref[pl.ds(0, rows)] for ref in pieces])
    lines = sums.shape[0]
    for k in range(2):
        part = pl.ds(k * T, T)
        total = sums[:, part]
        for ref in pieces[1:]:
            total = total + ref[pl.ds(rows + k * lines, lines)].astype(F32)
        total = total * scaling
        weight[:, part] = total[:T]
        offset[:, part] = jnp.sum(total[T:], axis=0, keepdims=True)


def finish(pieces, sums, scaling):
    width = sums.shape[-1]
    return pl.pallas_call(
        functools.partial(finish_kernel, scaling=scaling),
        out_shape=[
            jax.ShapeDtypeStruct(pieces[0].shape, F32),
            jax.ShapeDtypeStruct((T, width), F32),
            jax.ShapeDtypeStruct((1, width), F32),
        ],
        in_specs=[VMEM] * 5,
        out_specs=[VMEM] * 3,
        compiler_params=room(10),
    )(*pieces, sums)


def dense_kernel(*refs, step):
    parts, (grad, weight, offset), rest = refs[:5], refs[5:8], refs[8:]
    hidden, projected, sums = rest[-3:]
    second = len(rest) > 3

    @pl.when(pl.program_id(0) == 0)
    def _():
        sums[...] = rest[1][...] if second else jnp.zeros_like(sums)

    mixed = total_of([ref[...] for ref in parts])
    high = mixed.astype(BF16)
    low = (mixed - high.astype(F32)).astype(BF16)
    w = weight[...]
    pre = jnp.dot(high, w, preferred_element_type=F32)
    pre = pre + jnp.dot(low, w, preferred_element_type=F32) + offset[...]
    s = jax.nn.sigmoid(pre)
    hidden[...] = (pre * s).astype(BF16)
    slope = (grad[...].astype(F32) * s * (1.0 + pre * (1.0 - s))).astype(BF16)
    projected[pl.ds(pl.multiple_of(pl.program_id(0) * step, step), step)] = lax.dot_general(
        slope, w, (((1,), (1,)), ((), ())), preferred_element_type=F32
    ).astype(BF16)
    over_rows = (((0,), (0,)), ((), ()))
    sums[:T] += lax.dot_general(
        high, slope, over_rows, preferred_element_type=F32
    ) + lax.dot_general(low, slope, over_rows, preferred_element_type=F32)
    sums[T:] += jnp.sum(slope.astype(F32).reshape(-1, 16, slope.shape[1]), axis=0)

    @pl.when((pl.program_id(0) == pl.num_programs(0) - 1) & second)
    def _():
        lines = sums.shape[0]
        for k in range(2 if second else 0):
            part = sums[:, k * T : (k + 1) * T].astype(BF16)
            projected[pl.ds(projected.shape[0] - (2 - k) * lines, lines)] = part


def dense(parts, grad, weight, offset, part, before):
    width, rows = weight.shape[1], grad.shape[0]
    step = 1024
    steps = rows // 2 // step
    shift = part * steps
    tail = 2 * (T + 16) if before else 0
    half = pl.BlockSpec((step, T), lambda i: (i, 0))
    full = pl.BlockSpec((step, width), lambda i: (i + shift, 0))

    def whole(*shape):
        return pl.BlockSpec(shape, lambda i: (0, 0))

    return pl.pallas_call(
        functools.partial(dense_kernel, step=step),
        grid=(steps,),
        out_shape=[
            jax.ShapeDtypeStruct((rows, width), BF16),
            jax.ShapeDtypeStruct((rows // 2 + tail, T), BF16),
            jax.ShapeDtypeStruct((T + 16, width), F32),
        ],
        in_specs=[half] * 5
        + [full, whole(T, width), whole(1, width)]
        + ([ANY, whole(T + 16, width), ANY] if before else []),
        out_specs=[full, whole(rows // 2 + tail, T), whole(T + 16, width)],
        input_output_aliases={8: 0} if before else {},
        compiler_params=room(20),
    )(*parts, grad, weight, offset, *before)


def on_device(features, weight, offset, tile_values, tile_rows, tile_cols, live_tiles, grad_hidden):
    tiles = tile_values.reshape(tile_values.shape[2:])
    nodes_here = features.shape[0]
    scaling = 1.0 / math.sqrt(nodes_here * lax.axis_size("row") * lax.axis_size("col"))
    at_row, at_col = lax.axis_index("row"), lax.axis_index("col")
    live = live_tiles.reshape(1)
    meta, tables = prepare(at_row.reshape(1), at_col.reshape(1), live, tile_rows, tile_cols)

    pieces = ring_gather(features, along_inner)
    *sends, said, lists, counts = pack(pieces, ring_gather(meta, along_outer))
    named = ring_swap([None] + sends, along_outer)[1:]
    full = functools.reduce(jnp.maximum, ring_gather(said, along_inner))[0, 0] > 0.5

    def forward_all(outs, pieces):
        whole = ring_gather(jnp.concatenate(pieces), along_outer)
        spans = (4 * nodes_here,) * 4
        return products(live, tables, 2, 0, tiles, whole, spans, (32,) * 4, (1,))

    spans = (nodes_here,) * 4 + (CAP * T,) * 3
    outs = products(live, tables, 1, 0, tiles, pieces + named, spans, (32,) * 4, (1,))
    outs = lax.cond(full, forward_all, lambda outs, pieces: outs, outs, pieces)

    part_rows = nodes_here // 2
    halves = []
    for send, keep in zip(outs[:2], outs[2:]):
        got = other_core(send)
        far = []
        for d in (1, 2, 3):
            at = slice(d * part_rows, (d + 1) * part_rows)
            far.append((keep[at].astype(F32) + got[at].astype(F32)).astype(BF16))
        halves.append([keep, got] + ring_swap([None] + far, along_y)[1:])
    before, own, others = (), [], []
    for part, parts in enumerate(halves):
        hidden, projected, sums = dense(
            parts, grad_hidden, weight, offset.reshape(1, -1), part, before
        )
        here = ring_gather(projected, along_y)
        own.append(here)
        others.append([other_core(piece) for piece in here])
        before = (hidden, sums, others[0][0])

    gathered = others[1] + own[1] + others[0] + own[0]
    spans, outs = (part_rows,) * 16, (64,) + (CAP,) * 3
    here, *parts, sums = products(
        live, tables, 3, 1, tiles, gathered, spans, outs, (0,), tailed=8
    )
    parts = ring_swap([None] + parts, along_outer)[1:]

    def backward_all(outs, gathered):
        mine = products(live, tables, 3, 2, tiles, gathered, spans, (64,) * 4, (0,))
        mine = total_of(ring_swap(mine, along_outer)).reshape(4, nodes_here, T)
        far = [outs[d].at[:nodes_here].set(mine[d].astype(BF16)) for d in (1, 2, 3)]
        return [mine[0]] + far

    *outs, sums = combine(lists, counts, here, sums, parts)
    outs = lax.cond(full, backward_all, lambda outs, gathered: outs, outs, gathered)
    outs = ring_swap(outs, along_inner)
    grad_features, grad_weight, grad_offset = finish(outs, sums, scaling)
    return (hidden, grad_features, grad_weight, grad_offset.reshape(-1))


def solution(mesh):
    in_specs = (
        P(("col", "row"), None),
        P(),
        P(),
        P("row", "col", None, None, None),
        P("row", "col", None),
        P("row", "col", None),
        P("row", "col"),
        P(("row", "col"), None),
    )
    out_specs = (P(("row", "col"), None), P(("col", "row"), None), P(), P())
    return jax.shard_map(
        on_device, mesh=mesh, in_specs=in_specs, out_specs=out_specs, check_vma=False
    )
```
